512 devices in a mesh: gx: 16 (over x, y), gy: 32 (over z, core).
Axes of the slice: x: 4, y: 4, z: 16, core: 2. Of those that a mesh axis runs over, the one named last changes fastest.
Arguments:
- pressure_rhs: float32 [128, 256, 256], P('gx', 'gy'), may hold values from -6 to 6
- storage_fine: float32 [128, 256, 256], P('gx', 'gy'), may hold values from 0.003 to 0.03
- mobility_fine: float32 [3, 128, 256, 256], P(None, 'gx', 'gy'), may hold values from 0.1 to 10
- storage_mid: float32 [64, 128, 128], P('gx', 'gy'), may hold values from 0.024 to 0.24
- mobility_mid: float32 [3, 64, 128, 128], P(None, 'gx', 'gy'), may hold values from 0.4 to 40
- storage_coarse: float32 [32, 64, 64], P('gx', 'gy'), may hold values from 0.19 to 1.9
- mobility_coarse: float32 [3, 32, 64, 64], P(None, 'gx', 'gy'), may hold values from 1.6 to 160
Outputs:
- pressure: float32 [128, 256, 256], P('gx', 'gy')
- residual: float32 [128, 256, 256], P('gx', 'gy')
The draws below stay inside these ranges and needn't reach their ends.
All inputs are finite; a program needn't handle non-finite values.
Results may differ from the reference program's by a relative error of at most 0.0002.
Values sent between devices are 32-bit elements; how exact they have to be, the bound alone decides.
A program may use at most 192 MiB of HBM per device.

```python
import math
import jax
import jax.numpy as jnp
from jax import lax

CX = 8
CY = 8
NU = 2
KC = 6
GROUP = 8
NX = 128
NY = 256
NZ = 256


def level_of(own_key, shape, pieces, least, high):
    loudness, own = 1.0, jax.random.fold_in(own_key, 6)
    for axis_at, blocks in pieces:
        draws = jnp.exp(jax.random.uniform(jax.random.fold_in(own, axis_at), (blocks,), jnp.float32, least / len(pieces), high / len(pieces)))
        loudness = loudness * jnp.repeat(draws, shape[axis_at] // blocks).reshape([-1 if axis == axis_at else 1 for axis in range(len(shape))])
    return loudness


def gaussian(key, shape, width, reach, split=(), held_as=jnp.bfloat16):
    loudness = level_of(key, shape, split, -0.22, 0.18) if split else 1.0
    result = jax.random.normal(key, shape, jnp.float32) * width * loudness
    return jnp.minimum(jnp.maximum(result, -reach), reach).astype(held_as)


def setup_inputs(seed: int = 0) -> dict:
    streams_of = jax.random.split(jax.random.key(seed), 8)
    return {
        "pressure_rhs": gaussian(streams_of[0], (NX, NY, NZ), 1.0, 6.0, ((0, 16), (1, 32)), jnp.float32),
        "storage_fine": jnp.clip(jnp.exp(math.log(0.03) - 2.3025851 * jax.random.uniform(streams_of[1], (NX, NY, NZ), jnp.float32) ** level_of(streams_of[1], (NX, NY, NZ), ((0, 16), (1, 32)), -0.2, 0.2)), 0.003, 0.03),
        "mobility_fine": jnp.clip(jnp.exp(math.log(10.0) - 4.6051702 * jax.random.uniform(streams_of[2], (3, NX, NY, NZ), jnp.float32) ** level_of(streams_of[2], (3, NX, NY, NZ), ((1, 16), (2, 32)), -0.2, 0.2)), 0.1, 10.0),
        "storage_mid": jnp.clip(jnp.exp(math.log(0.24) - 2.3025851 * jax.random.uniform(streams_of[3], (NX // 2, NY // 2, NZ // 2), jnp.float32) ** level_of(streams_of[3], (NX // 2, NY // 2, NZ // 2), ((0, 16), (1, 32)), -0.2, 0.2)), 0.024, 0.24),
        "mobility_mid": jnp.clip(jnp.exp(math.log(40.0) - 4.6051702 * jax.random.uniform(streams_of[4], (3, NX // 2, NY // 2, NZ // 2), jnp.float32) ** level_of(streams_of[4], (3, NX // 2, NY // 2, NZ // 2), ((1, 16), (2, 32)), -0.2, 0.2)), 0.4, 40.0),
        "storage_coarse": jnp.clip(jnp.exp(math.log(1.9) - 2.3025851 * jax.random.uniform(streams_of[5], (NX // 4, NY // 4, NZ // 4), jnp.float32) ** level_of(streams_of[5], (NX // 4, NY // 4, NZ // 4), ((0, 16), (1, 32)), -0.2, 0.2)), 0.19, 1.9),
        "mobility_coarse": jnp.clip(jnp.exp(math.log(160.0) - 4.6051702 * jax.random.uniform(streams_of[6], (3, NX // 4, NY // 4, NZ // 4), jnp.float32) ** level_of(streams_of[6], (3, NX // 4, NY // 4, NZ // 4), ((1, 16), (2, 32)), -0.2, 0.2)), 1.6, 160.0),
    }


damping = 2.0 / 3.0

def harmonic(left, right):
    return 2.0 * left * right / (left + right)

def shifted(values, dim, upward):
    n = values.shape[dim]
    edge = jnp.zeros_like(lax.slice_in_dim(values, 0, 1, axis=dim))
    if upward:
        return jnp.concatenate([lax.slice_in_dim(values, 1, n, axis=dim), edge], axis=dim)
    return jnp.concatenate([edge, lax.slice_in_dim(values, 0, n - 1, axis=dim)], axis=dim)

def operator_parts(storage, mobility, block_specs):
    uppers = []
    lowers = []
    for dim in range(3):
        widths = [(0, 0), (0, 0), (0, 0)]
        widths[dim] = (1, 1)
        padded = jnp.pad(mobility[dim], widths)
        n = padded.shape[dim]
        centre = lax.slice_in_dim(padded, 1, n - 1, axis=dim)
        upper_w = harmonic(centre, lax.slice_in_dim(padded, 2, n, axis=dim))
        lower_w = harmonic(lax.slice_in_dim(padded, 0, n - 2, axis=dim), centre)
        block, offset = block_specs[dim]
        if block > 0:
            index = jnp.arange(n - 2, dtype=jnp.int32)
            shape = [1, 1, 1]
            shape[dim] = n - 2
            keep_up = ((index + 1 - offset) % block != 0).reshape(shape)
            keep_down = ((index - offset) % block != 0).reshape(shape)
            upper_w = jnp.where(keep_up, upper_w, jnp.zeros_like(upper_w))
            lower_w = jnp.where(keep_down, lower_w, jnp.zeros_like(lower_w))
        uppers.append(upper_w)
        lowers.append(lower_w)
    diagonal = storage + (uppers[0] + lowers[0]) + (uppers[1] + lowers[1]) + (uppers[2] + lowers[2])
    return (uppers, lowers, diagonal)

def apply_operator(values, parts):
    uppers, lowers, diagonal = parts
    total = diagonal * values
    for dim in range(3):
        total = total - uppers[dim] * shifted(values, dim, True) - lowers[dim] * shifted(values, dim, False)
    return total

def smooth(values, source, parts, sweeps):
    for turn in range(sweeps):
        values = values + damping * (source - apply_operator(values, parts)) / parts[2]
    return values

def smooth_zero(source, parts):
    values = damping * source / parts[2]
    return smooth(values, source, parts, NU - 1)

def restrict(values):
    a, b, c = values.shape
    return values.reshape(a // 2, 2, b // 2, 2, c // 2, 2).sum(axis=(1, 3, 5))

def prolong(values):
    return jnp.repeat(jnp.repeat(jnp.repeat(values, 2, axis=0), 2, axis=1), 2, axis=2)

def line_solve(lower_band, diagonal, upper_band, source):
    return lax.linalg.tridiagonal_solve(lower_band, diagonal, upper_band, source[..., None])[..., 0]

def coarse_solve(source, parts):
    uppers, lowers, diagonal = parts
    lower_band = -lowers[2]
    upper_band = -uppers[2]
    answer = line_solve(lower_band, diagonal, upper_band, source)
    for turn in range(KC - 1):
        push = source + uppers[0] * shifted(answer, 0, True) + lowers[0] * shifted(answer, 0, False)
        push = push + uppers[1] * shifted(answer, 1, True) + lowers[1] * shifted(answer, 1, False)
        answer = line_solve(lower_band, diagonal, upper_band, push)
    return answer

def reference(pressure_rhs, storage_fine, mobility_fine, storage_mid, mobility_mid, storage_coarse, mobility_coarse):
    fine_parts = operator_parts(storage_fine, mobility_fine, ((0, 0), (0, 0), (0, 0)))
    fine_x = smooth_zero(pressure_rhs, fine_parts)
    fine_res = pressure_rhs - apply_operator(fine_x, fine_parts)
    mid_source = restrict(fine_res)
    mid_parts = operator_parts(storage_mid, mobility_mid, ((0, 0), (0, 0), (0, 0)))
    mid_y = smooth_zero(mid_source, mid_parts)
    mid_res = mid_source - apply_operator(mid_y, mid_parts)
    coarse_source = restrict(mid_res)
    coarse_parts = operator_parts(storage_coarse, mobility_coarse, ((CX // 4, 0), (GROUP * (CY // 4), 2 * (CY // 4)), (0, 0)))
    coarse_z = coarse_solve(coarse_source, coarse_parts)
    mid_y = smooth(mid_y + prolong(coarse_z), mid_source, mid_parts, NU)
    fine_x = smooth(fine_x + prolong(mid_y), pressure_rhs, fine_parts, NU)
    residual = pressure_rhs - apply_operator(fine_x, fine_parts)
    return (fine_x, residual)
```

```python
import functools

import jax
import jax.numpy as jnp
from jax import lax
from jax.experimental import pallas as pl
from jax.experimental.pallas import tpu as pltpu
from jax.sharding import PartitionSpec as P

KC = 6
GROUP = 8
DAMPING = 2.0 / 3.0

MESH = pl.DeviceIdType.MESH

O = 4
ROWS = 16
NEIGHBOURS = ((1, 0), (-1, 0), (1, 1), (1, -1), (-1, 1), (-1, -1), (0, 1), (0, -1))


def reciprocal(values):
    guess = pl.reciprocal(values, approx=True)
    return guess * (2.0 - values * guess)


def harmonic(left, right):
    return 2.0 * left * right * reciprocal(left + right)


def next_of(values, axis):
    return pltpu.roll(values, values.shape[axis] - 1, axis)


def prev_of(values, axis):
    return pltpu.roll(values, 1, axis)


def swapped(values):
    return jnp.concatenate([values[1:2], values[0:1]], axis=0)


def next_z(values):
    moved = next_of(values, values.ndim - 1)
    if values.ndim == 2:
        return moved
    lane = lax.broadcasted_iota(jnp.int32, values.shape, 2)
    return jnp.where(lane == 127, swapped(moved), moved)


def prev_z(values):
    moved = prev_of(values, values.ndim - 1)
    if values.ndim == 2:
        return moved
    lane = lax.broadcasted_iota(jnp.int32, values.shape, 2)
    return jnp.where(lane == 0, swapped(moved), moved)


def next_y(values):
    return next_of(values, values.ndim - 2)


def prev_y(values):
    return prev_of(values, values.ndim - 2)


def one_hot(shape, test):
    row = lax.broadcasted_iota(jnp.int32, shape, 0)
    column = lax.broadcasted_iota(jnp.int32, shape, 1)
    return jnp.where(test(row, column), 1.0, 0.0).astype(jnp.bfloat16)


def thirds(values):
    head = values.astype(jnp.bfloat16)
    rest = values - head.astype(jnp.float32)
    middle = rest.astype(jnp.bfloat16)
    tail = (rest - middle.astype(jnp.float32)).astype(jnp.bfloat16)
    return [head, middle, tail]


def times_one_hot(values, matrix):
    rows = values.shape[0]
    product = jnp.dot(jnp.concatenate(thirds(values), axis=0), matrix, preferred_element_type=jnp.float32)
    return product[:rows] + product[rows : 2 * rows] + product[2 * rows :]


def source_span(step, n, width):
    return (n - width, n) if step > 0 else (0, width) if step < 0 else (0, n)


def target_span(step, n, width):
    return (O - width, O) if step > 0 else (O + n, O + n + width) if step < 0 else (O, O + n)


def face_weights(level, field, own, rows, keep_x, keep_y, keep_z):
    wx, wyu, wyd, wzu, wzd, diag, damp = level
    first, last = rows

    def along_x(x, _):
        wx[x] = harmonic(field[0, x], field[0, x + 1])
        return 0

    lax.fori_loop(first - 1, last, along_x, 0, unroll=True)
    wx[O - 1] = wx[O - 1] * keep_x[0]
    wx[O + own - 1] = wx[O + own - 1] * keep_x[1]

    def rest(x, _):
        second = field[1, x]
        third = field[2, x]
        up_y = harmonic(second, next_y(second)) * keep_y
        up_z = harmonic(third, next_z(third)) * keep_z
        down_y = prev_y(up_y)
        down_z = prev_z(up_z)
        wyu[x] = up_y
        wyd[x] = down_y
        wzu[x] = up_z
        wzd[x] = down_z
        total = field[3, x] + (wx[x] + wx[x - 1]) + (up_y + down_y) + (up_z + down_z)
        diag[x] = total
        damp[x] = DAMPING * reciprocal(total)
        return 0

    lax.fori_loop(first, last, rest, 0, unroll=True)


def row_residual(level, source, field, x):
    wx, wyu, wyd, wzu, wzd, diag, damp = level
    v = field[x]
    left = source[x] - diag[x] * v
    left = left + (wx[x] * field[x + 1] + wx[x - 1] * field[x - 1])
    left = left + (wyu[x] * next_y(v) + wyd[x] * prev_y(v))
    left = left + (wzu[x] * next_z(v) + wzd[x] * prev_z(v))
    return left


def sweep(level, source, field, result, rows):
    damp = level[6]

    def body(x, _):
        result[x] = field[x] + damp[x] * row_residual(level, source, field, x)
        return 0

    lax.fori_loop(rows[0], rows[1], body, 0, unroll=True)


def start_sweep(level, source, result, rows):
    damp = level[6]

    def body(x, _):
        result[x] = damp[x] * source[x]
        return 0

    lax.fori_loop(rows[0], rows[1], body, 0, unroll=True)


def kernel(
    count_x,
    count_y,
    rhs_h,
    store_f_h,
    mob_f_h,
    store_m_h,
    mob_m_h,
    store_c_h,
    mob_c_h,
    pressure_h,
    residual_h,
    f_in,
    f_wx,
    f_wyu,
    f_wyd,
    f_wzu,
    f_wzd,
    f_diag,
    f_damp,
    f_a,
    f_b,
    f_x,
    m_in,
    m_src,
    m_wx,
    m_wyu,
    m_wyd,
    m_wzu,
    m_wzd,
    m_diag,
    m_damp,
    m_a,
    m_b,
    m_y,
    m_fold,
    f_spread,
    c_coef,
    c_src,
    c_ext,
    c_spread,
    c_weights,
    c_alpha,
    c_gamma,
    local_sem,
    send_sem,
    recv_sem,
):
    gx = lax.axis_index("gx")
    gy = lax.axis_index("gy")
    place = lax.rem(gy + (2 * GROUP - 2), GROUP)
    leader = gy - place + count_y

    def beside(sx, sy):
        return {
            "gx": lax.rem(gx + (sx + count_x), count_x),
            "gy": lax.rem(gy + (sy + count_y), count_y),
        }

    def member(d):
        return {"gx": gx, "gy": lax.rem(leader + lax.rem(place + d, GROUP), count_y)}

    c_coef[...] = jnp.ones_like(c_coef)
    c_src[...] = jnp.zeros_like(c_src)

    barrier = pltpu.get_barrier_semaphore()
    for sx, sy in NEIGHBOURS:
        pl.semaphore_signal(barrier, inc=1, device_id=beside(sx, sy), device_id_type=MESH)
    for d in range(1, GROUP):
        pl.semaphore_signal(barrier, inc=1, device_id=member(d), device_id_type=MESH)

    locals_ = []

    def bring(source, target):
        copy = pltpu.make_async_copy(source, target, local_sem.at[len(locals_)])
        copy.start()
        locals_.append(copy)
        return copy

    sends = []

    def push(source, target, device):
        at = len(sends)
        copy = pltpu.make_async_remote_copy(
            src_ref=source,
            dst_ref=target,
            send_sem=send_sem.at[at],
            recv_sem=recv_sem.at[at],
            device_id=device,
            device_id_type=MESH,
        )
        copy.start()
        sends.append(copy)
        return copy

    own8 = slice(O, O + 8)
    own4 = slice(O, O + 4)
    fine_in = []
    for half in range(2):
        z = slice(128 * half, 128 * half + 128)
        fine_in.append(bring(mob_f_h.at[:, :, :, z], f_in.at[0:3, own8, half, own8, :]))
        fine_in.append(bring(store_f_h.at[:, :, z], f_in.at[3, own8, half, own8, :]))
        fine_in.append(bring(rhs_h.at[:, :, z], f_in.at[4, own8, half, own8, :]))
    coarse_in = []
    for iy in range(2):
        coarse_in.append(bring(store_c_h.at[:, iy, :], c_coef.at[0, iy, 0:2, :]))
        coarse_in.append(bring(mob_c_h.at[:, :, iy, :], c_coef.at[1:4, iy, 0:2, :]))
    mid_in = [
        bring(mob_m_h, m_in.at[0:3, own4, own4, :]),
        bring(store_m_h, m_in.at[3, own4, own4, :]),
    ]
    f_src = f_in.at[4]

    def spans(sx, sy, n, wide_x, wide_y):
        ax, ay = source_span(sx, n, wide_x), source_span(sy, n, wide_y)
        return (
            slice(ax[0] + O, ax[1] + O),
            slice(ay[0] + O, ay[1] + O),
            slice(*target_span(sx, n, wide_x)),
            slice(*target_span(sy, n, wide_y)),
        )

    faces_x = [step for step in NEIGHBOURS if step[1] == 0]
    faces_y = [step for step in NEIGHBOURS if step[0] == 0]
    corners = [step for step in NEIGHBOURS if step[0] != 0 and step[1] != 0]

    for copy in fine_in:
        copy.wait()
    pl.semaphore_wait(barrier, len(NEIGHBOURS) + GROUP - 1)

    fine_halo = []

    def push_fine(fields, step, wide):
        ax, ay, bx, by = spans(*step, 8, wide, wide)
        fine_halo.append(push(f_in.at[fields, ax, :, ay, :], f_in.at[fields, bx, :, by, :], beside(*step)))

    for step in faces_x:
        push_fine(slice(0, 1), step, 3)
        push_fine(slice(1, 5), step, 2)
    for step in corners:
        push_fine(slice(0, 5), step, 2)
    for copy in coarse_in:
        copy.wait()
    coarse_halo = [
        push(c_coef.at[:, 0:2, 0:2, :], c_coef.at[:, 2 * d : 2 * d + 2, 0:2, :], member(GROUP - d))
        for d in range(1, GROUP)
    ]
    for step in faces_y:
        push_fine(slice(0, 5), step, 3)

    for copy in mid_in:
        copy.wait()
    mid_halo = []
    for step in NEIGHBOURS:
        wide = 3 if step in corners else 4
        ax, ay, bx, by = spans(*step, 4, wide, wide)
        mid_halo.append(push(m_in.at[:, ax, ay, :], m_in.at[:, bx, by, :], beside(*step)))

    one = jnp.float32(1.0)
    nil = jnp.float32(0.0)
    keep_x = (jnp.where(gx == 0, nil, one), jnp.where(gx == count_x - 1, nil, one))

    def keep_yz(own, shape):
        row = lax.broadcasted_iota(jnp.int32, shape, len(shape) - 2)
        column = lax.broadcasted_iota(jnp.int32, shape, len(shape) - 1)
        if len(shape) == 3:
            column = column + 128 * lax.broadcasted_iota(jnp.int32, shape, 0)
        columns = 128 * (len(shape) - 1)
        end = jnp.where(gy == 0, O - 1, -1)
        other = jnp.where(gy == count_y - 1, O + own - 1, -1)
        keep_y = jnp.where((row == end) | (row == other), 0.0, 1.0)
        keep_z = jnp.where(column == columns - 1, 0.0, 1.0)
        return keep_y, keep_z

    half_f = one_hot((256, 128), lambda row, column: row // 2 == column)
    half_m = one_hot((64, 128), lambda row, column: row == column // 2)

    for copy in coarse_halo:
        copy.wait_recv()
    coef = [c_coef[k].reshape(128, 64).T for k in range(4)]
    column = lax.broadcasted_iota(jnp.int32, (64, 128), 1)
    level_row = lax.broadcasted_iota(jnp.int32, (64, 128), 0)
    cell_y = column // 8
    holder = lax.rem(place + cell_y // 2, GROUP)
    last_cell = (holder == GROUP - 1) | (lax.rem(leader + holder, count_y) == count_y - 1)
    shut = last_cell & (lax.rem(cell_y, 2) == 1)
    up_x = jnp.where(lax.rem(column, 8) == 0, harmonic(coef[1], next_of(coef[1], 1)), 0.0)
    down_x = prev_of(up_x, 1)
    up_y = jnp.where(shut, 0.0, harmonic(coef[2], pltpu.roll(coef[2], 120, 1)))
    down_y = pltpu.roll(up_y, 8, 1)
    up_z = jnp.where(level_row == 63, 0.0, harmonic(coef[3], next_of(coef[3], 0)))
    down_z = prev_of(up_z, 0)
    c_weights[0] = up_x
    c_weights[1] = down_x
    c_weights[2] = up_y
    c_weights[3] = down_y
    main = coef[0] + (up_x + down_x) + (up_y + down_y) + (up_z + down_z)
    low, high = -down_z, -up_z
    for step in range(6):
        far = 1 << step
        inverse = reciprocal(main)
        alpha = -low * pltpu.roll(inverse, far, 0)
        gamma = -high * pltpu.roll(inverse, 64 - far, 0)
        c_alpha[step] = alpha
        c_gamma[step] = gamma
        main = main + alpha * pltpu.roll(high, far, 0) + gamma * pltpu.roll(low, 64 - far, 0)
        low, high = alpha * pltpu.roll(low, far, 0), gamma * pltpu.roll(high, 64 - far, 0)
    c_weights[4] = reciprocal(main)

    def lines(values):
        for step in range(6):
            far = 1 << step
            lower = pltpu.roll(values, far, 0)
            upper = pltpu.roll(values, 64 - far, 0)
            values = values + c_alpha[step] * lower + c_gamma[step] * upper
        return values * c_weights[4]

    fine = (f_wx, f_wyu, f_wyd, f_wzu, f_wzd, f_diag, f_damp)
    for copy in fine_halo:
        copy.wait_recv()
    keep_y, keep_z = keep_yz(8, (2, ROWS, 128))
    face_weights(fine, f_in, 8, (O - 2, O + 10), keep_x, keep_y, keep_z)
    start_sweep(fine, f_src, f_a, (O - 2, O + 10))
    sweep(fine, f_src, f_a, f_b, (O - 1, O + 9))

    def folded(x, _):
        first = row_residual(fine, f_src, f_b, O + 2 * x)
        f_spread[x] = first + row_residual(fine, f_src, f_b, O + 2 * x + 1)
        return 0

    lax.fori_loop(0, 4, folded, 0, unroll=True)
    halves = [f_spread[0:4, half].reshape(4 * ROWS, 128) for half in range(2)]
    m_fold[0:4] = times_one_hot(jnp.concatenate(halves, axis=1), half_f).reshape(4, ROWS, 128)

    def pairs(x, _):
        even = m_fold[x, pl.ds(O, 4, stride=2), :]
        m_src[O + x, O : O + 4, :] = even + m_fold[x, pl.ds(O + 1, 4, stride=2), :]
        return 0

    lax.fori_loop(0, 4, pairs, 0, unroll=True)

    mid_source = []
    for sx, sy in NEIGHBOURS:
        wide = 2 if sx != 0 and sy != 0 else 3
        ax, ay, bx, by = spans(sx, sy, 4, wide, wide)
        mid_source.append(push(m_src.at[ax, ay, :], m_src.at[bx, by, :], beside(sx, sy)))

    def keep_fine(x, _):
        f_x[x, :, O : O + 8, :] = f_b[x, :, O : O + 8, :]
        return 0

    lax.fori_loop(O, O + 8, keep_fine, 0, unroll=True)
    fine_iterate = []
    for sx, sy in NEIGHBOURS:
        wide = 2 if sx != 0 and sy != 0 else 3
        ax, ay, bx, by = spans(sx, sy, 8, wide, wide)
        fine_iterate.append(push(f_x.at[ax, :, ay, :], f_x.at[bx, :, by, :], beside(sx, sy)))

    for copy in fine_halo + coarse_halo + mid_halo:
        copy.wait_send()

    mid = (m_wx, m_wyu, m_wyd, m_wzu, m_wzd, m_diag, m_damp)
    for copy in mid_halo:
        copy.wait_recv()
    keep_y, keep_z = keep_yz(4, (ROWS, 128))
    face_weights(mid, m_in, 4, (O - 3, O + 7), keep_x, keep_y, keep_z)
    for copy in mid_source:
        copy.wait_recv()
    start_sweep(mid, m_src, m_a, (O - 2, O + 6))
    sweep(mid, m_src, m_a, m_b, (O - 1, O + 5))
    for ix in range(2):
        fold = row_residual(mid, m_src, m_b, O + 2 * ix) + row_residual(mid, m_src, m_b, O + 2 * ix + 1)
        for iy in range(2):
            c_src[iy, ix : ix + 1, :] = fold[O + 2 * iy : O + 2 * iy + 1] + fold[O + 2 * iy + 1 : O + 2 * iy + 2]
    coarse_source = [
        push(c_src.at[0:2, 0:2, :], c_src.at[2 * d : 2 * d + 2, 0:2, :], member(GROUP - d))
        for d in range(1, GROUP)
    ]

    def keep_mid(x, _):
        m_y[x, O : O + 4, :] = m_b[x, O : O + 4, :]
        return 0

    lax.fori_loop(O, O + 4, keep_mid, 0, unroll=True)
    mid_iterate = []
    for sx, sy in NEIGHBOURS:
        wide = 3 if sx != 0 and sy != 0 else 4
        ax, ay, bx, by = spans(sx, sy, 4, wide, wide)
        mid_iterate.append(push(m_y.at[ax, ay, :], m_y.at[bx, by, :], beside(sx, sy)))

    for copy in coarse_source:
        copy.wait_recv()
    source = lax.dot_general(
        jnp.concatenate([half_m] * 3, axis=1),
        jnp.concatenate(thirds(c_src[...].reshape(128, 128)), axis=1),
        (((1,), (1,)), ((), ())),
        preferred_element_type=jnp.float32,
    )

    def turn(_, z):
        pushed = source + (c_weights[0] * next_of(z, 1) + c_weights[1] * prev_of(z, 1))
        pushed = pushed + (c_weights[2] * pltpu.roll(z, 120, 1) + c_weights[3] * pltpu.roll(z, 8, 1))
        return lines(pushed)

    z = lax.fori_loop(0, KC - 1, turn, lines(source))
    spread = times_one_hot(z.T[0:16], half_m)
    for ix in range(2):
        for iy in range(2):
            c_ext[2 + ix, 2 + iy : 3 + iy, :] = spread[8 * iy + ix : 8 * iy + ix + 1]
    coarse_iterate = []
    for sx, sy in NEIGHBOURS:
        target = c_ext.at[2 - 2 * sx : 4 - 2 * sx, 2 - 2 * sy : 4 - 2 * sy, :]
        coarse_iterate.append(push(c_ext.at[2:4, 2:4, :], target, beside(sx, sy)))

    for copy in mid_source + fine_iterate + coarse_source + mid_iterate:
        copy.wait_send()

    for copy in mid_iterate:
        copy.wait_recv()
    for copy in coarse_iterate:
        copy.wait_recv()

    def raise_mid(x, _):
        rows = c_ext[x]
        c_spread[x, pl.ds(0, 8, stride=2), :] = rows
        c_spread[x, pl.ds(1, 8, stride=2), :] = rows
        doubled = c_spread[x]
        m_a[2 * x] = m_y[2 * x] + doubled
        m_a[2 * x + 1] = m_y[2 * x + 1] + doubled
        return 0

    lax.fori_loop(0, 6, raise_mid, 0, unroll=True)
    sweep(mid, m_src, m_a, m_b, (O - 3, O + 7))
    sweep(mid, m_src, m_b, m_a, (O - 2, O + 6))

    def raise_rows(x, _):
        rows = m_a[O - 2 + x, O - 2 : O + 6, :]
        m_fold[x, pl.ds(0, 8, stride=2), :] = rows
        m_fold[x, pl.ds(1, 8, stride=2), :] = rows
        return 0

    lax.fori_loop(0, 8, raise_rows, 0, unroll=True)
    double_f = one_hot((128, 256), lambda row, column: row == column // 2)
    doubled_z = times_one_hot(m_fold[...].reshape(8 * ROWS, 128), double_f)
    for half in range(2):
        f_spread[:, half] = doubled_z[:, 128 * half : 128 * half + 128].reshape(8, ROWS, 128)
    for copy in fine_iterate:
        copy.wait_recv()

    def raise_fine(x, _):
        f_a[2 * x] = f_x[2 * x] + f_spread[x]
        f_a[2 * x + 1] = f_x[2 * x + 1] + f_spread[x]
        return 0

    lax.fori_loop(0, 8, raise_fine, 0, unroll=True)
    sweep(fine, f_src, f_a, f_b, (O - 2, O + 10))
    sweep(fine, f_src, f_b, f_a, (O - 1, O + 9))
    outs = [
        bring(f_a.at[own8, half, own8, :], pressure_h.at[:, :, 128 * half : 128 * half + 128])
        for half in range(2)
    ]

    def last(x, _):
        f_b[x] = row_residual(fine, f_src, f_a, x)
        return 0

    lax.fori_loop(O, O + 8, last, 0, unroll=True)
    for half in range(2):
        outs.append(bring(f_b.at[own8, half, own8, :], residual_h.at[:, :, 128 * half : 128 * half + 128]))
    for copy in coarse_iterate:
        copy.wait_send()
    for copy in outs:
        copy.wait()


def local(pressure_rhs, storage_fine, mobility_fine, storage_mid, mobility_mid, storage_coarse, mobility_coarse):
    count_x = lax.axis_size("gx")
    count_y = lax.axis_size("gy")
    f32 = jnp.float32
    fine = pltpu.VMEM((8 + 2 * O, 2, ROWS, 128), f32)
    mid = pltpu.VMEM((4 + 2 * O, ROWS, 128), f32)
    anywhere = pl.BlockSpec(memory_space=pl.ANY)
    out = jax.ShapeDtypeStruct(pressure_rhs.shape, f32)
    return pl.pallas_call(
        functools.partial(kernel, count_x, count_y),
        out_shape=(out, out),
        in_specs=[anywhere] * 7,
        out_specs=(anywhere, anywhere),
        scratch_shapes=[
            pltpu.VMEM((5, 8 + 2 * O, 2, ROWS, 128), f32),
            *[fine] * 10,
            pltpu.VMEM((4, 4 + 2 * O, ROWS, 128), f32),
            *[mid] * 11,
            pltpu.VMEM((8, ROWS, 128), f32),
            pltpu.VMEM((8, 2, ROWS, 128), f32),
            pltpu.VMEM((4, 16, 8, 64), f32),
            pltpu.VMEM((16, 8, 128), f32),
            pltpu.VMEM((6, 8, 128), f32),
            pltpu.VMEM((6, ROWS, 128), f32),
            pltpu.VMEM((5, 64, 128), f32),
            pltpu.VMEM((6, 64, 128), f32),
            pltpu.VMEM((6, 64, 128), f32),
            pltpu.SemaphoreType.DMA((16,)),
            pltpu.SemaphoreType.DMA((96,)),
            pltpu.SemaphoreType.DMA((96,)),
        ],
        compiler_params=pltpu.CompilerParams(
            collective_id=0, has_side_effects=True, vmem_limit_bytes=56 * 1024 * 1024
        ),
    )(pressure_rhs, storage_fine, mobility_fine, storage_mid, mobility_mid, storage_coarse, mobility_coarse)


def solution(mesh):
    placed = (
        P("gx", "gy", None),
        P("gx", "gy", None),
        P(None, "gx", "gy", None),
        P("gx", "gy", None),
        P(None, "gx", "gy", None),
        P("gx", "gy", None),
        P(None, "gx", "gy", None),
    )
    return jax.shard_map(
        local,
        mesh=mesh,
        in_specs=placed,
        out_specs=(P("gx", "gy", None), P("gx", "gy", None)),
        check_vma=False,
    )
```

```python
import functools

import jax
import jax.numpy as jnp
from jax import lax
from jax.experimental import pallas as pl
from jax.experimental.pallas import tpu as pltpu
from jax.sharding import PartitionSpec as P

KC = 6
GROUP = 8
REACH = 4
DAMPING = 2.0 / 3.0

MESH = pl.DeviceIdType.MESH

O = 4
ROWS = 16
OWN_C = slice(15, 17)
FINE_X, FINE_Y, COEF_X, COEF_Y, MID_IN, MID_F, FINE_V, COARSE_F, MID_V = range(9)
EXCHANGES = 9
NEIGHBOURS = ((1, 0), (-1, 0), (1, 1), (1, -1), (-1, 1), (-1, -1), (0, 1), (0, -1))


def reciprocal(values):
    guess = pl.reciprocal(values, approx=True)
    return guess * (2.0 - values * guess)


def harmonic(left, right):
    return 2.0 * left * right * reciprocal(left + right)


def next_of(values, axis):
    return pltpu.roll(values, values.shape[axis] - 1, axis)


def prev_of(values, axis):
    return pltpu.roll(values, 1, axis)


def swapped(values):
    return jnp.concatenate([values[1:2], values[0:1]], axis=0)


def next_z(values):
    moved = next_of(values, values.ndim - 1)
    if values.ndim == 2:
        return moved
    lane = lax.broadcasted_iota(jnp.int32, values.shape, 2)
    return jnp.where(lane == 127, swapped(moved), moved)


def prev_z(values):
    moved = prev_of(values, values.ndim - 1)
    if values.ndim == 2:
        return moved
    lane = lax.broadcasted_iota(jnp.int32, values.shape, 2)
    return jnp.where(lane == 0, swapped(moved), moved)


def next_y(values):
    return next_of(values, values.ndim - 2)


def prev_y(values):
    return prev_of(values, values.ndim - 2)


def one_hot(shape, test):
    row = lax.broadcasted_iota(jnp.int32, shape, 0)
    column = lax.broadcasted_iota(jnp.int32, shape, 1)
    return jnp.where(test(row, column), 1.0, 0.0).astype(jnp.bfloat16)


def thirds(values):
    head = values.astype(jnp.bfloat16)
    rest = values - head.astype(jnp.float32)
    middle = rest.astype(jnp.bfloat16)
    tail = (rest - middle.astype(jnp.float32)).astype(jnp.bfloat16)
    return [head, middle, tail]


def times_one_hot(values, matrix):
    rows = values.shape[0]
    product = jnp.dot(jnp.concatenate(thirds(values), axis=0), matrix, preferred_element_type=jnp.float32)
    return product[:rows] + product[rows : 2 * rows] + product[2 * rows :]


def source_span(step, n, width):
    return (n - width, n) if step > 0 else (0, width) if step < 0 else (0, n)


def target_span(step, n, width):
    return (O - width, O) if step > 0 else (O + n, O + n + width) if step < 0 else (O, O + n)


def weights_x(level, field, rows):
    wx = level[0]

    def body(x, _):
        wx[x] = harmonic(field[0, x], field[0, x + 1])
        return 0

    lax.fori_loop(*rows, body, 0, unroll=True)


def weights_yz(level, field, rows, keep_y, keep_z):
    wx, wyu, wyd, wzu, wzd, diag, damp = level

    def body(x, _):
        second = field[1, x]
        third = field[2, x]
        up_y = harmonic(second, next_y(second)) * keep_y
        up_z = harmonic(third, next_z(third)) * keep_z
        wyu[x] = up_y
        wyd[x] = prev_y(up_y)
        wzu[x] = up_z
        wzd[x] = prev_z(up_z)
        return 0

    lax.fori_loop(*rows, body, 0, unroll=True)


def diagonals(level, field, rows):
    wx, wyu, wyd, wzu, wzd, diag, damp = level

    def body(x, _):
        total = field[3, x] + (wx[x] + wx[x - 1]) + (wyu[x] + wyd[x]) + (wzu[x] + wzd[x])
        diag[x] = total
        damp[x] = DAMPING * reciprocal(total)
        return 0

    lax.fori_loop(*rows, body, 0, unroll=True)


def row_residual(level, source, field, x):
    wx, wyu, wyd, wzu, wzd, diag, damp = level
    v = field[x]
    left = source[x] - diag[x] * v
    left = left + (wx[x] * field[x + 1] + wx[x - 1] * field[x - 1])
    left = left + (wyu[x] * next_y(v) + wyd[x] * prev_y(v))
    left = left + (wzu[x] * next_z(v) + wzd[x] * prev_z(v))
    return left


def sweep(level, source, field, result, rows):
    damp = level[6]

    def body(x, _):
        result[x] = field[x] + damp[x] * row_residual(level, source, field, x)
        return 0

    lax.fori_loop(rows[0], rows[1], body, 0, unroll=True)


def start_sweep(level, source, result, rows):
    damp = level[6]

    def body(x, _):
        result[x] = damp[x] * source[x]
        return 0

    lax.fori_loop(rows[0], rows[1], body, 0, unroll=True)


def kernel(
    count_x,
    count_y,
    rhs_h,
    store_f_h,
    mob_f_h,
    store_m_h,
    mob_m_h,
    store_c_h,
    mob_c_h,
    pressure,
    residual,
    f_in,
    f_wx,
    f_wyu,
    f_wyd,
    f_wzu,
    f_wzd,
    f_diag,
    f_damp,
    f_a,
    f_b,
    f_x,
    m_in,
    m_src,
    m_wx,
    m_wyu,
    m_wyd,
    m_wzu,
    m_wzd,
    m_diag,
    m_damp,
    m_a,
    m_b,
    m_y,
    m_fold,
    f_spread,
    c_coef,
    c_src,
    c_ext,
    c_spread,
    c_weights,
    c_alpha,
    c_gamma,
    meter,
    local_sem,
    send_sem,
    recv_sem,
):
    gx = lax.axis_index("gx")
    gy = lax.axis_index("gy")

    def beside(sx, sy):
        return {
            "gx": lax.rem(gx + (sx + count_x), count_x),
            "gy": lax.rem(gy + (sy + count_y), count_y),
        }

    c_coef[:, 6:8] = jnp.ones((4, 2, 32, 64), jnp.float32)
    c_src[6:8] = jnp.zeros((2, 32, 128), jnp.float32)

    partners = NEIGHBOURS + tuple((0, e) for e in range(-REACH, REACH + 1) if abs(e) > 1)
    barrier = pltpu.get_barrier_semaphore()
    for step in partners:
        pl.semaphore_signal(barrier, inc=1, device_id=beside(*step), device_id_type=MESH)

    locals_ = []

    def bring(source, target):
        copy = pltpu.make_async_copy(source, target, local_sem.at[len(locals_)])
        copy.start()
        locals_.append(copy)
        return copy

    def push(at, source, target, step):
        pltpu.make_async_remote_copy(
            src_ref=source,
            dst_ref=target,
            send_sem=send_sem.at[at],
            recv_sem=recv_sem.at[at],
            device_id=beside(*step),
            device_id_type=MESH,
        ).start()
        rows = 1
        for size in source.shape[:-1]:
            rows = rows * size
        rows_of[at] = rows_of.get(at, 0) + rows

    rows_of = {}

    def all_of(at):
        if at == COEF_X:
            return c_coef.at[:, 0:4, 0:2, :]
        if at == COEF_Y:
            return c_coef.at[:, 0:6, 0:16, :]
        return meter.at[0 : rows_of[at], :]

    def received(at):
        pltpu.make_async_copy(all_of(at), all_of(at), recv_sem.at[at]).wait()

    def sent(at):
        pltpu.make_async_copy(all_of(at), all_of(at), send_sem.at[at]).wait()

    own8 = slice(O, O + 8)
    own4 = slice(O, O + 4)
    fine_in = []
    for half in range(2):
        z = slice(128 * half, 128 * half + 128)
        fine_in.append(bring(mob_f_h.at[:, :, :, z], f_in.at[0:3, own8, half, own8, :]))
        fine_in.append(bring(store_f_h.at[:, :, z], f_in.at[3, own8, half, own8, :]))
        fine_in.append(bring(rhs_h.at[:, :, z], f_in.at[4, own8, half, own8, :]))
    coarse_in = [
        bring(store_c_h, c_coef.at[0, 2:4, OWN_C, :]),
        bring(mob_c_h, c_coef.at[1:4, 2:4, OWN_C, :]),
    ]
    mid_in = [
        bring(mob_m_h, m_in.at[0:3, own4, own4, :]),
        bring(store_m_h, m_in.at[3, own4, own4, :]),
    ]
    f_src = f_in.at[4]

    def spans(sx, sy, n, wide_x, wide_y):
        ax, ay = source_span(sx, n, wide_x), source_span(sy, n, wide_y)
        return (
            slice(ax[0] + O, ax[1] + O),
            slice(ay[0] + O, ay[1] + O),
            slice(*target_span(sx, n, wide_x)),
            slice(*target_span(sy, n, wide_y)),
        )

    faces_x = [step for step in NEIGHBOURS if step[1] == 0]
    faces_y = [step for step in NEIGHBOURS if step[0] == 0]
    corners = [step for step in NEIGHBOURS if step[0] != 0 and step[1] != 0]

    for copy in fine_in:
        copy.wait()
    pl.semaphore_wait(barrier, len(partners))

    def push_fine(at, fields, step, wide):
        ax, ay, bx, by = spans(*step, 8, wide, wide)
        push(at, f_in.at[fields, ax, :, ay, :], f_in.at[fields, bx, :, by, :], step)

    for step in faces_x:
        push_fine(FINE_X, slice(0, 1), step, 3)
        push_fine(FINE_X, slice(1, 5), step, 2)
    for step in corners:
        push_fine(FINE_X, slice(0, 5), step, 2)
    for step in faces_y:
        push_fine(FINE_Y, slice(0, 5), step, 3)

    for copy in coarse_in:
        copy.wait()
    for sx, sy in faces_x:
        own = c_coef.at[:, 2:4, OWN_C, :]
        push(COEF_X, own, c_coef.at[:, 2 - 2 * sx : 4 - 2 * sx, OWN_C, :], (sx, sy))

    for copy in mid_in:
        copy.wait()
    for step in NEIGHBOURS:
        wide = 3 if step in corners else 4
        ax, ay, bx, by = spans(*step, 4, wide, wide)
        push(MID_IN, m_in.at[:, ax, ay, :], m_in.at[:, bx, by, :], step)

    one = jnp.float32(1.0)
    nil = jnp.float32(0.0)
    keep_x = (jnp.where(gx == 0, nil, one), jnp.where(gx == count_x - 1, nil, one))

    def keep_yz(own, shape):
        row = lax.broadcasted_iota(jnp.int32, shape, len(shape) - 2)
        column = lax.broadcasted_iota(jnp.int32, shape, len(shape) - 1)
        if len(shape) == 3:
            column = column + 128 * lax.broadcasted_iota(jnp.int32, shape, 0)
        columns = 128 * (len(shape) - 1)
        end = jnp.where(gy == 0, O - 1, -1)
        other = jnp.where(gy == count_y - 1, O + own - 1, -1)
        keep_y = jnp.where((row == end) | (row == other), 0.0, 1.0)
        keep_z = jnp.where(column == columns - 1, 0.0, 1.0)
        return keep_y, keep_z

    half_f = one_hot((256, 128), lambda row, column: row // 2 == column)
    half_m = one_hot((64, 128), lambda row, column: row == column // 2)

    fine = (f_wx, f_wyu, f_wyd, f_wzu, f_wzd, f_diag, f_damp)
    keep_y, keep_z = keep_yz(8, (2, ROWS, 128))
    received(FINE_Y)
    weights_yz(fine, f_in, (O, O + 8), keep_y, keep_z)
    weights_x(fine, f_in, (O, O + 7))
    diagonals(fine, f_in, (O + 1, O + 7))
    start_sweep(fine, f_src, f_a, (O + 1, O + 7))
    received(COEF_X)
    for e in range(-REACH, REACH + 1):
        if e != 0:
            target = c_coef.at[:, 0:6, OWN_C.start - 2 * e : OWN_C.stop - 2 * e, :]
            push(COEF_Y, c_coef.at[:, 0:6, OWN_C, :], target, (0, e))
    received(FINE_X)
    for rows in ((O - 3, O), (O + 7, O + 10)):
        weights_x(fine, f_in, rows)
    f_wx[O - 1] = f_wx[O - 1] * keep_x[0]
    f_wx[O + 7] = f_wx[O + 7] * keep_x[1]
    for rows in ((O - 2, O), (O + 8, O + 10)):
        weights_yz(fine, f_in, rows, keep_y, keep_z)
    for rows in ((O - 2, O + 1), (O + 7, O + 10)):
        diagonals(fine, f_in, rows)
        start_sweep(fine, f_src, f_a, rows)
    sweep(fine, f_src, f_a, f_b, (O - 1, O + 9))

    def folded(x, _):
        first = row_residual(fine, f_src, f_b, O + 2 * x)
        f_spread[x] = first + row_residual(fine, f_src, f_b, O + 2 * x + 1)
        return 0

    lax.fori_loop(0, 4, folded, 0, unroll=True)
    halves = [f_spread[0:4, half].reshape(4 * ROWS, 128) for half in range(2)]
    m_fold[0:4] = times_one_hot(jnp.concatenate(halves, axis=1), half_f).reshape(4, ROWS, 128)

    def pairs(x, _):
        even = m_fold[x, pl.ds(O, 4, stride=2), :]
        m_src[O + x, O : O + 4, :] = even + m_fold[x, pl.ds(O + 1, 4, stride=2), :]
        return 0

    lax.fori_loop(0, 4, pairs, 0, unroll=True)

    for sx, sy in NEIGHBOURS:
        wide = 2 if sx != 0 and sy != 0 else 3
        ax, ay, bx, by = spans(sx, sy, 4, wide, wide)
        push(MID_F, m_src.at[ax, ay, :], m_src.at[bx, by, :], (sx, sy))

    def keep_fine(x, _):
        f_x[x, :, O : O + 8, :] = f_b[x, :, O : O + 8, :]
        return 0

    lax.fori_loop(O, O + 8, keep_fine, 0, unroll=True)
    for sx, sy in NEIGHBOURS:
        wide = 2 if sx != 0 and sy != 0 else 3
        ax, ay, bx, by = spans(sx, sy, 8, wide, wide)
        push(FINE_V, f_x.at[ax, :, ay, :], f_x.at[bx, :, by, :], (sx, sy))

    mid = (m_wx, m_wyu, m_wyd, m_wzu, m_wzd, m_diag, m_damp)
    keep_y, keep_z = keep_yz(4, (ROWS, 128))
    received(MID_IN)
    weights_x(mid, m_in, (O - 4, O + 7))
    m_wx[O - 1] = m_wx[O - 1] * keep_x[0]
    m_wx[O + 3] = m_wx[O + 3] * keep_x[1]
    weights_yz(mid, m_in, (O - 3, O + 7), keep_y, keep_z)
    diagonals(mid, m_in, (O - 3, O + 7))

    received(COEF_Y)
    coef = [c_coef[k, :, 8:24, :].reshape(128, 64).T for k in range(4)]
    second_prev = c_coef[2, :, 7:23, :].reshape(128, 64).T
    second_next = c_coef[2, :, 9:25, :].reshape(128, 64).T
    column = lax.broadcasted_iota(jnp.int32, (64, 128), 1)
    level_row = lax.broadcasted_iota(jnp.int32, (64, 128), 0)
    cells = 2 * count_y
    cell = 2 * gy + lax.rem(column, 16) + (cells - 7)
    block = 2 * GROUP
    offset = 4 + cells - (cells // block) * block
    shut_up = (lax.rem(cell + 1 - offset + 2 * block, block) == 0) | (lax.rem(cell + 1, cells) == 0)
    shut_down = (lax.rem(cell - offset + 2 * block, block) == 0) | (lax.rem(cell, cells) == 0)
    up_x = jnp.where(lax.rem(column, 32) < 16, harmonic(coef[1], pltpu.roll(coef[1], 112, 1)), 0.0)
    down_x = pltpu.roll(up_x, 16, 1)
    up_y = jnp.where(shut_up, 0.0, harmonic(coef[2], second_next))
    down_y = jnp.where(shut_down, 0.0, harmonic(second_prev, coef[2]))
    up_z = jnp.where(level_row == 63, 0.0, harmonic(coef[3], next_of(coef[3], 0)))
    down_z = prev_of(up_z, 0)
    c_weights[0] = up_x
    c_weights[1] = down_x
    c_weights[2] = up_y
    c_weights[3] = down_y
    main = coef[0] + (up_x + down_x) + (up_y + down_y) + (up_z + down_z)
    low, high = -down_z, -up_z
    for step in range(6):
        far = 1 << step
        inverse = reciprocal(main)
        alpha = -low * pltpu.roll(inverse, far, 0)
        gamma = -high * pltpu.roll(inverse, 64 - far, 0)
        c_alpha[step] = alpha
        c_gamma[step] = gamma
        main = main + alpha * pltpu.roll(high, far, 0) + gamma * pltpu.roll(low, 64 - far, 0)
        low, high = alpha * pltpu.roll(low, far, 0), gamma * pltpu.roll(high, 64 - far, 0)
    c_weights[4] = reciprocal(main)

    def lines(values):
        for step in range(6):
            far = 1 << step
            lower = pltpu.roll(values, far, 0)
            upper = pltpu.roll(values, 64 - far, 0)
            values = values + c_alpha[step] * lower + c_gamma[step] * upper
        return values * c_weights[4]

    for at in (FINE_X, FINE_Y, COEF_X, COEF_Y, MID_IN):
        sent(at)

    received(MID_F)
    start_sweep(mid, m_src, m_a, (O - 2, O + 6))
    sweep(mid, m_src, m_a, m_b, (O - 1, O + 5))
    for ix in range(2):
        fold = row_residual(mid, m_src, m_b, O + 2 * ix) + row_residual(mid, m_src, m_b, O + 2 * ix + 1)
        for iy in range(2):
            first = O + 2 * iy
            at = OWN_C.start + iy
            c_src[2 + ix, at : at + 1, :] = fold[first : first + 1] + fold[first + 1 : first + 2]
    for e in sorted(range(-REACH, REACH + 1), key=lambda e: -abs(e)):
        for g in (1, -1, 0):
            if (g, e) != (0, 0):
                target = c_src.at[2 - 2 * g : 4 - 2 * g, OWN_C.start - 2 * e : OWN_C.stop - 2 * e, :]
                push(COARSE_F, c_src.at[2:4, OWN_C, :], target, (g, e))

    def keep_mid(x, _):
        m_y[x, O : O + 4, :] = m_b[x, O : O + 4, :]
        return 0

    lax.fori_loop(O, O + 4, keep_mid, 0, unroll=True)
    for sx, sy in NEIGHBOURS:
        wide = 3 if sx != 0 and sy != 0 else 4
        ax, ay, bx, by = spans(sx, sy, 4, wide, wide)
        push(MID_V, m_y.at[ax, ay, :], m_y.at[bx, by, :], (sx, sy))
    for at in (MID_F, FINE_V):
        sent(at)

    received(COARSE_F)
    source = lax.dot_general(
        jnp.concatenate([half_m] * 3, axis=1),
        jnp.concatenate(thirds(c_src[:, 8:24, :].reshape(128, 128)), axis=1),
        (((1,), (1,)), ((), ())),
        preferred_element_type=jnp.float32,
    )

    def turn(_, z):
        pushed = source + (c_weights[0] * pltpu.roll(z, 112, 1) + c_weights[1] * pltpu.roll(z, 16, 1))
        pushed = pushed + (c_weights[2] * next_of(z, 1) + c_weights[3] * prev_of(z, 1))
        return lines(pushed)

    z = lax.fori_loop(0, KC - 1, turn, lines(source))
    c_ext[...] = times_one_hot(z.T[0:96], half_m).reshape(6, 16, 128)

    received(MID_V)

    def raise_mid(x, _):
        rows = c_ext[x, 5:13, :]
        c_spread[x, pl.ds(0, 8, stride=2), :] = rows
        c_spread[x, pl.ds(1, 8, stride=2), :] = rows
        doubled = c_spread[x]
        m_a[2 * x] = m_y[2 * x] + doubled
        m_a[2 * x + 1] = m_y[2 * x + 1] + doubled
        return 0

    lax.fori_loop(0, 6, raise_mid, 0, unroll=True)
    sweep(mid, m_src, m_a, m_b, (O - 3, O + 7))
    sweep(mid, m_src, m_b, m_a, (O - 2, O + 6))

    def raise_rows(x, _):
        rows = m_a[O - 2 + x, O - 2 : O + 6, :]
        m_fold[x, pl.ds(0, 8, stride=2), :] = rows
        m_fold[x, pl.ds(1, 8, stride=2), :] = rows
        return 0

    lax.fori_loop(0, 8, raise_rows, 0, unroll=True)
    double_f = one_hot((128, 256), lambda row, column: row == column // 2)
    doubled_z = times_one_hot(m_fold[...].reshape(8 * ROWS, 128), double_f)
    for half in range(2):
        f_spread[:, half] = doubled_z[:, 128 * half : 128 * half + 128].reshape(8, ROWS, 128)
    received(FINE_V)

    def raise_fine(x, _):
        f_a[2 * x] = f_x[2 * x] + f_spread[x]
        f_a[2 * x + 1] = f_x[2 * x + 1] + f_spread[x]
        return 0

    lax.fori_loop(0, 8, raise_fine, 0, unroll=True)
    sweep(fine, f_src, f_a, f_b, (O - 2, O + 10))
    sweep(fine, f_src, f_b, f_a, (O - 1, O + 9))

    def last(x, _):
        left = row_residual(fine, f_src, f_a, x)
        own = f_a[x]
        for half in range(2):
            columns = slice(128 * half, 128 * half + 128)
            pressure[x - O, :, columns] = own[half, O : O + 8]
            residual[x - O, :, columns] = left[half, O : O + 8]
        return 0

    lax.fori_loop(O, O + 8, last, 0, unroll=True)
    for at in (COARSE_F, MID_V):
        sent(at)


def publish(pressure, residual, pressure_h, residual_h, sem):
    copies = [
        pltpu.make_async_copy(pressure, pressure_h, sem.at[0]),
        pltpu.make_async_copy(residual, residual_h, sem.at[1]),
    ]
    for copy in copies:
        copy.start()
    for copy in copies:
        copy.wait()


def local(pressure_rhs, storage_fine, mobility_fine, storage_mid, mobility_mid, storage_coarse, mobility_coarse):
    count_x = lax.axis_size("gx")
    count_y = lax.axis_size("gy")
    f32 = jnp.float32
    fine = pltpu.VMEM((8 + 2 * O, 2, ROWS, 128), f32)
    mid = pltpu.VMEM((4 + 2 * O, ROWS, 128), f32)
    in_hbm = pl.BlockSpec(memory_space=pltpu.HBM)
    in_vmem = pl.BlockSpec(memory_space=pltpu.VMEM)
    arrays = (pressure_rhs, storage_fine, mobility_fine, storage_mid, mobility_mid, storage_coarse, mobility_coarse)
    result = pl.pallas_call(
        functools.partial(kernel, count_x, count_y),
        out_shape=(pltpu.VMEM(pressure_rhs.shape, f32),) * 2,
        in_specs=[in_hbm] * 7,
        out_specs=(in_vmem, in_vmem),
        scratch_shapes=[
            pltpu.VMEM((5, 8 + 2 * O, 2, ROWS, 128), f32),
            *[fine] * 10,
            pltpu.VMEM((4, 4 + 2 * O, ROWS, 128), f32),
            *[mid] * 11,
            pltpu.VMEM((8, ROWS, 128), f32),
            pltpu.VMEM((8, 2, ROWS, 128), f32),
            pltpu.VMEM((4, 8, 32, 64), f32),
            pltpu.VMEM((8, 32, 128), f32),
            pltpu.VMEM((6, 16, 128), f32),
            pltpu.VMEM((6, ROWS, 128), f32),
            pltpu.VMEM((5, 64, 128), f32),
            pltpu.VMEM((6, 64, 128), f32),
            pltpu.VMEM((6, 64, 128), f32),
            pltpu.VMEM((1024, 128), f32),
            pltpu.SemaphoreType.DMA((16,)),
            pltpu.SemaphoreType.DMA((EXCHANGES,)),
            pltpu.SemaphoreType.DMA((EXCHANGES,)),
        ],
        compiler_params=pltpu.CompilerParams(
            collective_id=0, has_side_effects=True, vmem_limit_bytes=32 * 1024 * 1024
        ),
    )(*[pltpu.with_memory_space_constraint(array, pltpu.HBM) for array in arrays])
    out = jax.ShapeDtypeStruct(pressure_rhs.shape, f32)
    return pl.pallas_call(
        publish,
        out_shape=(out, out),
        in_specs=[in_vmem] * 2,
        out_specs=(in_hbm, in_hbm),
        scratch_shapes=[pltpu.SemaphoreType.DMA((2,))],
        compiler_params=pltpu.CompilerParams(vmem_limit_bytes=16 * 1024 * 1024),
    )(*result)


def solution(mesh):
    placed = (
        P("gx", "gy", None),
        P("gx", "gy", None),
        P(None, "gx", "gy", None),
        P("gx", "gy", None),
        P(None, "gx", "gy", None),
        P("gx", "gy", None),
        P(None, "gx", "gy", None),
    )
    return jax.shard_map(
        local,
        mesh=mesh,
        in_specs=placed,
        out_specs=(P("gx", "gy", None), P("gx", "gy", None)),
        check_vma=False,
    )
```

```python
import functools

import jax
import jax.numpy as jnp
from jax import lax
from jax.experimental import pallas as pl
from jax.experimental.pallas import tpu as pltpu
from jax.sharding import PartitionSpec as P

KC = 6
GROUP = 8
REACH = 4
DAMPING = 2.0 / 3.0

MESH = pl.DeviceIdType.MESH

O = 4
ROWS = 16
OWN_C = slice(15, 17)
FINE_X, FINE_Y, COEF_X, COEF_Y, MID_IN, MID_F, FINE_V, COARSE_F, MID_V = range(9)
EXCHANGES = 9
NEIGHBOURS = ((1, 0), (-1, 0), (1, 1), (1, -1), (-1, 1), (-1, -1), (0, 1), (0, -1))


def reciprocal(values):
    guess = pl.reciprocal(values, approx=True)
    return guess * (2.0 - values * guess)


def harmonic(left, right):
    return 2.0 * left * right * reciprocal(left + right)


def next_of(values, axis):
    return pltpu.roll(values, values.shape[axis] - 1, axis)


def prev_of(values, axis):
    return pltpu.roll(values, 1, axis)


def swapped(values):
    return jnp.concatenate([values[1:2], values[0:1]], axis=0)


def next_z(values):
    moved = next_of(values, values.ndim - 1)
    if values.ndim == 2:
        return moved
    lane = lax.broadcasted_iota(jnp.int32, values.shape, 2)
    return jnp.where(lane == 127, swapped(moved), moved)


def prev_z(values):
    moved = prev_of(values, values.ndim - 1)
    if values.ndim == 2:
        return moved
    lane = lax.broadcasted_iota(jnp.int32, values.shape, 2)
    return jnp.where(lane == 0, swapped(moved), moved)


def next_y(values):
    return next_of(values, values.ndim - 2)


def prev_y(values):
    return prev_of(values, values.ndim - 2)


def one_hot(shape, test):
    row = lax.broadcasted_iota(jnp.int32, shape, 0)
    column = lax.broadcasted_iota(jnp.int32, shape, 1)
    return jnp.where(test(row, column), 1.0, 0.0).astype(jnp.bfloat16)


def pieces(values):
    head = values.astype(jnp.bfloat16)
    return [head, (values - head.astype(jnp.float32)).astype(jnp.bfloat16)]


def times_one_hot(values, matrix):
    rows = values.shape[0]
    product = jnp.dot(jnp.concatenate(pieces(values), axis=0), matrix, preferred_element_type=jnp.float32)
    return product[:rows] + product[rows:]


def total(terms):
    while len(terms) > 1:
        pairs = [terms[i] + terms[i + 1] for i in range(0, len(terms) - 1, 2)]
        terms = pairs + terms[len(terms) - len(terms) % 2 :]
    return terms[0]


def source_span(step, n, width):
    return (n - width, n) if step > 0 else (0, width) if step < 0 else (0, n)


def target_span(step, n, width):
    return (O - width, O) if step > 0 else (O + n, O + n + width) if step < 0 else (O, O + n)


def weights_x(level, field, rows):
    wx = level[0]

    def body(x, _):
        wx[x] = harmonic(field[0, x], field[0, x + 1])
        return 0

    lax.fori_loop(*rows, body, 0, unroll=True)


def weights_yz(level, field, rows, keep_y, keep_z):
    wx, wyu, wyd, wzu, wzd, diag, damp = level

    def body(x, _):
        second = field[1, x]
        third = field[2, x]
        up_y = harmonic(second, next_y(second)) * keep_y
        up_z = harmonic(third, next_z(third)) * keep_z
        wyu[x] = up_y
        wyd[x] = prev_y(up_y)
        wzu[x] = up_z
        wzd[x] = prev_z(up_z)
        return 0

    lax.fori_loop(*rows, body, 0, unroll=True)


def diagonals(level, field, rows):
    wx, wyu, wyd, wzu, wzd, diag, damp = level

    def body(x, _):
        total = field[3, x] + (wx[x] + wx[x - 1]) + (wyu[x] + wyd[x]) + (wzu[x] + wzd[x])
        diag[x] = total
        damp[x] = DAMPING * reciprocal(total)
        return 0

    lax.fori_loop(*rows, body, 0, unroll=True)


def row_residual(level, source, field, x):
    wx, wyu, wyd, wzu, wzd, diag, damp = level
    v = field[x]
    left = source[x] - diag[x] * v
    left = left + (wx[x] * field[x + 1] + wx[x - 1] * field[x - 1])
    left = left + (wyu[x] * next_y(v) + wyd[x] * prev_y(v))
    left = left + (wzu[x] * next_z(v) + wzd[x] * prev_z(v))
    return left


def sweep(level, source, field, result, rows):
    damp = level[6]

    def body(x, _):
        result[x] = field[x] + damp[x] * row_residual(level, source, field, x)
        return 0

    lax.fori_loop(rows[0], rows[1], body, 0, unroll=True)


def start_sweep(level, source, result, rows):
    damp = level[6]

    def body(x, _):
        result[x] = damp[x] * source[x]
        return 0

    lax.fori_loop(rows[0], rows[1], body, 0, unroll=True)


def kernel(
    count_x,
    count_y,
    rhs_h,
    store_f_h,
    mob_f_h,
    store_m_h,
    mob_m_h,
    store_c_h,
    mob_c_h,
    pressure,
    residual,
    f_in,
    f_wx,
    f_wyu,
    f_wyd,
    f_wzu,
    f_wzd,
    f_diag,
    f_damp,
    f_a,
    f_b,
    f_x,
    m_in,
    m_src,
    m_wx,
    m_wyu,
    m_wyd,
    m_wzu,
    m_wzd,
    m_diag,
    m_damp,
    m_a,
    m_b,
    m_y,
    m_fold,
    f_spread,
    c_coef,
    c_src,
    c_ext,
    c_spread,
    c_weights,
    c_bands,
    c_inverse,
    meter,
    local_sem,
    send_sem,
    recv_sem,
):
    gx = lax.axis_index("gx")
    gy = lax.axis_index("gy")

    def beside(sx, sy):
        return {
            "gx": lax.rem(gx + (sx + count_x), count_x),
            "gy": lax.rem(gy + (sy + count_y), count_y),
        }

    c_coef[:, 6:8] = jnp.ones((4, 2, 32, 64), jnp.float32)
    c_src[6:8] = jnp.zeros((2, 32, 128), jnp.float32)

    partners = NEIGHBOURS + tuple((0, e) for e in range(-REACH, REACH + 1) if abs(e) > 1)
    barrier = pltpu.get_barrier_semaphore()
    for step in partners:
        pl.semaphore_signal(barrier, inc=1, device_id=beside(*step), device_id_type=MESH)

    locals_ = []

    def bring(source, target):
        copy = pltpu.make_async_copy(source, target, local_sem.at[len(locals_)])
        copy.start()
        locals_.append(copy)
        return copy

    def push(at, source, target, step):
        pltpu.make_async_remote_copy(
            src_ref=source,
            dst_ref=target,
            send_sem=send_sem.at[at],
            recv_sem=recv_sem.at[at],
            device_id=beside(*step),
            device_id_type=MESH,
        ).start()
        rows = 1
        for size in source.shape[:-1]:
            rows = rows * size
        rows_of[at] = rows_of.get(at, 0) + rows

    rows_of = {}

    def all_of(at):
        if at == COEF_X:
            return c_coef.at[:, 0:4, 0:2, :]
        if at == COEF_Y:
            return c_coef.at[:, 0:6, 0:16, :]
        return meter.at[0 : rows_of[at], :]

    def received(at):
        pltpu.make_async_copy(all_of(at), all_of(at), recv_sem.at[at]).wait()

    def sent(at):
        pltpu.make_async_copy(all_of(at), all_of(at), send_sem.at[at]).wait()

    own8 = slice(O, O + 8)
    own4 = slice(O, O + 4)
    fine_in = []
    for half in range(2):
        z = slice(128 * half, 128 * half + 128)
        fine_in.append(bring(mob_f_h.at[:, :, :, z], f_in.at[0:3, own8, half, own8, :]))
        fine_in.append(bring(store_f_h.at[:, :, z], f_in.at[3, own8, half, own8, :]))
        fine_in.append(bring(rhs_h.at[:, :, z], f_in.at[4, own8, half, own8, :]))
    coarse_in = [
        bring(store_c_h, c_coef.at[0, 2:4, OWN_C, :]),
        bring(mob_c_h, c_coef.at[1:4, 2:4, OWN_C, :]),
    ]
    mid_in = [
        bring(mob_m_h, m_in.at[0:3, own4, own4, :]),
        bring(store_m_h, m_in.at[3, own4, own4, :]),
    ]
    f_src = f_in.at[4]

    def spans(sx, sy, n, wide_x, wide_y):
        ax, ay = source_span(sx, n, wide_x), source_span(sy, n, wide_y)
        return (
            slice(ax[0] + O, ax[1] + O),
            slice(ay[0] + O, ay[1] + O),
            slice(*target_span(sx, n, wide_x)),
            slice(*target_span(sy, n, wide_y)),
        )

    faces_x = [step for step in NEIGHBOURS if step[1] == 0]
    faces_y = [step for step in NEIGHBOURS if step[0] == 0]
    corners = [step for step in NEIGHBOURS if step[0] != 0 and step[1] != 0]

    for copy in fine_in:
        copy.wait()
    pl.semaphore_wait(barrier, len(partners))

    def push_fine(at, fields, step, wide):
        ax, ay, bx, by = spans(*step, 8, wide, wide)
        push(at, f_in.at[fields, ax, :, ay, :], f_in.at[fields, bx, :, by, :], step)

    for copy in coarse_in:
        copy.wait()
    for sx, sy in faces_x:
        own = c_coef.at[:, 2:4, OWN_C, :]
        push(COEF_X, own, c_coef.at[:, 2 - 2 * sx : 4 - 2 * sx, OWN_C, :], (sx, sy))

    for step in faces_x:
        push_fine(FINE_X, slice(0, 1), step, 3)
        push_fine(FINE_X, slice(1, 5), step, 2)
    for step in corners:
        push_fine(FINE_X, slice(0, 2), step, 2)
        push_fine(FINE_X, slice(2, 5), step, 1)
    for step in faces_y:
        push_fine(FINE_Y, slice(0, 5), step, 3)

    for copy in mid_in:
        copy.wait()
    for step in NEIGHBOURS:
        wide = 3 if step in corners else 4
        ax, ay, bx, by = spans(*step, 4, wide, wide)
        push(MID_IN, m_in.at[:, ax, ay, :], m_in.at[:, bx, by, :], step)

    one = jnp.float32(1.0)
    nil = jnp.float32(0.0)
    keep_x = (jnp.where(gx == 0, nil, one), jnp.where(gx == count_x - 1, nil, one))

    def keep_yz(own, shape):
        row = lax.broadcasted_iota(jnp.int32, shape, len(shape) - 2)
        column = lax.broadcasted_iota(jnp.int32, shape, len(shape) - 1)
        if len(shape) == 3:
            column = column + 128 * lax.broadcasted_iota(jnp.int32, shape, 0)
        columns = 128 * (len(shape) - 1)
        end = jnp.where(gy == 0, O - 1, -1)
        other = jnp.where(gy == count_y - 1, O + own - 1, -1)
        keep_y = jnp.where((row == end) | (row == other), 0.0, 1.0)
        keep_z = jnp.where(column == columns - 1, 0.0, 1.0)
        return keep_y, keep_z

    half_f = one_hot((256, 128), lambda row, column: row // 2 == column)
    fold_c = one_hot((64, 128), lambda row, column: row // 8 + 8 * (row % 8) == column // 2)

    fine = (f_wx, f_wyu, f_wyd, f_wzu, f_wzd, f_diag, f_damp)
    keep_y, keep_z = keep_yz(8, (2, ROWS, 128))
    received(FINE_Y)
    weights_yz(fine, f_in, (O, O + 8), keep_y, keep_z)
    weights_x(fine, f_in, (O, O + 7))
    diagonals(fine, f_in, (O + 1, O + 7))
    start_sweep(fine, f_src, f_a, (O + 1, O + 7))
    received(COEF_X)
    for e in range(-REACH, REACH + 1):
        if e != 0:
            target = c_coef.at[:, 0:6, OWN_C.start - 2 * e : OWN_C.stop - 2 * e, :]
            push(COEF_Y, c_coef.at[:, 0:6, OWN_C, :], target, (0, e))
    received(FINE_X)
    for rows in ((O - 3, O), (O + 7, O + 10)):
        weights_x(fine, f_in, rows)
    f_wx[O - 1] = f_wx[O - 1] * keep_x[0]
    f_wx[O + 7] = f_wx[O + 7] * keep_x[1]
    for rows in ((O - 2, O), (O + 8, O + 10)):
        weights_yz(fine, f_in, rows, keep_y, keep_z)
    for rows in ((O - 2, O + 1), (O + 7, O + 10)):
        diagonals(fine, f_in, rows)
        start_sweep(fine, f_src, f_a, rows)
    sweep(fine, f_src, f_a, f_b, (O - 1, O + 9))

    def folded(x, _):
        first = row_residual(fine, f_src, f_b, O + 2 * x)
        f_spread[x] = first + row_residual(fine, f_src, f_b, O + 2 * x + 1)
        return 0

    lax.fori_loop(0, 4, folded, 0, unroll=True)
    halves = [f_spread[0:4, half].reshape(4 * ROWS, 128) for half in range(2)]
    m_fold[0:4] = times_one_hot(jnp.concatenate(halves, axis=1), half_f).reshape(4, ROWS, 128)

    def pairs(x, _):
        even = m_fold[x, pl.ds(O, 4, stride=2), :]
        m_src[O + x, O : O + 4, :] = even + m_fold[x, pl.ds(O + 1, 4, stride=2), :]
        return 0

    lax.fori_loop(0, 4, pairs, 0, unroll=True)

    for sx, sy in NEIGHBOURS:
        wide = 2 if sx != 0 and sy != 0 else 3
        ax, ay, bx, by = spans(sx, sy, 4, wide, wide)
        push(MID_F, m_src.at[ax, ay, :], m_src.at[bx, by, :], (sx, sy))

    def keep_fine(x, _):
        f_x[x, :, O : O + 8, :] = f_b[x, :, O : O + 8, :]
        return 0

    lax.fori_loop(O, O + 8, keep_fine, 0, unroll=True)
    for sx, sy in NEIGHBOURS:
        wide = 2 if sx != 0 and sy != 0 else 3
        ax, ay, bx, by = spans(sx, sy, 8, wide, wide)
        push(FINE_V, f_x.at[ax, :, ay, :], f_x.at[bx, :, by, :], (sx, sy))

    mid = (m_wx, m_wyu, m_wyd, m_wzu, m_wzd, m_diag, m_damp)
    keep_y, keep_z = keep_yz(4, (ROWS, 128))
    received(MID_IN)
    weights_x(mid, m_in, (O - 4, O + 7))
    m_wx[O - 1] = m_wx[O - 1] * keep_x[0]
    m_wx[O + 3] = m_wx[O + 3] * keep_x[1]
    weights_yz(mid, m_in, (O - 3, O + 7), keep_y, keep_z)
    diagonals(mid, m_in, (O - 3, O + 7))

    received(COEF_Y)
    coef = [c_coef[k, :, 8:24, :].reshape(128, 64).T for k in range(4)]
    second_prev = c_coef[2, :, 7:23, :].reshape(128, 64).T
    second_next = c_coef[2, :, 9:25, :].reshape(128, 64).T
    column = lax.broadcasted_iota(jnp.int32, (64, 128), 1)
    level_row = lax.broadcasted_iota(jnp.int32, (64, 128), 0)
    cells = 2 * count_y
    cell = 2 * gy + lax.rem(column, 16) + (cells - 7)
    block = 2 * GROUP
    offset = 4 + cells - (cells // block) * block
    shut_up = (lax.rem(cell + 1 - offset + 2 * block, block) == 0) | (lax.rem(cell + 1, cells) == 0)
    shut_down = (lax.rem(cell - offset + 2 * block, block) == 0) | (lax.rem(cell, cells) == 0)
    up_x = jnp.where(lax.rem(column, 32) < 16, harmonic(coef[1], pltpu.roll(coef[1], 112, 1)), 0.0)
    down_x = pltpu.roll(up_x, 16, 1)
    up_y = jnp.where(shut_up, 0.0, harmonic(coef[2], second_next))
    down_y = jnp.where(shut_down, 0.0, harmonic(second_prev, coef[2]))
    up_z = jnp.where(level_row == 63, 0.0, harmonic(coef[3], next_of(coef[3], 0)))
    down_z = prev_of(up_z, 0)
    main = coef[0] + (up_x + down_x) + (up_y + down_y) + (up_z + down_z)
    for at, band in enumerate((up_x, down_x, up_y, down_y, -down_z, main, -up_z)):
        c_bands[at] = band

    for at in (FINE_X, FINE_Y, COEF_X, COEF_Y, MID_IN):
        sent(at)

    received(MID_F)
    start_sweep(mid, m_src, m_a, (O - 2, O + 6))
    sweep(mid, m_src, m_a, m_b, (O - 1, O + 5))
    for ix in range(2):
        fold = row_residual(mid, m_src, m_b, O + 2 * ix) + row_residual(mid, m_src, m_b, O + 2 * ix + 1)
        for iy in range(2):
            first = O + 2 * iy
            at = OWN_C.start + iy
            c_src[2 + ix, at : at + 1, :] = fold[first : first + 1] + fold[first + 1 : first + 2]
    for e in sorted(range(-REACH, REACH + 1), key=lambda e: -abs(e)):
        for g in (1, -1, 0):
            if (g, e) != (0, 0):
                target = c_src.at[2 - 2 * g : 4 - 2 * g, OWN_C.start - 2 * e : OWN_C.stop - 2 * e, :]
                push(COARSE_F, c_src.at[2:4, OWN_C, :], target, (g, e))

    def keep_mid(x, _):
        m_y[x, O : O + 4, :] = m_b[x, O : O + 4, :]
        return 0

    lax.fori_loop(O, O + 4, keep_mid, 0, unroll=True)
    for sx, sy in NEIGHBOURS:
        wide = 3 if sx != 0 and sy != 0 else 4
        ax, ay, bx, by = spans(sx, sy, 4, wide, wide)
        push(MID_V, m_y.at[ax, ay, :], m_y.at[bx, by, :], (sx, sy))

    def registers(at):
        return [c_bands[at, pl.ds(place, 8, stride=8), :] for place in range(8)]

    for at in range(4):
        for place, values in enumerate(registers(at)):
            c_weights[at, place] = values
    low, main, high = (registers(at) for at in (4, 5, 6))
    ahead, back = [reciprocal(main[0])], {6: reciprocal(main[6])}
    upto, onfrom = [main[0]], {6: main[6]}
    for i in range(1, 7):
        upto.append(main[i] - low[i] * high[i - 1] * ahead[i - 1])
        ahead.append(reciprocal(upto[i]))
        j = 6 - i
        onfrom[j] = main[j] - high[j] * low[j + 1] * back[j + 1]
        back[j] = reciprocal(onfrom[j])
    rise = [-high[i] * ahead[i] for i in range(7)]
    fall = [-low[i] * back[i] for i in range(7)]
    inverse = {}
    for j in range(7):
        inverse[j, j] = reciprocal(upto[j] + onfrom[j] - main[j])
        for i in range(j - 1, -1, -1):
            inverse[i, j] = rise[i] * inverse[i + 1, j]
        for i in range(j + 1, 7):
            inverse[i, j] = fall[i] * inverse[i - 1, j]
    from_last = [inverse[i, 0] * low[0] for i in range(7)]
    from_own = [inverse[i, 6] * high[6] for i in range(7)]

    def turned(values, by):
        return pltpu.roll(values, by % 8, 0) if by % 8 else values

    face_main = main[7] - low[7] * from_own[6] - high[7] * turned(from_last[0], -1)
    face_low = -low[7] * from_last[6]
    face_high = -high[7] * turned(from_own[0], -1)
    spread_by = {0: jnp.ones((8, 128), jnp.float32)}
    for far in (1, 2, 4):
        over = reciprocal(face_main)
        alpha = -face_low * turned(over, far)
        gamma = -face_high * turned(over, -far)
        face_main = face_main + alpha * turned(face_high, far) + gamma * turned(face_low, -far)
        face_low, face_high = alpha * turned(face_low, far), gamma * turned(face_high, -far)
        wider = dict(spread_by)
        for by, values in spread_by.items():
            for step, factor in ((far, alpha), (-far, gamma)):
                term = factor * turned(values, step)
                key = (by + step) % 8
                wider[key] = wider[key] + term if key in wider else term
        spread_by = wider
    over = reciprocal(face_main)
    own_by = [over * spread_by[by] for by in range(8)]
    next_by = [own_by[(by + 1) % 8] * turned(high[7], by + 1) for by in range(8)]
    for i in range(7):
        for j in range(7):
            c_inverse[7 * i + j] = inverse[i, j]
        c_inverse[49 + i] = from_last[i]
        c_inverse[56 + i] = from_own[i]
    for by in range(8):
        c_inverse[64 + by] = own_by[by]
        c_inverse[72 + by] = next_by[by]
        c_inverse[80 + by] = turned(own_by[by - 1], 1)
        c_inverse[88 + by] = turned(next_by[by - 1], 1)
    c_inverse[63] = low[7]

    def lines(values):
        inner = [total([c_inverse[7 * i + j] * values[j] for j in range(7)]) for i in range(7)]
        face = values[7] - c_inverse[63] * inner[6]
        faces = [turned(face, by) for by in range(8)]
        firsts = [turned(inner[0], by) for by in range(8)]

        def interface(at):
            terms = [c_inverse[at + by] * faces[by] for by in range(8)]
            return total(terms) - total([c_inverse[at + 8 + by] * firsts[by] for by in range(8)])

        here, before = interface(64), interface(80)
        return tuple(inner[i] - (c_inverse[49 + i] * before + c_inverse[56 + i] * here) for i in range(7)) + (here,)

    for at in (MID_F, FINE_V):
        sent(at)

    received(COARSE_F)
    source = lax.dot_general(
        jnp.concatenate([fold_c] * 2, axis=1),
        jnp.concatenate(pieces(c_src[:, 8:24, :].reshape(128, 128)), axis=1),
        (((1,), (1,)), ((), ())),
        preferred_element_type=jnp.float32,
    )
    sources = [source[8 * place : 8 * place + 8] for place in range(8)]

    def turn(_, z):
        pushed = []
        for place in range(8):
            own = z[place]
            along_x = c_weights[0, place] * pltpu.roll(own, 112, 1) + c_weights[1, place] * pltpu.roll(own, 16, 1)
            along_y = c_weights[2, place] * next_of(own, 1) + c_weights[3, place] * prev_of(own, 1)
            pushed.append(sources[place] + (along_x + along_y))
        return lines(pushed)

    z = lax.fori_loop(0, KC - 1, turn, lines(sources))
    c_ext[...] = times_one_hot(jnp.concatenate(z, axis=0).T[0:96], fold_c).reshape(6, 16, 128)

    received(MID_V)

    def raise_mid(x, _):
        rows = c_ext[x, 5:13, :]
        c_spread[x, pl.ds(0, 8, stride=2), :] = rows
        c_spread[x, pl.ds(1, 8, stride=2), :] = rows
        doubled = c_spread[x]
        m_a[2 * x] = m_y[2 * x] + doubled
        m_a[2 * x + 1] = m_y[2 * x + 1] + doubled
        return 0

    lax.fori_loop(0, 6, raise_mid, 0, unroll=True)
    sweep(mid, m_src, m_a, m_b, (O - 3, O + 7))
    sweep(mid, m_src, m_b, m_a, (O - 2, O + 6))

    def raise_rows(x, _):
        rows = m_a[O - 2 + x, O - 2 : O + 6, :]
        m_fold[x, pl.ds(0, 8, stride=2), :] = rows
        m_fold[x, pl.ds(1, 8, stride=2), :] = rows
        return 0

    lax.fori_loop(0, 8, raise_rows, 0, unroll=True)
    double_f = one_hot((128, 256), lambda row, column: row == column // 2)
    doubled_z = times_one_hot(m_fold[...].reshape(8 * ROWS, 128), double_f)
    for half in range(2):
        f_spread[:, half] = doubled_z[:, 128 * half : 128 * half + 128].reshape(8, ROWS, 128)
    received(FINE_V)

    def raise_fine(x, _):
        f_a[2 * x] = f_x[2 * x] + f_spread[x]
        f_a[2 * x + 1] = f_x[2 * x + 1] + f_spread[x]
        return 0

    lax.fori_loop(0, 8, raise_fine, 0, unroll=True)
    sweep(fine, f_src, f_a, f_b, (O - 2, O + 10))
    sweep(fine, f_src, f_b, f_a, (O - 1, O + 9))

    def last(x, _):
        left = row_residual(fine, f_src, f_a, x)
        own = f_a[x]
        for half in range(2):
            columns = slice(128 * half, 128 * half + 128)
            pressure[x - O, :, columns] = own[half, O : O + 8]
            residual[x - O, :, columns] = left[half, O : O + 8]
        return 0

    lax.fori_loop(O, O + 8, last, 0, unroll=True)
    for at in (COARSE_F, MID_V):
        sent(at)


def publish(pressure, residual, pressure_h, residual_h, sem):
    copies = [
        pltpu.make_async_copy(pressure, pressure_h, sem.at[0]),
        pltpu.make_async_copy(residual, residual_h, sem.at[1]),
    ]
    for copy in copies:
        copy.start()
    for copy in copies:
        copy.wait()


def local(pressure_rhs, storage_fine, mobility_fine, storage_mid, mobility_mid, storage_coarse, mobility_coarse):
    count_x = lax.axis_size("gx")
    count_y = lax.axis_size("gy")
    f32 = jnp.float32
    fine = pltpu.VMEM((8 + 2 * O, 2, ROWS, 128), f32)
    mid = pltpu.VMEM((4 + 2 * O, ROWS, 128), f32)
    in_hbm = pl.BlockSpec(memory_space=pltpu.HBM)
    in_vmem = pl.BlockSpec(memory_space=pltpu.VMEM)
    arrays = (pressure_rhs, storage_fine, mobility_fine, storage_mid, mobility_mid, storage_coarse, mobility_coarse)
    result = pl.pallas_call(
        functools.partial(kernel, count_x, count_y),
        out_shape=(pltpu.VMEM(pressure_rhs.shape, f32),) * 2,
        in_specs=[in_hbm] * 7,
        out_specs=(in_vmem, in_vmem),
        scratch_shapes=[
            pltpu.VMEM((5, 8 + 2 * O, 2, ROWS, 128), f32),
            *[fine] * 10,
            pltpu.VMEM((4, 4 + 2 * O, ROWS, 128), f32),
            *[mid] * 11,
            pltpu.VMEM((8, ROWS, 128), f32),
            pltpu.VMEM((8, 2, ROWS, 128), f32),
            pltpu.VMEM((4, 8, 32, 64), f32),
            pltpu.VMEM((8, 32, 128), f32),
            pltpu.VMEM((6, 16, 128), f32),
            pltpu.VMEM((6, ROWS, 128), f32),
            pltpu.VMEM((4, 8, 8, 128), f32),
            pltpu.VMEM((7, 64, 128), f32),
            pltpu.VMEM((97, 8, 128), f32),
            pltpu.VMEM((1024, 128), f32),
            pltpu.SemaphoreType.DMA((16,)),
            pltpu.SemaphoreType.DMA((EXCHANGES,)),
            pltpu.SemaphoreType.DMA((EXCHANGES,)),
        ],
        compiler_params=pltpu.CompilerParams(
            collective_id=0, has_side_effects=True, vmem_limit_bytes=32 * 1024 * 1024
        ),
    )(*[pltpu.with_memory_space_constraint(array, pltpu.HBM) for array in arrays])
    out = jax.ShapeDtypeStruct(pressure_rhs.shape, f32)
    return pl.pallas_call(
        publish,
        out_shape=(out, out),
        in_specs=[in_vmem] * 2,
        out_specs=(in_hbm, in_hbm),
        scratch_shapes=[pltpu.SemaphoreType.DMA((2,))],
        compiler_params=pltpu.CompilerParams(vmem_limit_bytes=16 * 1024 * 1024),
    )(*result)


def solution(mesh):
    placed = (
        P("gx", "gy", None),
        P("gx", "gy", None),
        P(None, "gx", "gy", None),
        P("gx", "gy", None),
        P(None, "gx", "gy", None),
        P("gx", "gy", None),
        P(None, "gx", "gy", None),
    )
    return jax.shard_map(
        local,
        mesh=mesh,
        in_specs=placed,
        out_specs=(P("gx", "gy", None), P("gx", "gy", None)),
        check_vma=False,
    )
```

```python
import functools

import jax
import jax.numpy as jnp
from jax import lax
from jax.experimental import pallas as pl
from jax.experimental.pallas import tpu as pltpu
from jax.sharding import PartitionSpec as P

KC = 6
GROUP = 8
REACH = 4
DAMPING = 2.0 / 3.0

MESH = pl.DeviceIdType.MESH

O = 4
ROWS = 16
OWN_C = slice(15, 17)
FINE_X, FINE_Y, COEF_X, COEF_Y, MID_IN, MID_F, FINE_V, COARSE_F, MID_V = range(9)
EXCHANGES = 9
NEIGHBOURS = ((1, 0), (-1, 0), (1, 1), (1, -1), (-1, 1), (-1, -1), (0, 1), (0, -1))


def reciprocal(values):
    guess = pl.reciprocal(values, approx=True)
    return guess * (2.0 - values * guess)


def harmonic(left, right):
    return 2.0 * left * right * reciprocal(left + right)


def next_of(values, axis):
    return pltpu.roll(values, values.shape[axis] - 1, axis)


def prev_of(values, axis):
    return pltpu.roll(values, 1, axis)


def swapped(values):
    return jnp.concatenate([values[1:2], values[0:1]], axis=0)


def next_z(values):
    moved = next_of(values, values.ndim - 1)
    if values.ndim == 2:
        return moved
    lane = lax.broadcasted_iota(jnp.int32, values.shape, 2)
    return jnp.where(lane == 127, swapped(moved), moved)


def prev_z(values):
    moved = prev_of(values, values.ndim - 1)
    if values.ndim == 2:
        return moved
    lane = lax.broadcasted_iota(jnp.int32, values.shape, 2)
    return jnp.where(lane == 0, swapped(moved), moved)


def next_y(values):
    return next_of(values, values.ndim - 2)


def prev_y(values):
    return prev_of(values, values.ndim - 2)


def one_hot(shape, test):
    row = lax.broadcasted_iota(jnp.int32, shape, 0)
    column = lax.broadcasted_iota(jnp.int32, shape, 1)
    return jnp.where(test(row, column), 1.0, 0.0).astype(jnp.bfloat16)


def pieces(values):
    head = values.astype(jnp.bfloat16)
    return [head, (values - head.astype(jnp.float32)).astype(jnp.bfloat16)]


def times_one_hot(values, matrix):
    rows = values.shape[0]
    product = jnp.dot(jnp.concatenate(pieces(values), axis=0), matrix, preferred_element_type=jnp.float32)
    return product[:rows] + product[rows:]


def total(terms):
    while len(terms) > 1:
        pairs = [terms[i] + terms[i + 1] for i in range(0, len(terms) - 1, 2)]
        terms = pairs + terms[len(terms) - len(terms) % 2 :]
    return terms[0]


def source_span(step, n, width):
    return (n - width, n) if step > 0 else (0, width) if step < 0 else (0, n)


def target_span(step, n, width):
    return (O - width, O) if step > 0 else (O + n, O + n + width) if step < 0 else (O, O + n)


def weights_x(level, field, rows):
    wx = level[0]

    def body(x, _):
        wx[x] = harmonic(field[0, x], field[0, x + 1])
        return 0

    lax.fori_loop(*rows, body, 0)


def weights_yz(level, field, rows, keep_y, keep_z):
    wx, wyu, wyd, wzu, wzd, diag, damp = level

    def body(x, _):
        second = field[1, x]
        third = field[2, x]
        up_y = harmonic(second, next_y(second)) * keep_y
        up_z = harmonic(third, next_z(third)) * keep_z
        wyu[x] = up_y
        wyd[x] = prev_y(up_y)
        wzu[x] = up_z
        wzd[x] = prev_z(up_z)
        return 0

    lax.fori_loop(*rows, body, 0)


def diagonals(level, field, rows):
    wx, wyu, wyd, wzu, wzd, diag, damp = level

    def body(x, _):
        total = field[3, x] + (wx[x] + wx[x - 1]) + (wyu[x] + wyd[x]) + (wzu[x] + wzd[x])
        diag[x] = total
        damp[x] = DAMPING * reciprocal(total)
        return 0

    lax.fori_loop(*rows, body, 0)


def row_residual(level, source, field, x):
    wx, wyu, wyd, wzu, wzd, diag, damp = level
    v = field[x]
    left = source[x] - diag[x] * v
    left = left + (wx[x] * field[x + 1] + wx[x - 1] * field[x - 1])
    left = left + (wyu[x] * next_y(v) + wyd[x] * prev_y(v))
    left = left + (wzu[x] * next_z(v) + wzd[x] * prev_z(v))
    return left


def sweep(level, source, field, result, rows):
    damp = level[6]

    def body(x, _):
        result[x] = field[x] + damp[x] * row_residual(level, source, field, x)
        return 0

    lax.fori_loop(rows[0], rows[1], body, 0)


def start_sweep(level, source, result, rows):
    damp = level[6]

    def body(x, _):
        result[x] = damp[x] * source[x]
        return 0

    lax.fori_loop(rows[0], rows[1], body, 0)


def kernel(
    count_x,
    count_y,
    rhs_h,
    store_f_h,
    mob_f_h,
    store_m_h,
    mob_m_h,
    store_c_h,
    mob_c_h,
    pressure,
    residual,
    f_in,
    f_wx,
    f_wyu,
    f_wyd,
    f_wzu,
    f_wzd,
    f_diag,
    f_damp,
    f_a,
    f_b,
    f_x,
    m_in,
    m_src,
    m_wx,
    m_wyu,
    m_wyd,
    m_wzu,
    m_wzd,
    m_diag,
    m_damp,
    m_a,
    m_b,
    m_y,
    m_fold,
    f_spread,
    c_coef,
    c_src,
    c_ext,
    c_spread,
    c_weights,
    c_bands,
    c_inverse,
    meter,
    local_sem,
    send_sem,
    recv_sem,
):
    gx = lax.axis_index("gx")
    gy = lax.axis_index("gy")

    def stepped(at, step, count):
        to = at + step
        if step > 0:
            return jnp.where(to >= count, to - count, to)
        return jnp.where(to < 0, to + count, to) if step < 0 else at

    along_gx = {step: stepped(gx, step, count_x) for step in (-1, 0, 1)}
    along_gy = {step: stepped(gy, step, count_y) for step in range(-REACH, REACH + 1)}

    def beside(sx, sy):
        return {"gx": along_gx[sx], "gy": along_gy[sy]}

    partners = NEIGHBOURS + tuple((0, e) for e in range(-REACH, REACH + 1) if abs(e) > 1)
    barrier = pltpu.get_barrier_semaphore()
    for step in partners:
        pl.semaphore_signal(barrier, inc=1, device_id=beside(*step), device_id_type=MESH)

    c_coef[:, 6:8] = jnp.ones((4, 2, 32, 64), jnp.float32)
    c_src[6:8] = jnp.zeros((2, 32, 128), jnp.float32)

    locals_ = []

    def bring(source, target):
        copy = pltpu.make_async_copy(source, target, local_sem.at[len(locals_)])
        copy.start()
        locals_.append(copy)
        return copy

    def push(at, source, target, step):
        pltpu.make_async_remote_copy(
            src_ref=source,
            dst_ref=target,
            send_sem=send_sem.at[at],
            recv_sem=recv_sem.at[at],
            device_id=beside(*step),
            device_id_type=MESH,
        ).start()
        rows = 1
        for size in source.shape[:-1]:
            rows = rows * size
        rows_of[at] = rows_of.get(at, 0) + rows

    rows_of = {}

    def all_of(at):
        if at == COEF_X:
            return c_coef.at[:, 0:4, 0:2, :]
        if at == COEF_Y:
            return c_coef.at[:, 0:6, 0:16, :]
        return meter.at[0 : rows_of[at], :]

    def received(at):
        pltpu.make_async_copy(all_of(at), all_of(at), recv_sem.at[at]).wait()

    def sent(at):
        pltpu.make_async_copy(all_of(at), all_of(at), send_sem.at[at]).wait()

    own8 = slice(O, O + 8)
    own4 = slice(O, O + 4)
    fine_in = []
    for half in range(2):
        z = slice(128 * half, 128 * half + 128)
        fine_in.append(bring(mob_f_h.at[:, :, :, z], f_in.at[0:3, own8, half, own8, :]))
        fine_in.append(bring(store_f_h.at[:, :, z], f_in.at[3, own8, half, own8, :]))
        fine_in.append(bring(rhs_h.at[:, :, z], f_in.at[4, own8, half, own8, :]))
    coarse_in = [
        bring(store_c_h, c_coef.at[0, 2:4, OWN_C, :]),
        bring(mob_c_h, c_coef.at[1:4, 2:4, OWN_C, :]),
    ]
    mid_in = [
        bring(mob_m_h, m_in.at[0:3, own4, own4, :]),
        bring(store_m_h, m_in.at[3, own4, own4, :]),
    ]
    f_src = f_in.at[4]

    def spans(sx, sy, n, wide_x, wide_y):
        ax, ay = source_span(sx, n, wide_x), source_span(sy, n, wide_y)
        return (
            slice(ax[0] + O, ax[1] + O),
            slice(ay[0] + O, ay[1] + O),
            slice(*target_span(sx, n, wide_x)),
            slice(*target_span(sy, n, wide_y)),
        )

    faces_x = [step for step in NEIGHBOURS if step[1] == 0]
    faces_y = [step for step in NEIGHBOURS if step[0] == 0]
    corners = [step for step in NEIGHBOURS if step[0] != 0 and step[1] != 0]

    for copy in fine_in:
        copy.wait()
    pl.semaphore_wait(barrier, len(partners))

    def push_fine(at, fields, step, wide):
        ax, ay, bx, by = spans(*step, 8, wide, wide)
        push(at, f_in.at[fields, ax, :, ay, :], f_in.at[fields, bx, :, by, :], step)

    for copy in coarse_in:
        copy.wait()
    for sx, sy in faces_x:
        own = c_coef.at[:, 2:4, OWN_C, :]
        push(COEF_X, own, c_coef.at[:, 2 - 2 * sx : 4 - 2 * sx, OWN_C, :], (sx, sy))

    for step in faces_x:
        push_fine(FINE_X, slice(0, 1), step, 3)
        push_fine(FINE_X, slice(1, 5), step, 2)
    for step in corners:
        push_fine(FINE_X, slice(0, 2), step, 2)
        push_fine(FINE_X, slice(2, 5), step, 1)
    for step in faces_y:
        push_fine(FINE_Y, slice(0, 5), step, 3)

    for copy in mid_in:
        copy.wait()
    for step in NEIGHBOURS:
        wide = 3 if step in corners else 4
        ax, ay, bx, by = spans(*step, 4, wide, wide)
        push(MID_IN, m_in.at[:, ax, ay, :], m_in.at[:, bx, by, :], step)

    one = jnp.float32(1.0)
    nil = jnp.float32(0.0)
    keep_x = (jnp.where(gx == 0, nil, one), jnp.where(gx == count_x - 1, nil, one))

    def keep_yz(own, shape):
        row = lax.broadcasted_iota(jnp.int32, shape, len(shape) - 2)
        column = lax.broadcasted_iota(jnp.int32, shape, len(shape) - 1)
        if len(shape) == 3:
            column = column + 128 * lax.broadcasted_iota(jnp.int32, shape, 0)
        columns = 128 * (len(shape) - 1)
        end = jnp.where(gy == 0, O - 1, -1)
        other = jnp.where(gy == count_y - 1, O + own - 1, -1)
        keep_y = jnp.where((row == end) | (row == other), 0.0, 1.0)
        keep_z = jnp.where(column == columns - 1, 0.0, 1.0)
        return keep_y, keep_z

    half_f = one_hot((256, 128), lambda row, column: row // 2 == column)
    fold_c = one_hot((64, 128), lambda row, column: row // 8 + 8 * (row % 8) == column // 2)

    fine = (f_wx, f_wyu, f_wyd, f_wzu, f_wzd, f_diag, f_damp)
    keep_y, keep_z = keep_yz(8, (2, ROWS, 128))
    received(FINE_Y)
    weights_yz(fine, f_in, (O, O + 8), keep_y, keep_z)
    weights_x(fine, f_in, (O, O + 7))
    diagonals(fine, f_in, (O + 1, O + 7))
    start_sweep(fine, f_src, f_a, (O + 1, O + 7))
    received(COEF_X)
    for e in range(-REACH, REACH + 1):
        if e != 0:
            target = c_coef.at[:, 0:6, OWN_C.start - 2 * e : OWN_C.stop - 2 * e, :]
            push(COEF_Y, c_coef.at[:, 0:6, OWN_C, :], target, (0, e))
    received(FINE_X)
    for rows in ((O - 3, O), (O + 7, O + 10)):
        weights_x(fine, f_in, rows)
    f_wx[O - 1] = f_wx[O - 1] * keep_x[0]
    f_wx[O + 7] = f_wx[O + 7] * keep_x[1]
    for rows in ((O - 2, O), (O + 8, O + 10)):
        weights_yz(fine, f_in, rows, keep_y, keep_z)
    for rows in ((O - 2, O + 1), (O + 7, O + 10)):
        diagonals(fine, f_in, rows)
        start_sweep(fine, f_src, f_a, rows)
    sweep(fine, f_src, f_a, f_b, (O - 1, O + 9))

    def folded(x, _):
        first = row_residual(fine, f_src, f_b, O + 2 * x)
        f_spread[x] = first + row_residual(fine, f_src, f_b, O + 2 * x + 1)
        return 0

    lax.fori_loop(0, 4, folded, 0)
    halves = [f_spread[0:4, half].reshape(4 * ROWS, 128) for half in range(2)]
    m_fold[0:4] = times_one_hot(jnp.concatenate(halves, axis=1), half_f).reshape(4, ROWS, 128)

    def pairs(x, _):
        even = m_fold[x, pl.ds(O, 4, stride=2), :]
        m_src[O + x, O : O + 4, :] = even + m_fold[x, pl.ds(O + 1, 4, stride=2), :]
        return 0

    lax.fori_loop(0, 4, pairs, 0)

    for sx, sy in NEIGHBOURS:
        wide = 2 if sx != 0 and sy != 0 else 3
        ax, ay, bx, by = spans(sx, sy, 4, wide, wide)
        push(MID_F, m_src.at[ax, ay, :], m_src.at[bx, by, :], (sx, sy))

    def keep_fine(x, _):
        f_x[x, :, O : O + 8, :] = f_b[x, :, O : O + 8, :]
        return 0

    lax.fori_loop(O, O + 8, keep_fine, 0)
    for sx, sy in NEIGHBOURS:
        wide = 2 if sx != 0 and sy != 0 else 3
        ax, ay, bx, by = spans(sx, sy, 8, wide, wide)
        push(FINE_V, f_x.at[ax, :, ay, :], f_x.at[bx, :, by, :], (sx, sy))

    mid = (m_wx, m_wyu, m_wyd, m_wzu, m_wzd, m_diag, m_damp)
    keep_y, keep_z = keep_yz(4, (ROWS, 128))
    received(MID_IN)
    weights_x(mid, m_in, (O - 4, O + 7))
    m_wx[O - 1] = m_wx[O - 1] * keep_x[0]
    m_wx[O + 3] = m_wx[O + 3] * keep_x[1]
    weights_yz(mid, m_in, (O - 3, O + 7), keep_y, keep_z)
    diagonals(mid, m_in, (O - 3, O + 7))

    received(COEF_Y)
    coef = [c_coef[k, :, 8:24, :].reshape(128, 64).T for k in range(4)]
    second_prev = c_coef[2, :, 7:23, :].reshape(128, 64).T
    second_next = c_coef[2, :, 9:25, :].reshape(128, 64).T
    column = lax.broadcasted_iota(jnp.int32, (64, 128), 1)
    level_row = lax.broadcasted_iota(jnp.int32, (64, 128), 0)
    cells = 2 * count_y
    cell = 2 * gy + lax.rem(column, 16) + (cells - 7)
    block = 2 * GROUP
    offset = 4 + cells - (cells // block) * block
    shut_up = (lax.rem(cell + 1 - offset + 2 * block, block) == 0) | (lax.rem(cell + 1, cells) == 0)
    shut_down = (lax.rem(cell - offset + 2 * block, block) == 0) | (lax.rem(cell, cells) == 0)
    up_x = jnp.where(lax.rem(column, 32) < 16, harmonic(coef[1], pltpu.roll(coef[1], 112, 1)), 0.0)
    down_x = pltpu.roll(up_x, 16, 1)
    up_y = jnp.where(shut_up, 0.0, harmonic(coef[2], second_next))
    down_y = jnp.where(shut_down, 0.0, harmonic(second_prev, coef[2]))
    up_z = jnp.where(level_row == 63, 0.0, harmonic(coef[3], next_of(coef[3], 0)))
    down_z = prev_of(up_z, 0)
    main = coef[0] + (up_x + down_x) + (up_y + down_y) + (up_z + down_z)
    for at, band in enumerate((up_x, down_x, up_y, down_y, -down_z, main, -up_z)):
        c_bands[at] = band

    for at in (FINE_X, FINE_Y, COEF_X, COEF_Y, MID_IN):
        sent(at)

    received(MID_F)
    start_sweep(mid, m_src, m_a, (O - 2, O + 6))
    sweep(mid, m_src, m_a, m_b, (O - 1, O + 5))
    for ix in range(2):
        fold = row_residual(mid, m_src, m_b, O + 2 * ix) + row_residual(mid, m_src, m_b, O + 2 * ix + 1)
        for iy in range(2):
            first = O + 2 * iy
            at = OWN_C.start + iy
            c_src[2 + ix, at : at + 1, :] = fold[first : first + 1] + fold[first + 1 : first + 2]
    for e in sorted(range(-REACH, REACH + 1), key=lambda e: -abs(e)):
        for g in (1, -1, 0):
            if (g, e) != (0, 0):
                target = c_src.at[2 - 2 * g : 4 - 2 * g, OWN_C.start - 2 * e : OWN_C.stop - 2 * e, :]
                push(COARSE_F, c_src.at[2:4, OWN_C, :], target, (g, e))

    def keep_mid(x, _):
        m_y[x, O : O + 4, :] = m_b[x, O : O + 4, :]
        return 0

    lax.fori_loop(O, O + 4, keep_mid, 0)
    for sx, sy in NEIGHBOURS:
        wide = 3 if sx != 0 and sy != 0 else 4
        ax, ay, bx, by = spans(sx, sy, 4, wide, wide)
        push(MID_V, m_y.at[ax, ay, :], m_y.at[bx, by, :], (sx, sy))

    def registers(at):
        return [c_bands[at, pl.ds(place, 8, stride=8), :] for place in range(8)]

    for at in range(4):
        for place, values in enumerate(registers(at)):
            c_weights[at, place] = values
    low, main, high = (registers(at) for at in (4, 5, 6))
    ahead, back = [reciprocal(main[0])], {6: reciprocal(main[6])}
    upto, onfrom = [main[0]], {6: main[6]}
    for i in range(1, 7):
        upto.append(main[i] - low[i] * high[i - 1] * ahead[i - 1])
        ahead.append(reciprocal(upto[i]))
        j = 6 - i
        onfrom[j] = main[j] - high[j] * low[j + 1] * back[j + 1]
        back[j] = reciprocal(onfrom[j])
    rise = [-high[i] * ahead[i] for i in range(7)]
    fall = [-low[i] * back[i] for i in range(7)]
    inverse = {}
    for j in range(7):
        inverse[j, j] = reciprocal(upto[j] + onfrom[j] - main[j])
        for i in range(j - 1, -1, -1):
            inverse[i, j] = rise[i] * inverse[i + 1, j]
        for i in range(j + 1, 7):
            inverse[i, j] = fall[i] * inverse[i - 1, j]
    from_last = [inverse[i, 0] * low[0] for i in range(7)]
    from_own = [inverse[i, 6] * high[6] for i in range(7)]

    def turned(values, by):
        return pltpu.roll(values, by % 8, 0) if by % 8 else values

    face_main = main[7] - low[7] * from_own[6] - high[7] * turned(from_last[0], -1)
    face_low = -low[7] * from_last[6]
    face_high = -high[7] * turned(from_own[0], -1)
    spread_by = {0: jnp.ones((8, 128), jnp.float32)}
    for far in (1, 2, 4):
        over = reciprocal(face_main)
        alpha = -face_low * turned(over, far)
        gamma = -face_high * turned(over, -far)
        face_main = face_main + alpha * turned(face_high, far) + gamma * turned(face_low, -far)
        face_low, face_high = alpha * turned(face_low, far), gamma * turned(face_high, -far)
        wider = dict(spread_by)
        for by, values in spread_by.items():
            for step, factor in ((far, alpha), (-far, gamma)):
                term = factor * turned(values, step)
                key = (by + step) % 8
                wider[key] = wider[key] + term if key in wider else term
        spread_by = wider
    over = reciprocal(face_main)
    own_by = [over * spread_by[by] for by in range(8)]
    next_by = [own_by[(by + 1) % 8] * turned(high[7], by + 1) for by in range(8)]
    for i in range(7):
        for j in range(7):
            c_inverse[7 * i + j] = inverse[i, j]
        c_inverse[49 + i] = from_last[i]
        c_inverse[56 + i] = from_own[i]
    for by in range(8):
        c_inverse[64 + by] = own_by[by]
        c_inverse[72 + by] = next_by[by]
        c_inverse[80 + by] = turned(own_by[by - 1], 1)
        c_inverse[88 + by] = turned(next_by[by - 1], 1)
    c_inverse[63] = low[7]

    def lines(values):
        inner = [total([c_inverse[7 * i + j] * values[j] for j in range(7)]) for i in range(7)]
        face = values[7] - c_inverse[63] * inner[6]
        faces = [turned(face, by) for by in range(8)]
        firsts = [turned(inner[0], by) for by in range(8)]

        def interface(at):
            terms = [c_inverse[at + by] * faces[by] for by in range(8)]
            return total(terms) - total([c_inverse[at + 8 + by] * firsts[by] for by in range(8)])

        here, before = interface(64), interface(80)
        return tuple(inner[i] - (c_inverse[49 + i] * before + c_inverse[56 + i] * here) for i in range(7)) + (here,)

    for at in (MID_F, FINE_V):
        sent(at)

    received(COARSE_F)
    source = lax.dot_general(
        jnp.concatenate([fold_c] * 2, axis=1),
        jnp.concatenate(pieces(c_src[:, 8:24, :].reshape(128, 128)), axis=1),
        (((1,), (1,)), ((), ())),
        preferred_element_type=jnp.float32,
    )
    sources = [source[8 * place : 8 * place + 8] for place in range(8)]

    def turn(_, z):
        pushed = []
        for place in range(8):
            own = z[place]
            along_x = c_weights[0, place] * pltpu.roll(own, 112, 1) + c_weights[1, place] * pltpu.roll(own, 16, 1)
            along_y = c_weights[2, place] * next_of(own, 1) + c_weights[3, place] * prev_of(own, 1)
            pushed.append(sources[place] + (along_x + along_y))
        return lines(pushed)

    z = lax.fori_loop(0, KC, turn, tuple(jnp.zeros((8, 128), jnp.float32) for _ in range(8)))
    c_ext[...] = times_one_hot(jnp.concatenate(z, axis=0).T[0:96], fold_c).reshape(6, 16, 128)

    received(MID_V)

    def raise_mid(x, _):
        rows = c_ext[x, 5:13, :]
        c_spread[x, pl.ds(0, 8, stride=2), :] = rows
        c_spread[x, pl.ds(1, 8, stride=2), :] = rows
        doubled = c_spread[x]
        m_a[2 * x] = m_y[2 * x] + doubled
        m_a[2 * x + 1] = m_y[2 * x + 1] + doubled
        return 0

    lax.fori_loop(0, 6, raise_mid, 0)
    sweep(mid, m_src, m_a, m_b, (O - 3, O + 7))
    sweep(mid, m_src, m_b, m_a, (O - 2, O + 6))

    def raise_rows(x, _):
        rows = m_a[O - 2 + x, O - 2 : O + 6, :]
        m_fold[x, pl.ds(0, 8, stride=2), :] = rows
        m_fold[x, pl.ds(1, 8, stride=2), :] = rows
        return 0

    lax.fori_loop(0, 8, raise_rows, 0)
    double_f = one_hot((128, 256), lambda row, column: row == column // 2)
    doubled_z = times_one_hot(m_fold[...].reshape(8 * ROWS, 128), double_f)
    for half in range(2):
        f_spread[:, half] = doubled_z[:, 128 * half : 128 * half + 128].reshape(8, ROWS, 128)
    received(FINE_V)

    def raise_fine(x, _):
        f_a[2 * x] = f_x[2 * x] + f_spread[x]
        f_a[2 * x + 1] = f_x[2 * x + 1] + f_spread[x]
        return 0

    lax.fori_loop(0, 8, raise_fine, 0)
    sweep(fine, f_src, f_a, f_b, (O - 2, O + 10))
    sweep(fine, f_src, f_b, f_a, (O - 1, O + 9))

    def last(x, _):
        left = row_residual(fine, f_src, f_a, x)
        own = f_a[x]
        for half in range(2):
            columns = slice(128 * half, 128 * half + 128)
            pressure[x - O, :, columns] = own[half, O : O + 8]
            residual[x - O, :, columns] = left[half, O : O + 8]
        return 0

    lax.fori_loop(O, O + 8, last, 0)
    for at in (COARSE_F, MID_V):
        sent(at)


def publish(pressure, residual, pressure_h, residual_h, sem):
    copies = [
        pltpu.make_async_copy(pressure, pressure_h, sem.at[0]),
        pltpu.make_async_copy(residual, residual_h, sem.at[1]),
    ]
    for copy in copies:
        copy.start()
    for copy in copies:
        copy.wait()


def local(pressure_rhs, storage_fine, mobility_fine, storage_mid, mobility_mid, storage_coarse, mobility_coarse):
    count_x = lax.axis_size("gx")
    count_y = lax.axis_size("gy")
    f32 = jnp.float32
    fine = pltpu.VMEM((8 + 2 * O, 2, ROWS, 128), f32)
    mid = pltpu.VMEM((4 + 2 * O, ROWS, 128), f32)
    in_hbm = pl.BlockSpec(memory_space=pltpu.HBM)
    in_vmem = pl.BlockSpec(memory_space=pltpu.VMEM)
    arrays = (pressure_rhs, storage_fine, mobility_fine, storage_mid, mobility_mid, storage_coarse, mobility_coarse)
    result = pl.pallas_call(
        functools.partial(kernel, count_x, count_y),
        out_shape=(pltpu.VMEM(pressure_rhs.shape, f32),) * 2,
        in_specs=[in_hbm] * 7,
        out_specs=(in_vmem, in_vmem),
        scratch_shapes=[
            pltpu.VMEM((5, 8 + 2 * O, 2, ROWS, 128), f32),
            *[fine] * 10,
            pltpu.VMEM((4, 4 + 2 * O, ROWS, 128), f32),
            *[mid] * 11,
            pltpu.VMEM((8, ROWS, 128), f32),
            pltpu.VMEM((8, 2, ROWS, 128), f32),
            pltpu.VMEM((4, 8, 32, 64), f32),
            pltpu.VMEM((8, 32, 128), f32),
            pltpu.VMEM((6, 16, 128), f32),
            pltpu.VMEM((6, ROWS, 128), f32),
            pltpu.VMEM((4, 8, 8, 128), f32),
            pltpu.VMEM((7, 64, 128), f32),
            pltpu.VMEM((97, 8, 128), f32),
            pltpu.VMEM((1024, 128), f32),
            pltpu.SemaphoreType.DMA((16,)),
            pltpu.SemaphoreType.DMA((EXCHANGES,)),
            pltpu.SemaphoreType.DMA((EXCHANGES,)),
        ],
        compiler_params=pltpu.CompilerParams(
            collective_id=0, has_side_effects=True, vmem_limit_bytes=32 * 1024 * 1024
        ),
    )(*[pltpu.with_memory_space_constraint(array, pltpu.HBM) for array in arrays])
    out = jax.ShapeDtypeStruct(pressure_rhs.shape, f32)
    return pl.pallas_call(
        publish,
        out_shape=(out, out),
        in_specs=[in_vmem] * 2,
        out_specs=(in_hbm, in_hbm),
        scratch_shapes=[pltpu.SemaphoreType.DMA((2,))],
        compiler_params=pltpu.CompilerParams(vmem_limit_bytes=16 * 1024 * 1024),
    )(*result)


def solution(mesh):
    placed = (
        P("gx", "gy", None),
        P("gx", "gy", None),
        P(None, "gx", "gy", None),
        P("gx", "gy", None),
        P(None, "gx", "gy", None),
        P("gx", "gy", None),
        P(None, "gx", "gy", None),
    )
    return jax.shard_map(
        local,
        mesh=mesh,
        in_specs=placed,
        out_specs=(P("gx", "gy", None), P("gx", "gy", None)),
        check_vma=False,
    )
```

```python
import functools

import jax
import jax.numpy as jnp
from jax import lax
from jax.experimental import pallas as pl
from jax.experimental.pallas import tpu as pltpu
from jax.sharding import PartitionSpec as P

KC = 6
GROUP = 8
REACH = 4
DAMPING = 2.0 / 3.0

MESH = pl.DeviceIdType.MESH

O = 4
OP = 2
M0, M2, STORE, SOURCE, M1 = range(5)
OWN_C = slice(15, 17)
FINE_X, FINE_Y, COEF_X, COEF_Y, MID_IN, MID_F, FINE_V, COARSE_F, MID_V = range(9)
EXCHANGES = 9
NEIGHBOURS = ((1, 0), (-1, 0), (1, 1), (1, -1), (-1, 1), (-1, -1), (0, 1), (0, -1))


def reciprocal(values):
    guess = pl.reciprocal(values, approx=True)
    return guess * (2.0 - values * guess)


def harmonic(left, right):
    return 2.0 * left * right * reciprocal(left + right)


def next_of(values, axis):
    return pltpu.roll(values, values.shape[axis] - 1, axis)


def prev_of(values, axis):
    return pltpu.roll(values, 1, axis)


def next_paired(values, axis, pairs):
    first, second = lax.slice_in_dim(values, 0, 1, axis=axis), lax.slice_in_dim(values, 1, 2, axis=axis)
    return jnp.concatenate([second, next_of(first, pairs)], axis=axis)


def prev_paired(values, axis, pairs):
    first, second = lax.slice_in_dim(values, 0, 1, axis=axis), lax.slice_in_dim(values, 1, 2, axis=axis)
    return jnp.concatenate([prev_of(second, pairs), first], axis=axis)


def next_y(values):
    return next_paired(values, 0, values.ndim - 2)


def prev_y(values):
    return prev_paired(values, 0, values.ndim - 2)


def next_z(values):
    return next_paired(values, 1, 3) if values.ndim == 4 else next_of(values, 2)


def prev_z(values):
    return prev_paired(values, 1, 3) if values.ndim == 4 else prev_of(values, 2)


def one_hot(shape, test):
    row = lax.broadcasted_iota(jnp.int32, shape, 0)
    column = lax.broadcasted_iota(jnp.int32, shape, 1)
    return jnp.where(test(row, column), 1.0, 0.0).astype(jnp.bfloat16)


def pieces(values, count):
    parts = []
    for _ in range(count - 1):
        parts.append(values.astype(jnp.bfloat16))
        values = values - parts[-1].astype(jnp.float32)
    return parts + [values.astype(jnp.bfloat16)]


def times_one_hot(values, matrix, count):
    rows = values.shape[0]
    product = jnp.dot(jnp.concatenate(pieces(values, count), axis=0), matrix, preferred_element_type=jnp.float32)
    return total([product[at * rows : (at + 1) * rows] for at in range(count)])


def total(terms):
    while len(terms) > 1:
        pairs = [terms[i] + terms[i + 1] for i in range(0, len(terms) - 1, 2)]
        terms = pairs + terms[len(terms) - len(terms) % 2 :]
    return terms[0]


def source_span(step, first, n, width):
    return slice(first + n - width, first + n) if step > 0 else slice(first, first + (width if step < 0 else n))


def target_span(step, first, n, width):
    if step > 0:
        return slice(first - width, first)
    return slice(first + n, first + n + width) if step < 0 else slice(first, first + n)


def weights_x(level, mob, rows):
    wx = level[0]

    def body(x, _):
        wx[x] = harmonic(mob[0][x], mob[0][x + 1])
        return 0

    lax.fori_loop(*rows, body, 0, unroll=True)


def weights_yz(level, mob, rows, keep_y, keep_z):
    wx, wyu, wyd, wzu, wzd, diag, damp = level

    def body(x, _):
        second = mob[1][x]
        third = mob[2][x]
        up_y = harmonic(second, next_y(second)) * keep_y
        up_z = harmonic(third, next_z(third)) * keep_z
        wyu[x] = up_y
        wyd[x] = prev_y(up_y)
        wzu[x] = up_z
        wzd[x] = prev_z(up_z)
        return 0

    lax.fori_loop(*rows, body, 0, unroll=True)


def diagonals(level, store, rows):
    wx, wyu, wyd, wzu, wzd, diag, damp = level

    def body(x, _):
        all_of_it = store[x] + (wx[x] + wx[x - 1]) + (wyu[x] + wyd[x]) + (wzu[x] + wzd[x])
        diag[x] = all_of_it
        damp[x] = DAMPING * reciprocal(all_of_it)
        return 0

    lax.fori_loop(*rows, body, 0, unroll=True)


def row_residual(level, source, field, x):
    wx, wyu, wyd, wzu, wzd, diag, damp = level
    v = field[x]
    left = source[x] - diag[x] * v
    left = left + (wx[x] * field[x + 1] + wx[x - 1] * field[x - 1])
    left = left + (wyu[x] * next_y(v) + wyd[x] * prev_y(v))
    left = left + (wzu[x] * next_z(v) + wzd[x] * prev_z(v))
    return left


def sweep(level, source, field, result, rows):
    damp = level[6]

    def body(x, _):
        result[x] = field[x] + damp[x] * row_residual(level, source, field, x)
        return 0

    lax.fori_loop(rows[0], rows[1], body, 0, unroll=True)


def start_sweep(level, source, result, rows):
    damp = level[6]

    def body(x, _):
        result[x] = damp[x] * source[x]
        return 0

    lax.fori_loop(rows[0], rows[1], body, 0, unroll=True)


def kernel(
    count_x,
    count_y,
    rhs_h,
    store_f_h,
    mob_f_h,
    store_m_h,
    mob_m_h,
    store_c_h,
    mob_c_h,
    pressure,
    residual,
    f_stage,
    f_mixed,
    f_in,
    f_wx,
    f_wyu,
    f_wyd,
    f_wzu,
    f_wzd,
    f_diag,
    f_damp,
    f_a,
    f_b,
    f_x,
    m_in,
    m_src,
    m_wx,
    m_wyu,
    m_wyd,
    m_wzu,
    m_wzd,
    m_diag,
    m_damp,
    m_a,
    m_b,
    m_y,
    m_fold,
    f_rows,
    c_coef,
    c_src,
    c_ext,
    c_weights,
    c_bands,
    c_inverse,
    meter,
    local_sem,
    send_sem,
    recv_sem,
):
    gx = lax.axis_index("gx")
    gy = lax.axis_index("gy")

    def stepped(at, step, count):
        to = at + step
        if step > 0:
            return jnp.where(to >= count, to - count, to)
        return jnp.where(to < 0, to + count, to) if step < 0 else at

    along_gx = {step: stepped(gx, step, count_x) for step in (-1, 0, 1)}
    along_gy = {step: stepped(gy, step, count_y) for step in range(-REACH, REACH + 1)}

    def beside(sx, sy):
        return {"gx": along_gx[sx], "gy": along_gy[sy]}

    partners = NEIGHBOURS + tuple((0, e) for e in range(-REACH, REACH + 1) if abs(e) > 1)
    barrier = pltpu.get_barrier_semaphore()
    for step in partners:
        pl.semaphore_signal(barrier, inc=1, device_id=beside(*step), device_id_type=MESH)

    c_coef[:, 6:8] = jnp.ones((4, 2, 32, 64), jnp.float32)
    c_src[6:8] = jnp.zeros((2, 32, 128), jnp.float32)

    locals_ = []

    def bring(source, target):
        copy = pltpu.make_async_copy(source, target, local_sem.at[len(locals_)])
        copy.start()
        locals_.append(copy)
        return copy

    def push(at, source, target, step):
        pltpu.make_async_remote_copy(
            src_ref=source,
            dst_ref=target,
            send_sem=send_sem.at[at],
            recv_sem=recv_sem.at[at],
            device_id=beside(*step),
            device_id_type=MESH,
        ).start()
        rows = 1
        for size in source.shape[:-1]:
            rows = rows * size
        rows_of[at] = rows_of.get(at, 0) + rows

    rows_of = {}

    def all_of(at):
        if at == COEF_X:
            return c_coef.at[:, 0:4, 0:2, :]
        if at == COEF_Y:
            return c_coef.at[:, 0:6, 0:16, :]
        return meter.at[0 : rows_of[at], :]

    def received(at):
        pltpu.make_async_copy(all_of(at), all_of(at), recv_sem.at[at]).wait()

    def sent(at):
        pltpu.make_async_copy(all_of(at), all_of(at), send_sem.at[at]).wait()

    own8, pairs8 = slice(O, O + 8), slice(OP, OP + 4)
    own4, pairs4 = slice(O, O + 4), slice(OP, OP + 2)
    fine_in = [
        bring(mob_f_h, f_stage.at[0:3]),
        bring(store_f_h, f_stage.at[3]),
        bring(rhs_h, f_stage.at[4]),
    ]
    coarse_in = [
        bring(store_c_h, c_coef.at[0, 2:4, OWN_C, :]),
        bring(mob_c_h, c_coef.at[1:4, 2:4, OWN_C, :]),
    ]
    mid_in = []
    for y in range(4):
        parity, pair = y % 2, OP + y // 2
        mid_in.append(bring(mob_m_h.at[:, :, y, :], m_in.at[0:3, own4, parity, pair, :]))
        mid_in.append(bring(store_m_h.at[:, y, :], m_in.at[3, own4, parity, pair, :]))
    f_src = f_in.at[SOURCE]

    def spans(sx, sy, n, wide_x, wide_y):
        return (
            source_span(sx, O, n, wide_x),
            source_span(sy, OP, n // 2, wide_y),
            target_span(sx, O, n, wide_x),
            target_span(sy, OP, n // 2, wide_y),
        )

    faces_x = [step for step in NEIGHBOURS if step[1] == 0]
    faces_y = [step for step in NEIGHBOURS if step[0] == 0]
    corners = [step for step in NEIGHBOURS if step[0] != 0 and step[1] != 0]

    apart = one_hot((256, 256), lambda row, column: row == 2 * (column % 128) + column // 128)
    for copy in fine_in:
        copy.wait()
    sorted_z = times_one_hot(f_stage[...].reshape(320, 256), apart, 3)
    for half in range(2):
        f_mixed[half] = sorted_z[:, 128 * half : 128 * half + 128].reshape(40, 8, 128)

    def sort_y(x, _):
        for at, to in enumerate((M0, M1, M2, STORE, SOURCE)):
            for parity in range(2):
                for half in range(2):
                    rows = f_mixed[half, 8 * at + x, pl.ds(parity, 4, stride=2), :]
                    f_in[to, O + x, parity, half, pairs8] = rows
        return 0

    lax.fori_loop(0, 8, sort_y, 0, unroll=True)
    pl.semaphore_wait(barrier, len(partners))

    def push_fine(at, first, last, step, wide_x, wide_y):
        fields = slice(first, last + 1)
        ax, ay, bx, by = spans(*step, 8, wide_x, wide_y)
        push(at, f_in.at[fields, ax, :, :, ay, :], f_in.at[fields, bx, :, :, by, :], step)

    for copy in coarse_in:
        copy.wait()
    for sx, sy in faces_x:
        own = c_coef.at[:, 2:4, OWN_C, :]
        push(COEF_X, own, c_coef.at[:, 2 - 2 * sx : 4 - 2 * sx, OWN_C, :], (sx, sy))

    for step in faces_x:
        push_fine(FINE_X, M0, M0, step, 3, 1)
        push_fine(FINE_X, M2, M1, step, 2, 1)
    for step in corners:
        push_fine(FINE_X, M0, M0, step, 2, 1)
        push_fine(FINE_X, M1, M1, step, 2, 1)
        push_fine(FINE_X, M2, SOURCE, step, 1, 1)
    for step in faces_y:
        push_fine(FINE_Y, M0, SOURCE, step, 1, 1)
        push_fine(FINE_Y, M1, M1, step, 1, 2)

    for copy in mid_in:
        copy.wait()
    for step in NEIGHBOURS:
        ax, ay, bx, by = spans(*step, 4, 3 if step in corners else 4, 2)
        push(MID_IN, m_in.at[:, ax, :, ay, :], m_in.at[:, bx, :, by, :], step)

    one = jnp.float32(1.0)
    nil = jnp.float32(0.0)
    keep_x = (jnp.where(gx == 0, nil, one), jnp.where(gx == count_x - 1, nil, one))

    def keep_yz(own, shape):
        def index(axis):
            return lax.broadcasted_iota(jnp.int32, shape, axis)

        parity, pair, lane = index(0), index(len(shape) - 2), index(len(shape) - 1)
        end = jnp.where(gy == 0, OP - 1, -1)
        other = jnp.where(gy == count_y - 1, OP + own // 2 - 1, -1)
        keep_y = jnp.where((parity == 1) & ((pair == end) | (pair == other)), 0.0, 1.0)
        last_z = (lane == 127) if len(shape) == 3 else (lane == 127) & (index(1) == 1)
        return keep_y, jnp.where(last_z, 0.0, 1.0)

    fold_c = one_hot((64, 128), lambda row, column: row // 8 + 8 * (row % 8) == column // 2)

    fine = (f_wx, f_wyu, f_wyd, f_wzu, f_wzd, f_diag, f_damp)
    f_mob = (f_in.at[M0], f_in.at[M1], f_in.at[M2])
    f_store = f_in.at[STORE]
    keep_y, keep_z = keep_yz(8, (2, 2, 8, 128))
    received(FINE_Y)
    weights_yz(fine, f_mob, (O, O + 8), keep_y, keep_z)
    weights_x(fine, f_mob, (O, O + 7))
    diagonals(fine, f_store, (O + 1, O + 7))
    start_sweep(fine, f_src, f_a, (O + 1, O + 7))
    received(COEF_X)
    for e in range(-REACH, REACH + 1):
        if e != 0:
            target = c_coef.at[:, 0:6, OWN_C.start - 2 * e : OWN_C.stop - 2 * e, :]
            push(COEF_Y, c_coef.at[:, 0:6, OWN_C, :], target, (0, e))
    received(FINE_X)
    for rows in ((O - 3, O), (O + 7, O + 10)):
        weights_x(fine, f_mob, rows)
    f_wx[O - 1] = f_wx[O - 1] * keep_x[0]
    f_wx[O + 7] = f_wx[O + 7] * keep_x[1]
    for rows in ((O - 2, O), (O + 8, O + 10)):
        weights_yz(fine, f_mob, rows, keep_y, keep_z)
    for rows in ((O - 2, O + 1), (O + 7, O + 10)):
        diagonals(fine, f_store, rows)
        start_sweep(fine, f_src, f_a, rows)
    sweep(fine, f_src, f_a, f_b, (O - 1, O + 9))

    def folded(x, _):
        both = row_residual(fine, f_src, f_b, O + 2 * x) + row_residual(fine, f_src, f_b, O + 2 * x + 1)
        m_fold[x] = (both[0, 0] + both[0, 1]) + (both[1, 0] + both[1, 1])
        for parity in range(2):
            m_src[O + x, parity, pairs4] = m_fold[x, pl.ds(OP + parity, 2, stride=2), :]
        return 0

    lax.fori_loop(0, 4, folded, 0, unroll=True)
    for step in NEIGHBOURS:
        ax, ay, bx, by = spans(*step, 4, 2 if step in corners else 3, 1 if step in corners else 2)
        push(MID_F, m_src.at[ax, :, ay, :], m_src.at[bx, :, by, :], step)

    def keep_fine(x, _):
        f_x[x, :, :, pairs8] = f_b[x, :, :, pairs8]
        return 0

    lax.fori_loop(O, O + 8, keep_fine, 0, unroll=True)
    for step in NEIGHBOURS:
        ax, ay, bx, by = spans(*step, 8, 2 if step in corners else 3, 1 if step in corners else 2)
        push(FINE_V, f_x.at[ax, :, :, ay, :], f_x.at[bx, :, :, by, :], step)

    mid = (m_wx, m_wyu, m_wyd, m_wzu, m_wzd, m_diag, m_damp)
    m_mob = (m_in.at[0], m_in.at[1], m_in.at[2])
    keep_y, keep_z = keep_yz(4, (2, 8, 128))
    received(MID_IN)
    weights_x(mid, m_mob, (O - 4, O + 7))
    m_wx[O - 1] = m_wx[O - 1] * keep_x[0]
    m_wx[O + 3] = m_wx[O + 3] * keep_x[1]
    weights_yz(mid, m_mob, (O - 3, O + 7), keep_y, keep_z)
    diagonals(mid, m_in.at[3], (O - 3, O + 7))

    received(COEF_Y)
    coef = [c_coef[k, :, 8:24, :].reshape(128, 64).T for k in range(4)]
    second_prev = c_coef[2, :, 7:23, :].reshape(128, 64).T
    second_next = c_coef[2, :, 9:25, :].reshape(128, 64).T
    column = lax.broadcasted_iota(jnp.int32, (64, 128), 1)
    level_row = lax.broadcasted_iota(jnp.int32, (64, 128), 0)
    cells = 2 * count_y
    cell = 2 * gy + lax.rem(column, 16) + (cells - 7)
    block = 2 * GROUP
    offset = 4 + cells - (cells // block) * block
    shut_up = (lax.rem(cell + 1 - offset + 2 * block, block) == 0) | (lax.rem(cell + 1, cells) == 0)
    shut_down = (lax.rem(cell - offset + 2 * block, block) == 0) | (lax.rem(cell, cells) == 0)
    up_x = jnp.where(lax.rem(column, 32) < 16, harmonic(coef[1], pltpu.roll(coef[1], 112, 1)), 0.0)
    down_x = pltpu.roll(up_x, 16, 1)
    up_y = jnp.where(shut_up, 0.0, harmonic(coef[2], second_next))
    down_y = jnp.where(shut_down, 0.0, harmonic(second_prev, coef[2]))
    up_z = jnp.where(level_row == 63, 0.0, harmonic(coef[3], next_of(coef[3], 0)))
    down_z = prev_of(up_z, 0)
    main = coef[0] + (up_x + down_x) + (up_y + down_y) + (up_z + down_z)
    for at, band in enumerate((up_x, down_x, up_y, down_y, -down_z, main, -up_z)):
        c_bands[at] = band

    for at in (FINE_X, FINE_Y, COEF_X, COEF_Y, MID_IN):
        sent(at)

    received(MID_F)
    start_sweep(mid, m_src, m_a, (O - 2, O + 6))
    sweep(mid, m_src, m_a, m_b, (O - 1, O + 5))
    for ix in range(2):
        fold = row_residual(mid, m_src, m_b, O + 2 * ix) + row_residual(mid, m_src, m_b, O + 2 * ix + 1)
        c_src[2 + ix, OWN_C, :] = (fold[0] + fold[1])[pairs4]
    for e in sorted(range(-REACH, REACH + 1), key=lambda e: -abs(e)):
        for g in (1, -1, 0):
            if (g, e) != (0, 0):
                target = c_src.at[2 - 2 * g : 4 - 2 * g, OWN_C.start - 2 * e : OWN_C.stop - 2 * e, :]
                push(COARSE_F, c_src.at[2:4, OWN_C, :], target, (g, e))

    def keep_mid(x, _):
        m_y[x, :, pairs4] = m_b[x, :, pairs4]
        return 0

    lax.fori_loop(O, O + 4, keep_mid, 0, unroll=True)
    for step in NEIGHBOURS:
        ax, ay, bx, by = spans(*step, 4, 3 if step in corners else 4, 2)
        push(MID_V, m_y.at[ax, :, ay, :], m_y.at[bx, :, by, :], step)

    def registers(at):
        return [c_bands[at, pl.ds(place, 8, stride=8), :] for place in range(8)]

    for at in range(4):
        for place, values in enumerate(registers(at)):
            c_weights[at, place] = values
    low, main, high = (registers(at) for at in (4, 5, 6))
    ahead, back = [reciprocal(main[0])], {6: reciprocal(main[6])}
    upto, onfrom = [main[0]], {6: main[6]}
    for i in range(1, 7):
        upto.append(main[i] - low[i] * high[i - 1] * ahead[i - 1])
        ahead.append(reciprocal(upto[i]))
        j = 6 - i
        onfrom[j] = main[j] - high[j] * low[j + 1] * back[j + 1]
        back[j] = reciprocal(onfrom[j])
    rise = [-high[i] * ahead[i] for i in range(7)]
    fall = [-low[i] * back[i] for i in range(7)]
    inverse = {}
    for j in range(7):
        inverse[j, j] = reciprocal(upto[j] + onfrom[j] - main[j])
        for i in range(j - 1, -1, -1):
            inverse[i, j] = rise[i] * inverse[i + 1, j]
        for i in range(j + 1, 7):
            inverse[i, j] = fall[i] * inverse[i - 1, j]
    from_last = [inverse[i, 0] * low[0] for i in range(7)]
    from_own = [inverse[i, 6] * high[6] for i in range(7)]

    def turned(values, by):
        return pltpu.roll(values, by % 8, 0) if by % 8 else values

    face_main = main[7] - low[7] * from_own[6] - high[7] * turned(from_last[0], -1)
    face_low = -low[7] * from_last[6]
    face_high = -high[7] * turned(from_own[0], -1)
    spread_by = {0: jnp.ones((8, 128), jnp.float32)}
    for far in (1, 2, 4):
        over = reciprocal(face_main)
        alpha = -face_low * turned(over, far)
        gamma = -face_high * turned(over, -far)
        face_main = face_main + alpha * turned(face_high, far) + gamma * turned(face_low, -far)
        face_low, face_high = alpha * turned(face_low, far), gamma * turned(face_high, -far)
        wider = dict(spread_by)
        for by, values in spread_by.items():
            for step, factor in ((far, alpha), (-far, gamma)):
                term = factor * turned(values, step)
                key = (by + step) % 8
                wider[key] = wider[key] + term if key in wider else term
        spread_by = wider
    over = reciprocal(face_main)
    own_by = [over * spread_by[by] for by in range(8)]
    next_by = [own_by[(by + 1) % 8] * turned(high[7], by + 1) for by in range(8)]
    for i in range(7):
        for j in range(7):
            c_inverse[7 * i + j] = inverse[i, j]
        c_inverse[49 + i] = from_last[i]
        c_inverse[56 + i] = from_own[i]
    for by in range(8):
        c_inverse[64 + by] = own_by[by]
        c_inverse[72 + by] = next_by[by]
        c_inverse[80 + by] = turned(own_by[by - 1], 1)
        c_inverse[88 + by] = turned(next_by[by - 1], 1)
    c_inverse[63] = low[7]

    def lines(values):
        inner = [total([c_inverse[7 * i + j] * values[j] for j in range(7)]) for i in range(7)]
        face = values[7] - c_inverse[63] * inner[6]
        faces = [turned(face, by) for by in range(8)]
        firsts = [turned(inner[0], by) for by in range(8)]

        def interface(at):
            terms = [c_inverse[at + by] * faces[by] for by in range(8)]
            return total(terms) - total([c_inverse[at + 8 + by] * firsts[by] for by in range(8)])

        here, before = interface(64), interface(80)
        return tuple(inner[i] - (c_inverse[49 + i] * before + c_inverse[56 + i] * here) for i in range(7)) + (here,)

    for at in (MID_F, FINE_V):
        sent(at)

    received(COARSE_F)
    source = lax.dot_general(
        jnp.concatenate([fold_c] * 2, axis=1),
        jnp.concatenate(pieces(c_src[:, 8:24, :].reshape(128, 128), 2), axis=1),
        (((1,), (1,)), ((), ())),
        preferred_element_type=jnp.float32,
    )
    sources = [source[8 * place : 8 * place + 8] for place in range(8)]

    def turn(_, z):
        pushed = []
        for place in range(8):
            own = z[place]
            along_x = c_weights[0, place] * pltpu.roll(own, 112, 1) + c_weights[1, place] * pltpu.roll(own, 16, 1)
            along_y = c_weights[2, place] * next_of(own, 1) + c_weights[3, place] * prev_of(own, 1)
            pushed.append(sources[place] + (along_x + along_y))
        return lines(pushed)

    z = lax.fori_loop(0, KC - 1, turn, lines(sources))
    c_ext[...] = times_one_hot(jnp.concatenate(z, axis=0).T[0:96], fold_c, 2).reshape(6, 16, 128)

    received(MID_V)

    def raise_mid(x, _):
        rows = c_ext[x, 5:13, :]
        for along in range(2):
            for parity in range(2):
                m_a[2 * x + along, parity] = m_y[2 * x + along, parity] + rows
        return 0

    lax.fori_loop(0, 6, raise_mid, 0, unroll=True)
    sweep(mid, m_src, m_a, m_b, (O - 3, O + 7))
    sweep(mid, m_src, m_b, m_a, (O - 2, O + 6))

    received(FINE_V)

    def raise_fine(x, _):
        for parity in range(2):
            m_fold[x, pl.ds(parity, 4, stride=2), :] = m_a[O - 2 + x, parity, 1:5]
        rows = m_fold[x]
        for along in range(2):
            for parity in range(2):
                for half in range(2):
                    at = (2 * x + along, parity, half)
                    f_a[at] = f_x[at] + rows
        return 0

    lax.fori_loop(0, 8, raise_fine, 0, unroll=True)
    sweep(fine, f_src, f_a, f_b, (O - 2, O + 10))
    sweep(fine, f_src, f_b, f_a, (O - 1, O + 9))

    together = one_hot((256, 256), lambda row, column: column == 2 * (row % 128) + row // 128)

    def in_order(field, result):
        def sort_back(x, _):
            for parity in range(2):
                for half in range(2):
                    f_rows[half, x, pl.ds(parity, 8, stride=2), :] = field[O + x, parity, half]
            return 0

        lax.fori_loop(0, 8, sort_back, 0, unroll=True)
        halves = [f_rows[half, :, O : O + 8, :].reshape(64, 128) for half in range(2)]
        result[...] = times_one_hot(jnp.concatenate(halves, axis=1), together, 3).reshape(8, 8, 256)

    in_order(f_a, pressure)

    def last(x, _):
        f_b[x] = row_residual(fine, f_src, f_a, x)
        return 0

    lax.fori_loop(O, O + 8, last, 0, unroll=True)
    in_order(f_b, residual)
    for at in (COARSE_F, MID_V):
        sent(at)


def publish(pressure, residual, pressure_h, residual_h, sem):
    copies = [
        pltpu.make_async_copy(pressure, pressure_h, sem.at[0]),
        pltpu.make_async_copy(residual, residual_h, sem.at[1]),
    ]
    for copy in copies:
        copy.start()
    for copy in copies:
        copy.wait()


def local(pressure_rhs, storage_fine, mobility_fine, storage_mid, mobility_mid, storage_coarse, mobility_coarse):
    count_x = lax.axis_size("gx")
    count_y = lax.axis_size("gy")
    f32 = jnp.float32
    fine = pltpu.VMEM((8 + 2 * O, 2, 2, 8, 128), f32)
    mid = pltpu.VMEM((4 + 2 * O, 2, 8, 128), f32)
    in_hbm = pl.BlockSpec(memory_space=pltpu.HBM)
    in_vmem = pl.BlockSpec(memory_space=pltpu.VMEM)
    arrays = (pressure_rhs, storage_fine, mobility_fine, storage_mid, mobility_mid, storage_coarse, mobility_coarse)
    result = pl.pallas_call(
        functools.partial(kernel, count_x, count_y),
        out_shape=(pltpu.VMEM(pressure_rhs.shape, f32),) * 2,
        in_specs=[in_hbm] * 7,
        out_specs=(in_vmem, in_vmem),
        scratch_shapes=[
            pltpu.VMEM((5, 8, 8, 256), f32),
            pltpu.VMEM((2, 40, 8, 128), f32),
            pltpu.VMEM((5, 8 + 2 * O, 2, 2, 8, 128), f32),
            *[fine] * 10,
            pltpu.VMEM((4, 4 + 2 * O, 2, 8, 128), f32),
            *[mid] * 11,
            pltpu.VMEM((8, 8, 128), f32),
            pltpu.VMEM((2, 8, 16, 128), f32),
            pltpu.VMEM((4, 8, 32, 64), f32),
            pltpu.VMEM((8, 32, 128), f32),
            pltpu.VMEM((6, 16, 128), f32),
            pltpu.VMEM((4, 8, 8, 128), f32),
            pltpu.VMEM((7, 64, 128), f32),
            pltpu.VMEM((97, 8, 128), f32),
            pltpu.VMEM((1024, 128), f32),
            pltpu.SemaphoreType.DMA((16,)),
            pltpu.SemaphoreType.DMA((EXCHANGES,)),
            pltpu.SemaphoreType.DMA((EXCHANGES,)),
        ],
        compiler_params=pltpu.CompilerParams(
            collective_id=0, has_side_effects=True, vmem_limit_bytes=32 * 1024 * 1024
        ),
    )(*[pltpu.with_memory_space_constraint(array, pltpu.HBM) for array in arrays])
    out = jax.ShapeDtypeStruct(pressure_rhs.shape, f32)
    return pl.pallas_call(
        publish,
        out_shape=(out, out),
        in_specs=[in_vmem] * 2,
        out_specs=(in_hbm, in_hbm),
        scratch_shapes=[pltpu.SemaphoreType.DMA((2,))],
        compiler_params=pltpu.CompilerParams(vmem_limit_bytes=16 * 1024 * 1024),
    )(*result)


def solution(mesh):
    placed = (
        P("gx", "gy", None),
        P("gx", "gy", None),
        P(None, "gx", "gy", None),
        P("gx", "gy", None),
        P(None, "gx", "gy", None),
        P("gx", "gy", None),
        P(None, "gx", "gy", None),
    )
    return jax.shard_map(
        local,
        mesh=mesh,
        in_specs=placed,
        out_specs=(P("gx", "gy", None), P("gx", "gy", None)),
        check_vma=False,
    )
```

```python
import functools

import jax
import jax.numpy as jnp
from jax import lax
from jax.experimental import pallas as pl
from jax.experimental.pallas import tpu as pltpu
from jax.sharding import PartitionSpec as P

KC = 6
GROUP = 8
REACH = 4
DAMPING = 2.0 / 3.0

MESH = pl.DeviceIdType.MESH

O = 4
OP = 2
M0, M2, STORE, SOURCE, M1 = range(5)
OWN_C = slice(15, 17)
FINE_X, FINE_Y, COEF_X, COEF_Y, MID_IN, MID_F, FINE_V, COARSE_F, MID_V = range(9)
EXCHANGES = 9
NEIGHBOURS = ((1, 0), (-1, 0), (1, 1), (1, -1), (-1, 1), (-1, -1), (0, 1), (0, -1))


def reciprocal(values):
    guess = pl.reciprocal(values, approx=True)
    return guess * (2.0 - values * guess)


def harmonic(left, right):
    return 2.0 * left * right * reciprocal(left + right)


def next_of(values, axis):
    return pltpu.roll(values, values.shape[axis] - 1, axis)


def prev_of(values, axis):
    return pltpu.roll(values, 1, axis)


def next_paired(values, axis, pairs):
    first, second = lax.slice_in_dim(values, 0, 1, axis=axis), lax.slice_in_dim(values, 1, 2, axis=axis)
    return jnp.concatenate([second, next_of(first, pairs)], axis=axis)


def prev_paired(values, axis, pairs):
    first, second = lax.slice_in_dim(values, 0, 1, axis=axis), lax.slice_in_dim(values, 1, 2, axis=axis)
    return jnp.concatenate([prev_of(second, pairs), first], axis=axis)


def next_y(values):
    return next_paired(values, 0, values.ndim - 2)


def prev_y(values):
    return prev_paired(values, 0, values.ndim - 2)


def next_z(values):
    return next_paired(values, 1, 3) if values.ndim == 4 else next_of(values, 2)


def prev_z(values):
    return prev_paired(values, 1, 3) if values.ndim == 4 else prev_of(values, 2)


def one_hot(shape, test):
    row = lax.broadcasted_iota(jnp.int32, shape, 0)
    column = lax.broadcasted_iota(jnp.int32, shape, 1)
    return jnp.where(test(row, column), 1.0, 0.0).astype(jnp.bfloat16)


def pieces(values, count):
    parts = []
    for _ in range(count - 1):
        parts.append(values.astype(jnp.bfloat16))
        values = values - parts[-1].astype(jnp.float32)
    return parts + [values.astype(jnp.bfloat16)]


def times_one_hot(values, matrix, count):
    rows = values.shape[0]
    product = jnp.dot(jnp.concatenate(pieces(values, count), axis=0), matrix, preferred_element_type=jnp.float32)
    return total([product[at * rows : (at + 1) * rows] for at in range(count)])


def total(terms):
    while len(terms) > 1:
        pairs = [terms[i] + terms[i + 1] for i in range(0, len(terms) - 1, 2)]
        terms = pairs + terms[len(terms) - len(terms) % 2 :]
    return terms[0]


def source_span(step, first, n, width):
    return slice(first + n - width, first + n) if step > 0 else slice(first, first + (width if step < 0 else n))


def target_span(step, first, n, width):
    if step > 0:
        return slice(first - width, first)
    return slice(first + n, first + n + width) if step < 0 else slice(first, first + n)


def weights_x(level, mob, rows):
    wx = level[0]

    def body(x, _):
        wx[x] = harmonic(mob[0][x], mob[0][x + 1])
        return 0

    lax.fori_loop(*rows, body, 0, unroll=True)


def weights_yz(level, mob, rows, keep_y, keep_z):
    wx, wyu, wyd, wzu, wzd, diag, damp = level

    def body(x, _):
        second = mob[1][x]
        third = mob[2][x]
        up_y = harmonic(second, next_y(second)) * keep_y
        up_z = harmonic(third, next_z(third)) * keep_z
        wyu[x] = up_y
        wyd[x] = prev_y(up_y)
        wzu[x] = up_z
        wzd[x] = prev_z(up_z)
        return 0

    lax.fori_loop(*rows, body, 0, unroll=True)


def diagonals(level, store, rows):
    wx, wyu, wyd, wzu, wzd, diag, damp = level

    def body(x, _):
        all_of_it = store[x] + (wx[x] + wx[x - 1]) + (wyu[x] + wyd[x]) + (wzu[x] + wzd[x])
        diag[x] = all_of_it
        damp[x] = DAMPING * reciprocal(all_of_it)
        return 0

    lax.fori_loop(*rows, body, 0, unroll=True)


def row_residual(level, source, field, x):
    wx, wyu, wyd, wzu, wzd, diag, damp = level
    v = field[x]
    left = source[x] - diag[x] * v
    left = left + (wx[x] * field[x + 1] + wx[x - 1] * field[x - 1])
    left = left + (wyu[x] * next_y(v) + wyd[x] * prev_y(v))
    left = left + (wzu[x] * next_z(v) + wzd[x] * prev_z(v))
    return left


def sweep(level, source, field, result, rows):
    damp = level[6]

    def body(x, _):
        result[x] = field[x] + damp[x] * row_residual(level, source, field, x)
        return 0

    lax.fori_loop(rows[0], rows[1], body, 0, unroll=True)


def start_sweep(level, source, result, rows):
    damp = level[6]

    def body(x, _):
        result[x] = damp[x] * source[x]
        return 0

    lax.fori_loop(rows[0], rows[1], body, 0, unroll=True)


def kernel(
    count_x,
    count_y,
    rhs_h,
    store_f_h,
    mob_f_h,
    store_m_h,
    mob_m_h,
    store_c_h,
    mob_c_h,
    pressure,
    residual,
    f_stage,
    f_mixed,
    f_in,
    f_wx,
    f_wyu,
    f_wyd,
    f_wzu,
    f_wzd,
    f_diag,
    f_damp,
    f_a,
    f_b,
    f_x,
    m_in,
    m_src,
    m_wx,
    m_wyu,
    m_wyd,
    m_wzu,
    m_wzd,
    m_diag,
    m_damp,
    m_a,
    m_b,
    m_y,
    m_fold,
    f_rows,
    c_coef,
    c_src,
    c_ext,
    c_weights,
    c_bands,
    c_inverse,
    meter,
    spare,
    c_spare,
    local_sem,
    send_sem,
    recv_sem,
):
    gx = lax.axis_index("gx")
    gy = lax.axis_index("gy")

    def stepped(at, step, count):
        to = at + step
        if step > 0:
            return jnp.where(to >= count, to - count, to)
        return jnp.where(to < 0, to + count, to) if step < 0 else at

    along_gx = {step: stepped(gx, step, count_x) for step in (-1, 0, 1)}
    along_gy = {step: stepped(gy, step, count_y) for step in range(-REACH, REACH + 1)}

    def beside(sx, sy):
        return {"gx": along_gx[sx], "gy": along_gy[sy]}

    def ahead_of(sx):
        return gx < count_x - 1 if sx > 0 else gx > 0

    barrier = pltpu.get_barrier_semaphore()

    def greet(steps):
        for step in steps:
            pl.semaphore_signal(barrier, inc=1, device_id=beside(*step), device_id_type=MESH)

    for side in (1, -1):

        @pl.when(ahead_of(side))
        def _():
            greet([step for step in NEIGHBOURS if step[0] == side])

    straight = [(0, e) for e in range(-REACH, REACH + 1) if e != 0]
    greet(straight)
    partners = len(straight) + jnp.where(gx > 0, 3, 0) + jnp.where(gx < count_x - 1, 3, 0)

    c_coef[:, 6:8] = jnp.ones((4, 2, 32, 64), jnp.float32)
    c_src[6:8] = jnp.zeros((2, 32, 128), jnp.float32)

    locals_ = []

    def bring(source, target):
        copy = pltpu.make_async_copy(source, target, local_sem.at[len(locals_)])
        copy.start()
        locals_.append(copy)
        return copy

    def exchange(at, messages):
        sizes = []
        for source, _, _ in messages:
            rows = 1
            for size in source.shape[:-1]:
                rows = rows * size
            sizes.append(rows)
        rows_of[at] = rows_of.get(at, 0) + sum(sizes)

        def send(side):
            for source, target, step in messages:
                if step[0] == side:
                    pltpu.make_async_remote_copy(
                        src_ref=source,
                        dst_ref=target,
                        send_sem=send_sem.at[at],
                        recv_sem=recv_sem.at[at],
                        device_id=beside(*step),
                        device_id_type=MESH,
                    ).start()

        for side in (1, -1):
            rows = sum(size for size, message in zip(sizes, messages) if message[2][0] == side)
            if rows == 0:
                continue
            first = spent[0]
            spent[0] += rows

            @pl.when(ahead_of(side))
            def _():
                send(side)

            @pl.when(jnp.logical_not(ahead_of(side)))
            def _():
                if at == COEF_X:
                    pltpu.make_async_copy(c_coef.at[:, 2:4, OWN_C, :], c_spare, send_sem.at[at]).start()
                else:
                    spare_to = spare.at[first : first + rows, :]
                    pltpu.make_async_copy(meter.at[0:rows, :], spare_to, send_sem.at[at]).start()

            @pl.when(jnp.logical_not(ahead_of(-side)))
            def _():
                for source, target, step in messages:
                    if step[0] == side:
                        pltpu.make_async_copy(source, target, recv_sem.at[at]).start()

        send(0)

    spent = [0]
    rows_of = {}

    def all_of(at):
        if at == COEF_X:
            return c_coef.at[:, 0:4, 0:2, :]
        if at == COEF_Y:
            return c_coef.at[:, 0:6, 0:16, :]
        return meter.at[0 : rows_of[at], :]

    def received(at):
        pltpu.make_async_copy(all_of(at), all_of(at), recv_sem.at[at]).wait()

    def sent(at):
        pltpu.make_async_copy(all_of(at), all_of(at), send_sem.at[at]).wait()

    own8, pairs8 = slice(O, O + 8), slice(OP, OP + 4)
    own4, pairs4 = slice(O, O + 4), slice(OP, OP + 2)
    fine_in = [
        bring(mob_f_h, f_stage.at[0:3]),
        bring(store_f_h, f_stage.at[3]),
        bring(rhs_h, f_stage.at[4]),
    ]
    coarse_in = [
        bring(store_c_h, c_coef.at[0, 2:4, OWN_C, :]),
        bring(mob_c_h, c_coef.at[1:4, 2:4, OWN_C, :]),
    ]
    mid_in = []
    for y in range(4):
        parity, pair = y % 2, OP + y // 2
        mid_in.append(bring(mob_m_h.at[:, :, y, :], m_in.at[0:3, own4, parity, pair, :]))
        mid_in.append(bring(store_m_h.at[:, y, :], m_in.at[3, own4, parity, pair, :]))
    f_src = f_in.at[SOURCE]

    def spans(sx, sy, n, wide_x, wide_y):
        return (
            source_span(sx, O, n, wide_x),
            source_span(sy, OP, n // 2, wide_y),
            target_span(sx, O, n, wide_x),
            target_span(sy, OP, n // 2, wide_y),
        )

    faces_x = [step for step in NEIGHBOURS if step[1] == 0]
    faces_y = [step for step in NEIGHBOURS if step[0] == 0]
    corners = [step for step in NEIGHBOURS if step[0] != 0 and step[1] != 0]

    apart = one_hot((256, 256), lambda row, column: row == 2 * (column % 128) + column // 128)
    for copy in fine_in:
        copy.wait()
    sorted_z = times_one_hot(f_stage[...].reshape(320, 256), apart, 3)
    for half in range(2):
        f_mixed[half] = sorted_z[:, 128 * half : 128 * half + 128].reshape(40, 8, 128)

    def sort_y(x, _):
        for at, to in enumerate((M0, M1, M2, STORE, SOURCE)):
            for parity in range(2):
                for half in range(2):
                    rows = f_mixed[half, 8 * at + x, pl.ds(parity, 4, stride=2), :]
                    f_in[to, O + x, parity, half, pairs8] = rows
        return 0

    lax.fori_loop(0, 8, sort_y, 0, unroll=True)
    pl.semaphore_wait(barrier, partners)

    def part(first, last, step, wide_x, wide_y):
        fields = slice(first, last + 1)
        ax, ay, bx, by = spans(*step, 8, wide_x, wide_y)
        return (f_in.at[fields, ax, :, :, ay, :], f_in.at[fields, bx, :, :, by, :], step)

    for copy in coarse_in:
        copy.wait()
    exchange(
        COEF_X,
        [
            (c_coef.at[:, 2:4, OWN_C, :], c_coef.at[:, 2 - 2 * sx : 4 - 2 * sx, OWN_C, :], (sx, sy))
            for sx, sy in faces_x
        ],
    )

    messages = []
    for step in faces_x:
        messages += [part(M0, M0, step, 3, 1), part(M2, M1, step, 2, 1)]
    for step in corners:
        messages += [part(M0, M0, step, 2, 1), part(M1, M1, step, 2, 1), part(M2, SOURCE, step, 1, 1)]
    exchange(FINE_X, messages)
    messages = []
    for step in faces_y:
        messages += [part(M0, SOURCE, step, 1, 1), part(M1, M1, step, 1, 2)]
    exchange(FINE_Y, messages)

    for copy in mid_in:
        copy.wait()
    messages = []
    for step in NEIGHBOURS:
        ax, ay, bx, by = spans(*step, 4, 3 if step in corners else 4, 2)
        messages.append((m_in.at[:, ax, :, ay, :], m_in.at[:, bx, :, by, :], step))
    exchange(MID_IN, messages)

    one = jnp.float32(1.0)
    nil = jnp.float32(0.0)
    keep_x = (jnp.where(gx == 0, nil, one), jnp.where(gx == count_x - 1, nil, one))

    def keep_yz(own, shape):
        def index(axis):
            return lax.broadcasted_iota(jnp.int32, shape, axis)

        parity, pair, lane = index(0), index(len(shape) - 2), index(len(shape) - 1)
        end = jnp.where(gy == 0, OP - 1, -1)
        other = jnp.where(gy == count_y - 1, OP + own // 2 - 1, -1)
        keep_y = jnp.where((parity == 1) & ((pair == end) | (pair == other)), 0.0, 1.0)
        last_z = (lane == 127) if len(shape) == 3 else (lane == 127) & (index(1) == 1)
        return keep_y, jnp.where(last_z, 0.0, 1.0)

    fold_c = one_hot((64, 128), lambda row, column: row // 8 + 8 * (row % 8) == column // 2)

    fine = (f_wx, f_wyu, f_wyd, f_wzu, f_wzd, f_diag, f_damp)
    f_mob = (f_in.at[M0], f_in.at[M1], f_in.at[M2])
    f_store = f_in.at[STORE]
    keep_y, keep_z = keep_yz(8, (2, 2, 8, 128))
    received(FINE_Y)
    weights_yz(fine, f_mob, (O, O + 8), keep_y, keep_z)
    weights_x(fine, f_mob, (O, O + 7))
    diagonals(fine, f_store, (O + 1, O + 7))
    start_sweep(fine, f_src, f_a, (O + 1, O + 7))
    received(COEF_X)
    messages = []
    for step in straight:
        target = c_coef.at[:, 0:6, OWN_C.start - 2 * step[1] : OWN_C.stop - 2 * step[1], :]
        messages.append((c_coef.at[:, 0:6, OWN_C, :], target, step))
    exchange(COEF_Y, messages)
    received(FINE_X)
    for rows in ((O - 3, O), (O + 7, O + 10)):
        weights_x(fine, f_mob, rows)
    f_wx[O - 1] = f_wx[O - 1] * keep_x[0]
    f_wx[O + 7] = f_wx[O + 7] * keep_x[1]
    for rows in ((O - 2, O), (O + 8, O + 10)):
        weights_yz(fine, f_mob, rows, keep_y, keep_z)
    for rows in ((O - 2, O + 1), (O + 7, O + 10)):
        diagonals(fine, f_store, rows)
        start_sweep(fine, f_src, f_a, rows)
    sweep(fine, f_src, f_a, f_b, (O - 1, O + 9))

    def folded(x, _):
        both = row_residual(fine, f_src, f_b, O + 2 * x) + row_residual(fine, f_src, f_b, O + 2 * x + 1)
        m_fold[x] = (both[0, 0] + both[0, 1]) + (both[1, 0] + both[1, 1])
        for parity in range(2):
            m_src[O + x, parity, pairs4] = m_fold[x, pl.ds(OP + parity, 2, stride=2), :]
        return 0

    lax.fori_loop(0, 4, folded, 0, unroll=True)
    messages = []
    for step in NEIGHBOURS:
        ax, ay, bx, by = spans(*step, 4, 2 if step in corners else 3, 1 if step in corners else 2)
        messages.append((m_src.at[ax, :, ay, :], m_src.at[bx, :, by, :], step))
    exchange(MID_F, messages)

    def keep_fine(x, _):
        f_x[x, :, :, pairs8] = f_b[x, :, :, pairs8]
        return 0

    lax.fori_loop(O, O + 8, keep_fine, 0, unroll=True)
    messages = []
    for step in NEIGHBOURS:
        ax, ay, bx, by = spans(*step, 8, 2 if step in corners else 3, 1 if step in corners else 2)
        messages.append((f_x.at[ax, :, :, ay, :], f_x.at[bx, :, :, by, :], step))
    exchange(FINE_V, messages)

    mid = (m_wx, m_wyu, m_wyd, m_wzu, m_wzd, m_diag, m_damp)
    m_mob = (m_in.at[0], m_in.at[1], m_in.at[2])
    keep_y, keep_z = keep_yz(4, (2, 8, 128))
    received(MID_IN)
    weights_x(mid, m_mob, (O - 4, O + 7))
    m_wx[O - 1] = m_wx[O - 1] * keep_x[0]
    m_wx[O + 3] = m_wx[O + 3] * keep_x[1]
    weights_yz(mid, m_mob, (O - 3, O + 7), keep_y, keep_z)
    diagonals(mid, m_in.at[3], (O - 3, O + 7))

    received(COEF_Y)
    coef = [c_coef[k, :, 8:24, :].reshape(128, 64).T for k in range(4)]
    second_prev = c_coef[2, :, 7:23, :].reshape(128, 64).T
    second_next = c_coef[2, :, 9:25, :].reshape(128, 64).T
    column = lax.broadcasted_iota(jnp.int32, (64, 128), 1)
    level_row = lax.broadcasted_iota(jnp.int32, (64, 128), 0)
    cells = 2 * count_y
    cell = 2 * gy + lax.rem(column, 16) + (cells - 7)
    block = 2 * GROUP
    offset = 4 + cells - (cells // block) * block
    shut_up = (lax.rem(cell + 1 - offset + 2 * block, block) == 0) | (lax.rem(cell + 1, cells) == 0)
    shut_down = (lax.rem(cell - offset + 2 * block, block) == 0) | (lax.rem(cell, cells) == 0)
    up_x = jnp.where(lax.rem(column, 32) < 16, harmonic(coef[1], pltpu.roll(coef[1], 112, 1)), 0.0)
    down_x = pltpu.roll(up_x, 16, 1)
    up_y = jnp.where(shut_up, 0.0, harmonic(coef[2], second_next))
    down_y = jnp.where(shut_down, 0.0, harmonic(second_prev, coef[2]))
    up_z = jnp.where(level_row == 63, 0.0, harmonic(coef[3], next_of(coef[3], 0)))
    down_z = prev_of(up_z, 0)
    main = coef[0] + (up_x + down_x) + (up_y + down_y) + (up_z + down_z)
    for at, band in enumerate((up_x, down_x, up_y, down_y, -down_z, main, -up_z)):
        c_bands[at] = band

    for at in (FINE_X, FINE_Y, COEF_X, COEF_Y, MID_IN):
        sent(at)

    received(MID_F)
    start_sweep(mid, m_src, m_a, (O - 2, O + 6))
    sweep(mid, m_src, m_a, m_b, (O - 1, O + 5))
    for ix in range(2):
        fold = row_residual(mid, m_src, m_b, O + 2 * ix) + row_residual(mid, m_src, m_b, O + 2 * ix + 1)
        c_src[2 + ix, OWN_C, :] = (fold[0] + fold[1])[pairs4]
    messages = []
    for e in sorted(range(-REACH, REACH + 1), key=lambda e: -abs(e)):
        for g in (1, -1, 0):
            if (g, e) != (0, 0):
                target = c_src.at[2 - 2 * g : 4 - 2 * g, OWN_C.start - 2 * e : OWN_C.stop - 2 * e, :]
                messages.append((c_src.at[2:4, OWN_C, :], target, (g, e)))
    exchange(COARSE_F, messages)

    def keep_mid(x, _):
        m_y[x, :, pairs4] = m_b[x, :, pairs4]
        return 0

    lax.fori_loop(O, O + 4, keep_mid, 0, unroll=True)
    messages = []
    for step in NEIGHBOURS:
        ax, ay, bx, by = spans(*step, 4, 3 if step in corners else 4, 2)
        messages.append((m_y.at[ax, :, ay, :], m_y.at[bx, :, by, :], step))
    exchange(MID_V, messages)

    def registers(at):
        return [c_bands[at, pl.ds(place, 8, stride=8), :] for place in range(8)]

    for at in range(4):
        for place, values in enumerate(registers(at)):
            c_weights[at, place] = values
    low, main, high = (registers(at) for at in (4, 5, 6))
    ahead, back = [reciprocal(main[0])], {6: reciprocal(main[6])}
    upto, onfrom = [main[0]], {6: main[6]}
    for i in range(1, 7):
        upto.append(main[i] - low[i] * high[i - 1] * ahead[i - 1])
        ahead.append(reciprocal(upto[i]))
        j = 6 - i
        onfrom[j] = main[j] - high[j] * low[j + 1] * back[j + 1]
        back[j] = reciprocal(onfrom[j])
    rise = [-high[i] * ahead[i] for i in range(7)]
    fall = [-low[i] * back[i] for i in range(7)]
    inverse = {}
    for j in range(7):
        inverse[j, j] = reciprocal(upto[j] + onfrom[j] - main[j])
        for i in range(j - 1, -1, -1):
            inverse[i, j] = rise[i] * inverse[i + 1, j]
        for i in range(j + 1, 7):
            inverse[i, j] = fall[i] * inverse[i - 1, j]
    from_last = [inverse[i, 0] * low[0] for i in range(7)]
    from_own = [inverse[i, 6] * high[6] for i in range(7)]

    def turned(values, by):
        return pltpu.roll(values, by % 8, 0) if by % 8 else values

    face_main = main[7] - low[7] * from_own[6] - high[7] * turned(from_last[0], -1)
    face_low = -low[7] * from_last[6]
    face_high = -high[7] * turned(from_own[0], -1)
    spread_by = {0: jnp.ones((8, 128), jnp.float32)}
    for far in (1, 2, 4):
        over = reciprocal(face_main)
        alpha = -face_low * turned(over, far)
        gamma = -face_high * turned(over, -far)
        face_main = face_main + alpha * turned(face_high, far) + gamma * turned(face_low, -far)
        face_low, face_high = alpha * turned(face_low, far), gamma * turned(face_high, -far)
        wider = dict(spread_by)
        for by, values in spread_by.items():
            for step, factor in ((far, alpha), (-far, gamma)):
                term = factor * turned(values, step)
                key = (by + step) % 8
                wider[key] = wider[key] + term if key in wider else term
        spread_by = wider
    over = reciprocal(face_main)
    own_by = [over * spread_by[by] for by in range(8)]
    next_by = [own_by[(by + 1) % 8] * turned(high[7], by + 1) for by in range(8)]
    for i in range(7):
        for j in range(7):
            c_inverse[7 * i + j] = inverse[i, j]
        c_inverse[49 + i] = from_last[i]
        c_inverse[56 + i] = from_own[i]
    for by in range(8):
        c_inverse[64 + by] = own_by[by]
        c_inverse[72 + by] = next_by[by]
        c_inverse[80 + by] = turned(own_by[by - 1], 1)
        c_inverse[88 + by] = turned(next_by[by - 1], 1)
    c_inverse[63] = low[7]

    def lines(values):
        inner = [total([c_inverse[7 * i + j] * values[j] for j in range(7)]) for i in range(7)]
        face = values[7] - c_inverse[63] * inner[6]
        faces = [turned(face, by) for by in range(8)]
        firsts = [turned(inner[0], by) for by in range(8)]

        def interface(at):
            terms = [c_inverse[at + by] * faces[by] for by in range(8)]
            return total(terms) - total([c_inverse[at + 8 + by] * firsts[by] for by in range(8)])

        here, before = interface(64), interface(80)
        return tuple(inner[i] - (c_inverse[49 + i] * before + c_inverse[56 + i] * here) for i in range(7)) + (here,)

    for at in (MID_F, FINE_V):
        sent(at)

    received(COARSE_F)
    source = lax.dot_general(
        jnp.concatenate([fold_c] * 2, axis=1),
        jnp.concatenate(pieces(c_src[:, 8:24, :].reshape(128, 128), 2), axis=1),
        (((1,), (1,)), ((), ())),
        preferred_element_type=jnp.float32,
    )
    sources = [source[8 * place : 8 * place + 8] for place in range(8)]

    def turn(_, z):
        pushed = []
        for place in range(8):
            own = z[place]
            along_x = c_weights[0, place] * pltpu.roll(own, 112, 1) + c_weights[1, place] * pltpu.roll(own, 16, 1)
            along_y = c_weights[2, place] * next_of(own, 1) + c_weights[3, place] * prev_of(own, 1)
            pushed.append(sources[place] + (along_x + along_y))
        return lines(pushed)

    z = lax.fori_loop(0, KC - 1, turn, lines(sources))
    c_ext[...] = times_one_hot(jnp.concatenate(z, axis=0).T[0:96], fold_c, 2).reshape(6, 16, 128)

    received(MID_V)

    def raise_mid(x, _):
        rows = c_ext[x, 5:13, :]
        for along in range(2):
            for parity in range(2):
                m_a[2 * x + along, parity] = m_y[2 * x + along, parity] + rows
        return 0

    lax.fori_loop(0, 6, raise_mid, 0, unroll=True)
    sweep(mid, m_src, m_a, m_b, (O - 3, O + 7))
    sweep(mid, m_src, m_b, m_a, (O - 2, O + 6))

    received(FINE_V)

    def raise_fine(x, _):
        for parity in range(2):
            m_fold[x, pl.ds(parity, 4, stride=2), :] = m_a[O - 2 + x, parity, 1:5]
        rows = m_fold[x]
        for along in range(2):
            for parity in range(2):
                for half in range(2):
                    at = (2 * x + along, parity, half)
                    f_a[at] = f_x[at] + rows
        return 0

    lax.fori_loop(0, 8, raise_fine, 0, unroll=True)
    sweep(fine, f_src, f_a, f_b, (O - 2, O + 10))
    sweep(fine, f_src, f_b, f_a, (O - 1, O + 9))

    together = one_hot((256, 256), lambda row, column: column == 2 * (row % 128) + row // 128)

    def in_order(field, result):
        def sort_back(x, _):
            for parity in range(2):
                for half in range(2):
                    f_rows[half, x, pl.ds(parity, 8, stride=2), :] = field[O + x, parity, half]
            return 0

        lax.fori_loop(0, 8, sort_back, 0, unroll=True)
        halves = [f_rows[half, :, O : O + 8, :].reshape(64, 128) for half in range(2)]
        result[...] = times_one_hot(jnp.concatenate(halves, axis=1), together, 3).reshape(8, 8, 256)

    in_order(f_a, pressure)

    def last(x, _):
        f_b[x] = row_residual(fine, f_src, f_a, x)
        return 0

    lax.fori_loop(O, O + 8, last, 0, unroll=True)
    in_order(f_b, residual)
    for at in (COARSE_F, MID_V):
        sent(at)


def publish(pressure, residual, pressure_h, residual_h, sem):
    copies = [
        pltpu.make_async_copy(pressure, pressure_h, sem.at[0]),
        pltpu.make_async_copy(residual, residual_h, sem.at[1]),
    ]
    for copy in copies:
        copy.start()
    for copy in copies:
        copy.wait()


def local(pressure_rhs, storage_fine, mobility_fine, storage_mid, mobility_mid, storage_coarse, mobility_coarse):
    count_x = lax.axis_size("gx")
    count_y = lax.axis_size("gy")
    f32 = jnp.float32
    fine = pltpu.VMEM((8 + 2 * O, 2, 2, 8, 128), f32)
    mid = pltpu.VMEM((4 + 2 * O, 2, 8, 128), f32)
    in_hbm = pl.BlockSpec(memory_space=pltpu.HBM)
    in_vmem = pl.BlockSpec(memory_space=pltpu.VMEM)
    arrays = (pressure_rhs, storage_fine, mobility_fine, storage_mid, mobility_mid, storage_coarse, mobility_coarse)
    result = pl.pallas_call(
        functools.partial(kernel, count_x, count_y),
        out_shape=(pltpu.VMEM(pressure_rhs.shape, f32),) * 2,
        in_specs=[in_hbm] * 7,
        out_specs=(in_vmem, in_vmem),
        scratch_shapes=[
            pltpu.VMEM((5, 8, 8, 256), f32),
            pltpu.VMEM((2, 40, 8, 128), f32),
            pltpu.VMEM((5, 8 + 2 * O, 2, 2, 8, 128), f32),
            *[fine] * 10,
            pltpu.VMEM((4, 4 + 2 * O, 2, 8, 128), f32),
            *[mid] * 11,
            pltpu.VMEM((8, 8, 128), f32),
            pltpu.VMEM((2, 8, 16, 128), f32),
            pltpu.VMEM((4, 8, 32, 64), f32),
            pltpu.VMEM((8, 32, 128), f32),
            pltpu.VMEM((6, 16, 128), f32),
            pltpu.VMEM((4, 8, 8, 128), f32),
            pltpu.VMEM((7, 64, 128), f32),
            pltpu.VMEM((97, 8, 128), f32),
            pltpu.VMEM((1024, 128), f32),
            pltpu.VMEM((4096, 128), f32),
            pltpu.VMEM((4, 2, 2, 64), f32),
            pltpu.SemaphoreType.DMA((16,)),
            pltpu.SemaphoreType.DMA((EXCHANGES,)),
            pltpu.SemaphoreType.DMA((EXCHANGES,)),
        ],
        compiler_params=pltpu.CompilerParams(
            collective_id=0, has_side_effects=True, vmem_limit_bytes=32 * 1024 * 1024
        ),
    )(*[pltpu.with_memory_space_constraint(array, pltpu.HBM) for array in arrays])
    out = jax.ShapeDtypeStruct(pressure_rhs.shape, f32)
    return pl.pallas_call(
        publish,
        out_shape=(out, out),
        in_specs=[in_vmem] * 2,
        out_specs=(in_hbm, in_hbm),
        scratch_shapes=[pltpu.SemaphoreType.DMA((2,))],
        compiler_params=pltpu.CompilerParams(vmem_limit_bytes=16 * 1024 * 1024),
    )(*result)


def solution(mesh):
    placed = (
        P("gx", "gy", None),
        P("gx", "gy", None),
        P(None, "gx", "gy", None),
        P("gx", "gy", None),
        P(None, "gx", "gy", None),
        P("gx", "gy", None),
        P(None, "gx", "gy", None),
    )
    return jax.shard_map(
        local,
        mesh=mesh,
        in_specs=placed,
        out_specs=(P("gx", "gy", None), P("gx", "gy", None)),
        check_vma=False,
    )
```

```python
import functools

import jax
import jax.numpy as jnp
from jax import lax
from jax.experimental import pallas as pl
from jax.experimental.pallas import tpu as pltpu
from jax.sharding import PartitionSpec as P

KC = 6
GROUP = 8
REACH = 4
DAMPING = 2.0 / 3.0

MESH = pl.DeviceIdType.MESH

O = 4
OP = 2
M0, M2, STORE, SOURCE, M1 = range(5)
OWN_C = slice(15, 17)
FINE_X, FINE_Y, COEF_X, COEF_Y, MID_IN, MID_F, FINE_V, COARSE_F, MID_V = range(9)
EXCHANGES = 9
NEIGHBOURS = ((1, 0), (-1, 0), (1, 1), (1, -1), (-1, 1), (-1, -1), (0, 1), (0, -1))


def reciprocal(values):
    guess = pl.reciprocal(values, approx=True)
    return guess * (2.0 - values * guess)


def harmonic(left, right):
    return 2.0 * left * right * reciprocal(left + right)


def next_of(values, axis):
    return pltpu.roll(values, values.shape[axis] - 1, axis)


def prev_of(values, axis):
    return pltpu.roll(values, 1, axis)


def next_paired(values, axis, pairs):
    first, second = lax.slice_in_dim(values, 0, 1, axis=axis), lax.slice_in_dim(values, 1, 2, axis=axis)
    return jnp.concatenate([second, next_of(first, pairs)], axis=axis)


def prev_paired(values, axis, pairs):
    first, second = lax.slice_in_dim(values, 0, 1, axis=axis), lax.slice_in_dim(values, 1, 2, axis=axis)
    return jnp.concatenate([prev_of(second, pairs), first], axis=axis)


def next_y(values):
    return next_paired(values, 0, values.ndim - 2)


def prev_y(values):
    return prev_paired(values, 0, values.ndim - 2)


def next_z(values):
    return next_paired(values, 1, 3) if values.ndim == 4 else next_of(values, 2)


def prev_z(values):
    return prev_paired(values, 1, 3) if values.ndim == 4 else prev_of(values, 2)


def one_hot(shape, test):
    row = lax.broadcasted_iota(jnp.int32, shape, 0)
    column = lax.broadcasted_iota(jnp.int32, shape, 1)
    return jnp.where(test(row, column), 1.0, 0.0).astype(jnp.bfloat16)


def pieces(values, count):
    parts = []
    for _ in range(count - 1):
        parts.append(values.astype(jnp.bfloat16))
        values = values - parts[-1].astype(jnp.float32)
    return parts + [values.astype(jnp.bfloat16)]


def times_one_hot(values, matrix, count):
    rows = values.shape[0]
    product = jnp.dot(jnp.concatenate(pieces(values, count), axis=0), matrix, preferred_element_type=jnp.float32)
    return total([product[at * rows : (at + 1) * rows] for at in range(count)])


def total(terms):
    while len(terms) > 1:
        pairs = [terms[i] + terms[i + 1] for i in range(0, len(terms) - 1, 2)]
        terms = pairs + terms[len(terms) - len(terms) % 2 :]
    return terms[0]


def source_span(step, first, n, width):
    return slice(first + n - width, first + n) if step > 0 else slice(first, first + (width if step < 0 else n))


def target_span(step, first, n, width):
    if step > 0:
        return slice(first - width, first)
    return slice(first + n, first + n + width) if step < 0 else slice(first, first + n)


def weights_x(level, mob, rows):
    wx = level[0]

    def body(x, _):
        wx[x] = harmonic(mob[0][x], mob[0][x + 1])
        return 0

    lax.fori_loop(*rows, body, 0, unroll=True)


def weights_yz(level, mob, rows, keep_y, keep_z):
    wx, wyu, wyd, wzu, wzd, diag, damp = level

    def body(x, _):
        second = mob[1][x]
        third = mob[2][x]
        up_y = harmonic(second, next_y(second)) * keep_y
        up_z = harmonic(third, next_z(third)) * keep_z
        wyu[x] = up_y
        wyd[x] = prev_y(up_y)
        wzu[x] = up_z
        wzd[x] = prev_z(up_z)
        return 0

    lax.fori_loop(*rows, body, 0, unroll=True)


def diagonals(level, store, rows):
    wx, wyu, wyd, wzu, wzd, diag, damp = level

    def body(x, _):
        all_of_it = store[x] + (wx[x] + wx[x - 1]) + (wyu[x] + wyd[x]) + (wzu[x] + wzd[x])
        diag[x] = all_of_it
        damp[x] = DAMPING * reciprocal(all_of_it)
        return 0

    lax.fori_loop(*rows, body, 0, unroll=True)


def row_residual(level, source, field, x):
    wx, wyu, wyd, wzu, wzd, diag, damp = level
    v = field[x]
    left = source[x] - diag[x] * v
    left = left + (wx[x] * field[x + 1] + wx[x - 1] * field[x - 1])
    left = left + (wyu[x] * next_y(v) + wyd[x] * prev_y(v))
    left = left + (wzu[x] * next_z(v) + wzd[x] * prev_z(v))
    return left


def sweep(level, source, field, result, rows):
    damp = level[6]

    def body(x, _):
        result[x] = field[x] + damp[x] * row_residual(level, source, field, x)
        return 0

    lax.fori_loop(rows[0], rows[1], body, 0, unroll=True)


def start_sweep(level, source, result, rows):
    damp = level[6]

    def body(x, _):
        result[x] = damp[x] * source[x]
        return 0

    lax.fori_loop(rows[0], rows[1], body, 0, unroll=True)


def kernel(
    count_x,
    count_y,
    rhs_h,
    store_f_h,
    mob_f_h,
    store_m_h,
    mob_m_h,
    store_c_h,
    mob_c_h,
    pressure,
    residual,
    f_stage,
    f_mixed,
    f_in,
    f_wx,
    f_wyu,
    f_wyd,
    f_wzu,
    f_wzd,
    f_diag,
    f_damp,
    f_a,
    f_b,
    f_x,
    m_in,
    m_src,
    m_wx,
    m_wyu,
    m_wyd,
    m_wzu,
    m_wzd,
    m_diag,
    m_damp,
    m_a,
    m_b,
    m_y,
    m_fold,
    f_rows,
    together,
    c_coef,
    c_src,
    c_ext,
    c_weights,
    c_bands,
    c_inverse,
    meter,
    spare,
    c_spare,
    local_sem,
    send_sem,
    recv_sem,
):
    gx = lax.axis_index("gx")
    gy = lax.axis_index("gy")

    def stepped(at, step, count):
        to = at + step
        if step > 0:
            return jnp.where(to >= count, to - count, to)
        return jnp.where(to < 0, to + count, to) if step < 0 else at

    along_gx = {step: stepped(gx, step, count_x) for step in (-1, 0, 1)}
    along_gy = {step: stepped(gy, step, count_y) for step in range(-REACH, REACH + 1)}

    def beside(sx, sy):
        return {"gx": along_gx[sx], "gy": along_gy[sy]}

    def ahead_of(sx):
        return gx < count_x - 1 if sx > 0 else gx > 0

    barrier = pltpu.get_barrier_semaphore()

    def greet(steps):
        for step in steps:
            pl.semaphore_signal(barrier, inc=1, device_id=beside(*step), device_id_type=MESH)

    for side in (1, -1):

        @pl.when(ahead_of(side))
        def _():
            greet([step for step in NEIGHBOURS if step[0] == side])

    straight = [(0, e) for e in range(-REACH, REACH + 1) if e != 0]
    greet(straight)
    partners = len(straight) + jnp.where(gx > 0, 3, 0) + jnp.where(gx < count_x - 1, 3, 0)

    c_coef[:, 6:8] = jnp.ones((4, 2, 32, 64), jnp.float32)
    c_src[6:8] = jnp.zeros((2, 32, 128), jnp.float32)

    locals_ = []

    def bring(source, target):
        copy = pltpu.make_async_copy(source, target, local_sem.at[len(locals_)])
        copy.start()
        locals_.append(copy)
        return copy

    def exchange(at, messages):
        sizes = []
        for source, _, _ in messages:
            rows = 1
            for size in source.shape[:-1]:
                rows = rows * size
            sizes.append(rows)
        rows_of[at] = rows_of.get(at, 0) + sum(sizes)

        def send(side):
            for source, target, step in messages:
                if step[0] == side:
                    pltpu.make_async_remote_copy(
                        src_ref=source,
                        dst_ref=target,
                        send_sem=send_sem.at[at],
                        recv_sem=recv_sem.at[at],
                        device_id=beside(*step),
                        device_id_type=MESH,
                    ).start()

        for side in (1, -1):
            rows = sum(size for size, message in zip(sizes, messages) if message[2][0] == side)
            if rows == 0:
                continue
            first = spent[0]
            spent[0] += rows

            @pl.when(ahead_of(side))
            def _():
                send(side)

            @pl.when(jnp.logical_not(ahead_of(side)))
            def _():
                if at == COEF_X:
                    pltpu.make_async_copy(c_coef.at[:, 2:4, OWN_C, :], c_spare, send_sem.at[at]).start()
                else:
                    spare_to = spare.at[first : first + rows, :]
                    pltpu.make_async_copy(meter.at[0:rows, :], spare_to, send_sem.at[at]).start()

            @pl.when(jnp.logical_not(ahead_of(-side)))
            def _():
                for source, target, step in messages:
                    if step[0] == side:
                        pltpu.make_async_copy(source, target, recv_sem.at[at]).start()

        send(0)

    spent = [0]
    rows_of = {}

    def all_of(at):
        if at == COEF_X:
            return c_coef.at[:, 0:4, 0:2, :]
        if at == COEF_Y:
            return c_coef.at[:, 0:6, 0:16, :]
        return meter.at[0 : rows_of[at], :]

    def received(at):
        pltpu.make_async_copy(all_of(at), all_of(at), recv_sem.at[at]).wait()

    def sent(at):
        pltpu.make_async_copy(all_of(at), all_of(at), send_sem.at[at]).wait()

    own8, pairs8 = slice(O, O + 8), slice(OP, OP + 4)
    own4, pairs4 = slice(O, O + 4), slice(OP, OP + 2)
    fine_in = [
        bring(mob_f_h, f_stage.at[0:3]),
        bring(store_f_h, f_stage.at[3]),
        bring(rhs_h, f_stage.at[4]),
    ]
    coarse_in = [
        bring(store_c_h, c_coef.at[0, 2:4, OWN_C, :]),
        bring(mob_c_h, c_coef.at[1:4, 2:4, OWN_C, :]),
    ]
    mid_in = []
    for y in range(4):
        parity, pair = y % 2, OP + y // 2
        mid_in.append(bring(mob_m_h.at[:, :, y, :], m_in.at[0:3, own4, parity, pair, :]))
        mid_in.append(bring(store_m_h.at[:, y, :], m_in.at[3, own4, parity, pair, :]))
    f_src = f_in.at[SOURCE]

    def spans(sx, sy, n, wide_x, wide_y):
        return (
            source_span(sx, O, n, wide_x),
            source_span(sy, OP, n // 2, wide_y),
            target_span(sx, O, n, wide_x),
            target_span(sy, OP, n // 2, wide_y),
        )

    faces_x = [step for step in NEIGHBOURS if step[1] == 0]
    faces_y = [step for step in NEIGHBOURS if step[0] == 0]
    corners = [step for step in NEIGHBOURS if step[0] != 0 and step[1] != 0]

    apart = one_hot((256, 256), lambda row, column: row == 2 * (column % 128) + column // 128)
    for copy in fine_in:
        copy.wait()
    sorted_z = times_one_hot(f_stage[...].reshape(320, 256), apart, 2)
    for half in range(2):
        f_mixed[half] = sorted_z[:, 128 * half : 128 * half + 128].reshape(40, 8, 128)

    def sort_y(x, _):
        for at, to in enumerate((M0, M1, M2, STORE, SOURCE)):
            for parity in range(2):
                for half in range(2):
                    rows = f_mixed[half, 8 * at + x, pl.ds(parity, 4, stride=2), :]
                    f_in[to, O + x, parity, half, pairs8] = rows
        return 0

    lax.fori_loop(0, 8, sort_y, 0, unroll=True)
    pl.semaphore_wait(barrier, partners)

    def part(first, last, step, wide_x, wide_y):
        fields = slice(first, last + 1)
        ax, ay, bx, by = spans(*step, 8, wide_x, wide_y)
        return (f_in.at[fields, ax, :, :, ay, :], f_in.at[fields, bx, :, :, by, :], step)

    for copy in coarse_in:
        copy.wait()
    exchange(
        COEF_X,
        [
            (c_coef.at[:, 2:4, OWN_C, :], c_coef.at[:, 2 - 2 * sx : 4 - 2 * sx, OWN_C, :], (sx, sy))
            for sx, sy in faces_x
        ],
    )

    messages = []
    for step in faces_x:
        messages += [part(M0, M0, step, 3, 1), part(M2, M1, step, 2, 1)]
    for step in corners:
        messages += [part(M0, M0, step, 2, 1), part(M1, M1, step, 2, 1), part(M2, SOURCE, step, 1, 1)]
    exchange(FINE_X, messages)
    messages = []
    for step in faces_y:
        messages += [part(M0, SOURCE, step, 1, 1), part(M1, M1, step, 1, 2)]
    exchange(FINE_Y, messages)

    one = jnp.float32(1.0)
    nil = jnp.float32(0.0)
    keep_x = (jnp.where(gx == 0, nil, one), jnp.where(gx == count_x - 1, nil, one))

    def keep_yz(own, shape):
        def index(axis):
            return lax.broadcasted_iota(jnp.int32, shape, axis)

        parity, pair, lane = index(0), index(len(shape) - 2), index(len(shape) - 1)
        end = jnp.where(gy == 0, OP - 1, -1)
        other = jnp.where(gy == count_y - 1, OP + own // 2 - 1, -1)
        keep_y = jnp.where((parity == 1) & ((pair == end) | (pair == other)), 0.0, 1.0)
        last_z = (lane == 127) if len(shape) == 3 else (lane == 127) & (index(1) == 1)
        return keep_y, jnp.where(last_z, 0.0, 1.0)

    together[...] = one_hot((256, 256), lambda row, column: column == 2 * (row % 128) + row // 128)
    fold_c = one_hot((64, 128), lambda row, column: row // 8 + 8 * (row % 8) == column // 2)

    fine = (f_wx, f_wyu, f_wyd, f_wzu, f_wzd, f_diag, f_damp)
    f_mob = (f_in.at[M0], f_in.at[M1], f_in.at[M2])
    f_store = f_in.at[STORE]
    keep_y, keep_z = keep_yz(8, (2, 2, 8, 128))
    received(FINE_Y)
    weights_yz(fine, f_mob, (O, O + 8), keep_y, keep_z)
    weights_x(fine, f_mob, (O, O + 7))
    diagonals(fine, f_store, (O + 1, O + 7))
    start_sweep(fine, f_src, f_a, (O + 1, O + 7))
    for copy in mid_in:
        copy.wait()
    messages = []
    for step in NEIGHBOURS:
        ax, ay, bx, by = spans(*step, 4, 3 if step in corners else 4, 2)
        messages.append((m_in.at[:, ax, :, ay, :], m_in.at[:, bx, :, by, :], step))
    exchange(MID_IN, messages)

    received(COEF_X)
    messages = []
    for step in straight:
        target = c_coef.at[:, 0:6, OWN_C.start - 2 * step[1] : OWN_C.stop - 2 * step[1], :]
        messages.append((c_coef.at[:, 0:6, OWN_C, :], target, step))
    exchange(COEF_Y, messages)
    received(FINE_X)
    for rows in ((O - 3, O), (O + 7, O + 10)):
        weights_x(fine, f_mob, rows)
    f_wx[O - 1] = f_wx[O - 1] * keep_x[0]
    f_wx[O + 7] = f_wx[O + 7] * keep_x[1]
    for rows in ((O - 2, O), (O + 8, O + 10)):
        weights_yz(fine, f_mob, rows, keep_y, keep_z)
    for rows in ((O - 2, O + 1), (O + 7, O + 10)):
        diagonals(fine, f_store, rows)
        start_sweep(fine, f_src, f_a, rows)
    sweep(fine, f_src, f_a, f_b, (O - 1, O + 9))

    def folded(x, _):
        both = row_residual(fine, f_src, f_b, O + 2 * x) + row_residual(fine, f_src, f_b, O + 2 * x + 1)
        m_fold[x] = (both[0, 0] + both[0, 1]) + (both[1, 0] + both[1, 1])
        for parity in range(2):
            m_src[O + x, parity, pairs4] = m_fold[x, pl.ds(OP + parity, 2, stride=2), :]
        return 0

    lax.fori_loop(0, 4, folded, 0, unroll=True)
    messages = []
    for step in NEIGHBOURS:
        ax, ay, bx, by = spans(*step, 4, 2 if step in corners else 3, 1 if step in corners else 2)
        messages.append((m_src.at[ax, :, ay, :], m_src.at[bx, :, by, :], step))
    exchange(MID_F, messages)

    def keep_fine(x, _):
        f_x[x, :, :, pairs8] = f_b[x, :, :, pairs8]
        return 0

    lax.fori_loop(O, O + 8, keep_fine, 0, unroll=True)
    messages = []
    for step in NEIGHBOURS:
        ax, ay, bx, by = spans(*step, 8, 2 if step in corners else 3, 1 if step in corners else 2)
        messages.append((f_x.at[ax, :, :, ay, :], f_x.at[bx, :, :, by, :], step))
    exchange(FINE_V, messages)

    mid = (m_wx, m_wyu, m_wyd, m_wzu, m_wzd, m_diag, m_damp)
    m_mob = (m_in.at[0], m_in.at[1], m_in.at[2])
    keep_y, keep_z = keep_yz(4, (2, 8, 128))
    received(MID_IN)
    weights_x(mid, m_mob, (O - 4, O + 7))
    m_wx[O - 1] = m_wx[O - 1] * keep_x[0]
    m_wx[O + 3] = m_wx[O + 3] * keep_x[1]
    weights_yz(mid, m_mob, (O - 3, O + 7), keep_y, keep_z)
    diagonals(mid, m_in.at[3], (O - 3, O + 7))

    received(COEF_Y)
    coef = [c_coef[k, :, 8:24, :].reshape(128, 64).T for k in range(4)]
    second_prev = c_coef[2, :, 7:23, :].reshape(128, 64).T
    second_next = c_coef[2, :, 9:25, :].reshape(128, 64).T
    column = lax.broadcasted_iota(jnp.int32, (64, 128), 1)
    level_row = lax.broadcasted_iota(jnp.int32, (64, 128), 0)
    cells = 2 * count_y
    cell = 2 * gy + lax.rem(column, 16) + (cells - 7)
    block = 2 * GROUP
    offset = 4 + cells - (cells // block) * block
    shut_up = (lax.rem(cell + 1 - offset + 2 * block, block) == 0) | (lax.rem(cell + 1, cells) == 0)
    shut_down = (lax.rem(cell - offset + 2 * block, block) == 0) | (lax.rem(cell, cells) == 0)
    up_x = jnp.where(lax.rem(column, 32) < 16, harmonic(coef[1], pltpu.roll(coef[1], 112, 1)), 0.0)
    down_x = pltpu.roll(up_x, 16, 1)
    up_y = jnp.where(shut_up, 0.0, harmonic(coef[2], second_next))
    down_y = jnp.where(shut_down, 0.0, harmonic(second_prev, coef[2]))
    up_z = jnp.where(level_row == 63, 0.0, harmonic(coef[3], next_of(coef[3], 0)))
    down_z = prev_of(up_z, 0)
    main = coef[0] + (up_x + down_x) + (up_y + down_y) + (up_z + down_z)
    for at, band in enumerate((up_x, down_x, up_y, down_y, -down_z, main, -up_z)):
        c_bands[at] = band

    for at in (FINE_X, FINE_Y, COEF_X, COEF_Y, MID_IN):
        sent(at)

    received(MID_F)
    start_sweep(mid, m_src, m_a, (O - 2, O + 6))
    sweep(mid, m_src, m_a, m_b, (O - 1, O + 5))
    for ix in range(2):
        fold = row_residual(mid, m_src, m_b, O + 2 * ix) + row_residual(mid, m_src, m_b, O + 2 * ix + 1)
        c_src[2 + ix, OWN_C, :] = (fold[0] + fold[1])[pairs4]
    messages = []
    for e in sorted(range(-REACH, REACH + 1), key=lambda e: -abs(e)):
        for g in (1, -1, 0):
            if (g, e) != (0, 0):
                target = c_src.at[2 - 2 * g : 4 - 2 * g, OWN_C.start - 2 * e : OWN_C.stop - 2 * e, :]
                messages.append((c_src.at[2:4, OWN_C, :], target, (g, e)))
    exchange(COARSE_F, messages)

    def keep_mid(x, _):
        m_y[x, :, pairs4] = m_b[x, :, pairs4]
        return 0

    lax.fori_loop(O, O + 4, keep_mid, 0, unroll=True)
    messages = []
    for step in NEIGHBOURS:
        ax, ay, bx, by = spans(*step, 4, 3 if step in corners else 4, 2)
        messages.append((m_y.at[ax, :, ay, :], m_y.at[bx, :, by, :], step))
    exchange(MID_V, messages)

    def registers(at):
        return [c_bands[at, pl.ds(place, 8, stride=8), :] for place in range(8)]

    for at in range(4):
        for place, values in enumerate(registers(at)):
            c_weights[at, place] = values
    low, main, high = (registers(at) for at in (4, 5, 6))
    ahead, back = [reciprocal(main[0])], {6: reciprocal(main[6])}
    upto, onfrom = [main[0]], {6: main[6]}
    for i in range(1, 7):
        upto.append(main[i] - low[i] * high[i - 1] * ahead[i - 1])
        ahead.append(reciprocal(upto[i]))
        j = 6 - i
        onfrom[j] = main[j] - high[j] * low[j + 1] * back[j + 1]
        back[j] = reciprocal(onfrom[j])
    rise = [-high[i] * ahead[i] for i in range(7)]
    fall = [-low[i] * back[i] for i in range(7)]
    inverse = {}
    for j in range(7):
        inverse[j, j] = reciprocal(upto[j] + onfrom[j] - main[j])
        for i in range(j - 1, -1, -1):
            inverse[i, j] = rise[i] * inverse[i + 1, j]
        for i in range(j + 1, 7):
            inverse[i, j] = fall[i] * inverse[i - 1, j]
    from_last = [inverse[i, 0] * low[0] for i in range(7)]
    from_own = [inverse[i, 6] * high[6] for i in range(7)]

    def turned(values, by):
        return pltpu.roll(values, by % 8, 0) if by % 8 else values

    face_main = main[7] - low[7] * from_own[6] - high[7] * turned(from_last[0], -1)
    face_low = -low[7] * from_last[6]
    face_high = -high[7] * turned(from_own[0], -1)
    spread_by = {0: jnp.ones((8, 128), jnp.float32)}
    for far in (1, 2, 4):
        over = reciprocal(face_main)
        alpha = -face_low * turned(over, far)
        gamma = -face_high * turned(over, -far)
        face_main = face_main + alpha * turned(face_high, far) + gamma * turned(face_low, -far)
        face_low, face_high = alpha * turned(face_low, far), gamma * turned(face_high, -far)
        wider = dict(spread_by)
        for by, values in spread_by.items():
            for step, factor in ((far, alpha), (-far, gamma)):
                term = factor * turned(values, step)
                key = (by + step) % 8
                wider[key] = wider[key] + term if key in wider else term
        spread_by = wider
    over = reciprocal(face_main)
    own_by = [over * spread_by[by] for by in range(8)]
    next_by = [own_by[(by + 1) % 8] * turned(high[7], by + 1) for by in range(8)]
    for i in range(7):
        for j in range(7):
            c_inverse[7 * i + j] = inverse[i, j]
        c_inverse[49 + i] = from_last[i]
        c_inverse[56 + i] = from_own[i]
    for by in range(8):
        c_inverse[64 + by] = own_by[by]
        c_inverse[72 + by] = next_by[by]
        c_inverse[80 + by] = turned(own_by[by - 1], 1)
        c_inverse[88 + by] = turned(next_by[by - 1], 1)
    c_inverse[63] = low[7]

    def lines(values):
        inner = [total([c_inverse[7 * i + j] * values[j] for j in range(7)]) for i in range(7)]
        face = values[7] - c_inverse[63] * inner[6]
        faces = [turned(face, by) for by in range(8)]
        firsts = [turned(inner[0], by) for by in range(8)]

        def interface(at):
            terms = [c_inverse[at + by] * faces[by] for by in range(8)]
            return total(terms) - total([c_inverse[at + 8 + by] * firsts[by] for by in range(8)])

        here, before = interface(64), interface(80)
        return tuple(inner[i] - (c_inverse[49 + i] * before + c_inverse[56 + i] * here) for i in range(7)) + (here,)

    for at in (MID_F, FINE_V):
        sent(at)

    received(COARSE_F)
    source = lax.dot_general(
        jnp.concatenate([fold_c] * 2, axis=1),
        jnp.concatenate(pieces(c_src[:, 8:24, :].reshape(128, 128), 2), axis=1),
        (((1,), (1,)), ((), ())),
        preferred_element_type=jnp.float32,
    )
    sources = [source[8 * place : 8 * place + 8] for place in range(8)]

    def turn(_, z):
        pushed = []
        for place in range(8):
            own = z[place]
            along_x = c_weights[0, place] * pltpu.roll(own, 112, 1) + c_weights[1, place] * pltpu.roll(own, 16, 1)
            along_y = c_weights[2, place] * next_of(own, 1) + c_weights[3, place] * prev_of(own, 1)
            pushed.append(sources[place] + (along_x + along_y))
        return lines(pushed)

    z = lax.fori_loop(0, KC - 1, turn, lines(sources))
    c_ext[...] = times_one_hot(jnp.concatenate(z, axis=0).T[0:96], fold_c, 2).reshape(6, 16, 128)

    received(MID_V)

    def raise_mid(x, _):
        rows = c_ext[x, 5:13, :]
        for along in range(2):
            for parity in range(2):
                m_a[2 * x + along, parity] = m_y[2 * x + along, parity] + rows
        return 0

    lax.fori_loop(0, 6, raise_mid, 0, unroll=True)
    sweep(mid, m_src, m_a, m_b, (O - 3, O + 7))
    sweep(mid, m_src, m_b, m_a, (O - 2, O + 6))

    received(FINE_V)

    def raise_fine(x, _):
        for parity in range(2):
            m_fold[x, pl.ds(parity, 4, stride=2), :] = m_a[O - 2 + x, parity, 1:5]
        rows = m_fold[x]
        for along in range(2):
            for parity in range(2):
                for half in range(2):
                    at = (2 * x + along, parity, half)
                    f_a[at] = f_x[at] + rows
        return 0

    lax.fori_loop(0, 8, raise_fine, 0, unroll=True)
    sweep(fine, f_src, f_a, f_b, (O - 2, O + 10))
    sweep(fine, f_src, f_b, f_a, (O - 1, O + 9))


    def in_order(field, result):
        def sort_back(x, _):
            for parity in range(2):
                for half in range(2):
                    f_rows[half, x, pl.ds(parity, 8, stride=2), :] = field[O + x, parity, half]
            return 0

        lax.fori_loop(0, 8, sort_back, 0, unroll=True)
        halves = [f_rows[half, :, O : O + 8, :].reshape(64, 128) for half in range(2)]
        result[...] = times_one_hot(jnp.concatenate(halves, axis=1), together[...], 2).reshape(8, 8, 256)

    in_order(f_a, pressure)

    def last(x, _):
        f_b[x] = row_residual(fine, f_src, f_a, x)
        return 0

    lax.fori_loop(O, O + 8, last, 0, unroll=True)
    in_order(f_b, residual)
    for at in (COARSE_F, MID_V):
        sent(at)


def publish(pressure, residual, pressure_h, residual_h, sem):
    copies = [
        pltpu.make_async_copy(pressure, pressure_h, sem.at[0]),
        pltpu.make_async_copy(residual, residual_h, sem.at[1]),
    ]
    for copy in copies:
        copy.start()
    for copy in copies:
        copy.wait()


def local(pressure_rhs, storage_fine, mobility_fine, storage_mid, mobility_mid, storage_coarse, mobility_coarse):
    count_x = lax.axis_size("gx")
    count_y = lax.axis_size("gy")
    f32 = jnp.float32
    fine = pltpu.VMEM((8 + 2 * O, 2, 2, 8, 128), f32)
    mid = pltpu.VMEM((4 + 2 * O, 2, 8, 128), f32)
    in_hbm = pl.BlockSpec(memory_space=pltpu.HBM)
    in_vmem = pl.BlockSpec(memory_space=pltpu.VMEM)
    arrays = (pressure_rhs, storage_fine, mobility_fine, storage_mid, mobility_mid, storage_coarse, mobility_coarse)
    result = pl.pallas_call(
        functools.partial(kernel, count_x, count_y),
        out_shape=(pltpu.VMEM(pressure_rhs.shape, f32),) * 2,
        in_specs=[in_hbm] * 7,
        out_specs=(in_vmem, in_vmem),
        scratch_shapes=[
            pltpu.VMEM((5, 8, 8, 256), f32),
            pltpu.VMEM((2, 40, 8, 128), f32),
            pltpu.VMEM((5, 8 + 2 * O, 2, 2, 8, 128), f32),
            *[fine] * 10,
            pltpu.VMEM((4, 4 + 2 * O, 2, 8, 128), f32),
            *[mid] * 11,
            pltpu.VMEM((8, 8, 128), f32),
            pltpu.VMEM((2, 8, 16, 128), f32),
            pltpu.VMEM((256, 256), jnp.bfloat16),
            pltpu.VMEM((4, 8, 32, 64), f32),
            pltpu.VMEM((8, 32, 128), f32),
            pltpu.VMEM((6, 16, 128), f32),
            pltpu.VMEM((4, 8, 8, 128), f32),
            pltpu.VMEM((7, 64, 128), f32),
            pltpu.VMEM((97, 8, 128), f32),
            pltpu.VMEM((1024, 128), f32),
            pltpu.VMEM((4096, 128), f32),
            pltpu.VMEM((4, 2, 2, 64), f32),
            pltpu.SemaphoreType.DMA((16,)),
            pltpu.SemaphoreType.DMA((EXCHANGES,)),
            pltpu.SemaphoreType.DMA((EXCHANGES,)),
        ],
        compiler_params=pltpu.CompilerParams(
            collective_id=0, has_side_effects=True, vmem_limit_bytes=32 * 1024 * 1024
        ),
    )(*[pltpu.with_memory_space_constraint(array, pltpu.HBM) for array in arrays])
    out = jax.ShapeDtypeStruct(pressure_rhs.shape, f32)
    return pl.pallas_call(
        publish,
        out_shape=(out, out),
        in_specs=[in_vmem] * 2,
        out_specs=(in_hbm, in_hbm),
        scratch_shapes=[pltpu.SemaphoreType.DMA((2,))],
        compiler_params=pltpu.CompilerParams(vmem_limit_bytes=16 * 1024 * 1024),
    )(*result)


def solution(mesh):
    placed = (
        P("gx", "gy", None),
        P("gx", "gy", None),
        P(None, "gx", "gy", None),
        P("gx", "gy", None),
        P(None, "gx", "gy", None),
        P("gx", "gy", None),
        P(None, "gx", "gy", None),
    )
    return jax.shard_map(
        local,
        mesh=mesh,
        in_specs=placed,
        out_specs=(P("gx", "gy", None), P("gx", "gy", None)),
        check_vma=False,
    )
```

```python
import functools

import jax
import jax.numpy as jnp
from jax import lax
from jax.experimental import pallas as pl
from jax.experimental.pallas import tpu as pltpu
from jax.sharding import PartitionSpec as P

KC = 6
GROUP = 8
REACH = 4
DAMPING = 2.0 / 3.0

MESH = pl.DeviceIdType.MESH

O = 4
OP = 2
M0, M2, STORE, SOURCE, M1 = range(5)
OWN_C = slice(15, 17)
FINE_X, FINE_Y, COEF_X, COEF_Y, MID_IN, MID_F, FINE_V, COARSE_F, MID_V = range(9)
EXCHANGES = 9
NEIGHBOURS = ((1, 0), (-1, 0), (1, 1), (1, -1), (-1, 1), (-1, -1), (0, 1), (0, -1))


def reciprocal(values):
    guess = pl.reciprocal(values, approx=True)
    return guess * (2.0 - values * guess)


def harmonic(left, right):
    return 2.0 * left * right * reciprocal(left + right)


def next_of(values, axis):
    return pltpu.roll(values, values.shape[axis] - 1, axis)


def prev_of(values, axis):
    return pltpu.roll(values, 1, axis)


def next_paired(values, axis, pairs):
    first, second = lax.slice_in_dim(values, 0, 1, axis=axis), lax.slice_in_dim(values, 1, 2, axis=axis)
    return jnp.concatenate([second, next_of(first, pairs)], axis=axis)


def prev_paired(values, axis, pairs):
    first, second = lax.slice_in_dim(values, 0, 1, axis=axis), lax.slice_in_dim(values, 1, 2, axis=axis)
    return jnp.concatenate([prev_of(second, pairs), first], axis=axis)


def next_y(values):
    return next_paired(values, 0, values.ndim - 2)


def prev_y(values):
    return prev_paired(values, 0, values.ndim - 2)


def next_z(values):
    return next_paired(values, 1, 3) if values.ndim == 4 else next_of(values, 2)


def prev_z(values):
    return prev_paired(values, 1, 3) if values.ndim == 4 else prev_of(values, 2)


def one_hot(shape, test):
    row = lax.broadcasted_iota(jnp.int32, shape, 0)
    column = lax.broadcasted_iota(jnp.int32, shape, 1)
    return jnp.where(test(row, column), 1.0, 0.0).astype(jnp.bfloat16)


def pieces(values, count):
    parts = []
    for _ in range(count - 1):
        parts.append(values.astype(jnp.bfloat16))
        values = values - parts[-1].astype(jnp.float32)
    return parts + [values.astype(jnp.bfloat16)]


def times_one_hot(values, matrix, count):
    rows = values.shape[0]
    product = jnp.dot(jnp.concatenate(pieces(values, count), axis=0), matrix, preferred_element_type=jnp.float32)
    return total([product[at * rows : (at + 1) * rows] for at in range(count)])


def total(terms):
    while len(terms) > 1:
        pairs = [terms[i] + terms[i + 1] for i in range(0, len(terms) - 1, 2)]
        terms = pairs + terms[len(terms) - len(terms) % 2 :]
    return terms[0]


def source_span(step, first, n, width):
    return slice(first + n - width, first + n) if step > 0 else slice(first, first + (width if step < 0 else n))


def target_span(step, first, n, width):
    if step > 0:
        return slice(first - width, first)
    return slice(first + n, first + n + width) if step < 0 else slice(first, first + n)


def weights_x(level, mob, rows):
    wx = level[0]

    def body(x, _):
        wx[x] = harmonic(mob[0][x], mob[0][x + 1])
        return 0

    lax.fori_loop(*rows, body, 0, unroll=True)


def weights_yz(level, mob, rows, keep_y, keep_z):
    wx, wyu, wyd, wzu, wzd, diag, damp = level

    def body(x, _):
        second = mob[1][x]
        third = mob[2][x]
        up_y = harmonic(second, next_y(second)) * keep_y
        up_z = harmonic(third, next_z(third)) * keep_z
        wyu[x] = up_y
        wyd[x] = prev_y(up_y)
        wzu[x] = up_z
        wzd[x] = prev_z(up_z)
        return 0

    lax.fori_loop(*rows, body, 0, unroll=True)


def diagonals(level, store, rows):
    wx, wyu, wyd, wzu, wzd, diag, damp = level

    def body(x, _):
        all_of_it = store[x] + (wx[x] + wx[x - 1]) + (wyu[x] + wyd[x]) + (wzu[x] + wzd[x])
        diag[x] = all_of_it
        damp[x] = DAMPING * reciprocal(all_of_it)
        return 0

    lax.fori_loop(*rows, body, 0, unroll=True)


def row_residual(level, source, field, x):
    wx, wyu, wyd, wzu, wzd, diag, damp = level
    v = field[x]
    left = source[x] - diag[x] * v
    left = left + (wx[x] * field[x + 1] + wx[x - 1] * field[x - 1])
    left = left + (wyu[x] * next_y(v) + wyd[x] * prev_y(v))
    left = left + (wzu[x] * next_z(v) + wzd[x] * prev_z(v))
    return left


def sweep(level, source, field, result, rows):
    damp = level[6]

    def body(x, _):
        result[x] = field[x] + damp[x] * row_residual(level, source, field, x)
        return 0

    lax.fori_loop(rows[0], rows[1], body, 0, unroll=True)


def start_sweep(level, source, result, rows):
    damp = level[6]

    def body(x, _):
        result[x] = damp[x] * source[x]
        return 0

    lax.fori_loop(rows[0], rows[1], body, 0, unroll=True)


def kernel(
    count_x,
    count_y,
    rhs_h,
    store_f_h,
    mob_f_h,
    store_m_h,
    mob_m_h,
    store_c_h,
    mob_c_h,
    pressure,
    residual,
    f_stage,
    f_mixed,
    f_in,
    f_wx,
    f_wyu,
    f_wyd,
    f_wzu,
    f_wzd,
    f_diag,
    f_damp,
    f_a,
    f_b,
    f_x,
    m_in,
    m_src,
    m_wx,
    m_wyu,
    m_wyd,
    m_wzu,
    m_wzd,
    m_diag,
    m_damp,
    m_a,
    m_b,
    m_y,
    m_fold,
    f_rows,
    together,
    c_coef,
    c_src,
    c_ext,
    c_weights,
    c_bands,
    c_inverse,
    meter,
    spare,
    c_spare,
    local_sem,
    send_sem,
    recv_sem,
):
    gx = lax.axis_index("gx")
    gy = lax.axis_index("gy")

    def stepped(at, step, count):
        to = at + step
        if step > 0:
            return jnp.where(to >= count, to - count, to)
        return jnp.where(to < 0, to + count, to) if step < 0 else at

    along_gx = {step: stepped(gx, step, count_x) for step in (-1, 0, 1)}
    along_gy = {step: stepped(gy, step, count_y) for step in range(-REACH, REACH + 1)}

    def beside(sx, sy):
        return {"gx": along_gx[sx], "gy": along_gy[sy]}

    def ahead_of(sx):
        return gx < count_x - 1 if sx > 0 else gx > 0

    barrier = pltpu.get_barrier_semaphore()

    def greet(steps):
        for step in steps:
            pl.semaphore_signal(barrier, inc=1, device_id=beside(*step), device_id_type=MESH)

    for side in (1, -1):

        @pl.when(ahead_of(side))
        def _():
            greet([step for step in NEIGHBOURS if step[0] == side])

    straight = [(0, e) for e in range(-REACH, REACH + 1) if e != 0]
    greet(straight)
    partners = len(straight) + jnp.where(gx > 0, 3, 0) + jnp.where(gx < count_x - 1, 3, 0)

    c_coef[:, 6:8] = jnp.ones((4, 2, 32, 64), jnp.float32)
    c_src[6:8] = jnp.zeros((2, 32, 128), jnp.float32)

    locals_ = []

    def bring(source, target):
        copy = pltpu.make_async_copy(source, target, local_sem.at[len(locals_)])
        copy.start()
        locals_.append(copy)
        return copy

    def exchange(at, messages):
        sizes = []
        for source, _, _ in messages:
            rows = 1
            for size in source.shape[:-1]:
                rows = rows * size
            sizes.append(rows)
        rows_of[at] = rows_of.get(at, 0) + sum(sizes)

        def send(side):
            for source, target, step in messages:
                if step[0] == side:
                    pltpu.make_async_remote_copy(
                        src_ref=source,
                        dst_ref=target,
                        send_sem=send_sem.at[at],
                        recv_sem=recv_sem.at[at],
                        device_id=beside(*step),
                        device_id_type=MESH,
                    ).start()

        for side in (1, -1):
            rows = sum(size for size, message in zip(sizes, messages) if message[2][0] == side)
            if rows == 0:
                continue
            first = spent[0]
            spent[0] += rows

            @pl.when(ahead_of(side))
            def _():
                send(side)

            @pl.when(jnp.logical_not(ahead_of(side)))
            def _():
                if at == COEF_X:
                    pltpu.make_async_copy(c_coef.at[:, 2:4, OWN_C, :], c_spare, send_sem.at[at]).start()
                else:
                    spare_to = spare.at[first : first + rows, :]
                    pltpu.make_async_copy(meter.at[0:rows, :], spare_to, send_sem.at[at]).start()

            @pl.when(jnp.logical_not(ahead_of(-side)))
            def _():
                for source, target, step in messages:
                    if step[0] == side:
                        pltpu.make_async_copy(source, target, recv_sem.at[at]).start()

        send(0)

    spent = [0]
    rows_of = {}

    def all_of(at):
        if at == COEF_X:
            return c_coef.at[:, 0:4, 0:2, :]
        if at == COEF_Y:
            return c_coef.at[:, 0:6, 0:16, :]
        return meter.at[0 : rows_of[at], :]

    def received(at):
        pltpu.make_async_copy(all_of(at), all_of(at), recv_sem.at[at]).wait()

    def sent(at):
        pltpu.make_async_copy(all_of(at), all_of(at), send_sem.at[at]).wait()

    own8, pairs8 = slice(O, O + 8), slice(OP, OP + 4)
    own4, pairs4 = slice(O, O + 4), slice(OP, OP + 2)
    fine_in = [
        bring(mob_f_h, f_stage.at[0:3]),
        bring(store_f_h, f_stage.at[3]),
        bring(rhs_h, f_stage.at[4]),
    ]
    coarse_in = [
        bring(store_c_h, c_coef.at[0, 2:4, OWN_C, :]),
        bring(mob_c_h, c_coef.at[1:4, 2:4, OWN_C, :]),
    ]
    mid_in = []
    for y in range(4):
        parity, pair = y % 2, OP + y // 2
        mid_in.append(bring(mob_m_h.at[:, :, y, :], m_in.at[0:3, own4, parity, pair, :]))
        mid_in.append(bring(store_m_h.at[:, y, :], m_in.at[3, own4, parity, pair, :]))
    f_src = f_in.at[SOURCE]

    def spans(sx, sy, n, wide_x, wide_y):
        return (
            source_span(sx, O, n, wide_x),
            source_span(sy, OP, n // 2, wide_y),
            target_span(sx, O, n, wide_x),
            target_span(sy, OP, n // 2, wide_y),
        )

    faces_x = [step for step in NEIGHBOURS if step[1] == 0]
    faces_y = [step for step in NEIGHBOURS if step[0] == 0]
    corners = [step for step in NEIGHBOURS if step[0] != 0 and step[1] != 0]

    apart = one_hot((256, 256), lambda row, column: row == 2 * (column % 128) + column // 128)
    for copy in fine_in:
        copy.wait()
    sorted_z = times_one_hot(f_stage[...].reshape(320, 256), apart, 2)
    for half in range(2):
        f_mixed[half] = sorted_z[:, 128 * half : 128 * half + 128].reshape(40, 8, 128)

    def sort_y(x, _):
        for at, to in enumerate((M0, M1, M2, STORE, SOURCE)):
            for parity in range(2):
                for half in range(2):
                    rows = f_mixed[half, 8 * at + x, pl.ds(parity, 4, stride=2), :]
                    f_in[to, O + x, parity, half, pairs8] = rows
        return 0

    lax.fori_loop(0, 8, sort_y, 0, unroll=True)
    pl.semaphore_wait(barrier, partners)

    def part(first, last, step, wide_x, wide_y, parity=slice(0, 2)):
        fields = slice(first, last + 1)
        ax, ay, bx, by = spans(*step, 8, wide_x, wide_y)
        return (f_in.at[fields, ax, parity, :, ay, :], f_in.at[fields, bx, parity, :, by, :], step)

    for copy in coarse_in:
        copy.wait()
    exchange(
        COEF_X,
        [
            (c_coef.at[:, 2:4, OWN_C, :], c_coef.at[:, 2 - 2 * sx : 4 - 2 * sx, OWN_C, :], (sx, sy))
            for sx, sy in faces_x
        ],
    )

    messages = []
    for step in faces_x:
        messages += [part(M0, M0, step, 3, 1), part(M2, M1, step, 2, 1)]
    for step in corners:
        nearest = slice(1, 2) if step[1] > 0 else slice(0, 1)
        messages += [part(M0, M0, step, 2, 1), part(M1, M1, step, 2, 1), part(M2, SOURCE, step, 1, 1, nearest)]
    exchange(FINE_X, messages)
    messages = []
    for step in faces_y:
        messages += [part(M0, SOURCE, step, 1, 1), part(M1, M1, step, 1, 2)]
    exchange(FINE_Y, messages)

    for copy in mid_in:
        copy.wait()
    messages = []
    for step in NEIGHBOURS:
        ax, ay, bx, by = spans(*step, 4, 3 if step in corners else 4, 2)
        messages.append((m_in.at[:, ax, :, ay, :], m_in.at[:, bx, :, by, :], step))
    exchange(MID_IN, messages)

    one = jnp.float32(1.0)
    nil = jnp.float32(0.0)
    keep_x = (jnp.where(gx == 0, nil, one), jnp.where(gx == count_x - 1, nil, one))

    def keep_yz(own, shape):
        def index(axis):
            return lax.broadcasted_iota(jnp.int32, shape, axis)

        parity, pair, lane = index(0), index(len(shape) - 2), index(len(shape) - 1)
        end = jnp.where(gy == 0, OP - 1, -1)
        other = jnp.where(gy == count_y - 1, OP + own // 2 - 1, -1)
        keep_y = jnp.where((parity == 1) & ((pair == end) | (pair == other)), 0.0, 1.0)
        last_z = (lane == 127) if len(shape) == 3 else (lane == 127) & (index(1) == 1)
        return keep_y, jnp.where(last_z, 0.0, 1.0)

    together[...] = one_hot((256, 256), lambda row, column: column == 2 * (row % 128) + row // 128)
    fold_c = one_hot((64, 128), lambda row, column: row // 8 + 8 * (row % 8) == column // 2)

    fine = (f_wx, f_wyu, f_wyd, f_wzu, f_wzd, f_diag, f_damp)
    f_mob = (f_in.at[M0], f_in.at[M1], f_in.at[M2])
    f_store = f_in.at[STORE]
    keep_y, keep_z = keep_yz(8, (2, 2, 8, 128))
    received(FINE_Y)
    weights_yz(fine, f_mob, (O, O + 8), keep_y, keep_z)
    weights_x(fine, f_mob, (O, O + 7))
    diagonals(fine, f_store, (O + 1, O + 7))
    start_sweep(fine, f_src, f_a, (O + 1, O + 7))
    received(COEF_X)
    messages = []
    for step in straight:
        target = c_coef.at[:, 0:6, OWN_C.start - 2 * step[1] : OWN_C.stop - 2 * step[1], :]
        messages.append((c_coef.at[:, 0:6, OWN_C, :], target, step))
    exchange(COEF_Y, messages)
    sweep(fine, f_src, f_a, f_b, (O + 2, O + 6))
    received(FINE_X)
    for rows in ((O - 3, O), (O + 7, O + 10)):
        weights_x(fine, f_mob, rows)
    f_wx[O - 1] = f_wx[O - 1] * keep_x[0]
    f_wx[O + 7] = f_wx[O + 7] * keep_x[1]
    for rows in ((O - 2, O), (O + 8, O + 10)):
        weights_yz(fine, f_mob, rows, keep_y, keep_z)
    for rows in ((O - 2, O + 1), (O + 7, O + 10)):
        diagonals(fine, f_store, rows)
        start_sweep(fine, f_src, f_a, rows)
    for rows in ((O - 1, O + 2), (O + 6, O + 9)):
        sweep(fine, f_src, f_a, f_b, rows)

    def folded(x, _):
        both = row_residual(fine, f_src, f_b, O + 2 * x) + row_residual(fine, f_src, f_b, O + 2 * x + 1)
        m_fold[x] = (both[0, 0] + both[0, 1]) + (both[1, 0] + both[1, 1])
        for parity in range(2):
            m_src[O + x, parity, pairs4] = m_fold[x, pl.ds(OP + parity, 2, stride=2), :]
        return 0

    lax.fori_loop(0, 4, folded, 0, unroll=True)
    messages = []
    for step in NEIGHBOURS:
        ax, ay, bx, by = spans(*step, 4, 2 if step in corners else 3, 1 if step in corners else 2)
        messages.append((m_src.at[ax, :, ay, :], m_src.at[bx, :, by, :], step))
    exchange(MID_F, messages)

    def keep_fine(x, _):
        f_x[x, :, :, pairs8] = f_b[x, :, :, pairs8]
        return 0

    lax.fori_loop(O, O + 8, keep_fine, 0, unroll=True)
    messages = []
    for step in NEIGHBOURS:
        ax, ay, bx, by = spans(*step, 8, 2 if step in corners else 3, 1 if step in corners else 2)
        messages.append((f_x.at[ax, :, :, ay, :], f_x.at[bx, :, :, by, :], step))
    exchange(FINE_V, messages)

    mid = (m_wx, m_wyu, m_wyd, m_wzu, m_wzd, m_diag, m_damp)
    m_mob = (m_in.at[0], m_in.at[1], m_in.at[2])
    keep_y, keep_z = keep_yz(4, (2, 8, 128))
    received(MID_IN)
    weights_x(mid, m_mob, (O - 4, O + 7))
    m_wx[O - 1] = m_wx[O - 1] * keep_x[0]
    m_wx[O + 3] = m_wx[O + 3] * keep_x[1]
    weights_yz(mid, m_mob, (O - 3, O + 7), keep_y, keep_z)
    diagonals(mid, m_in.at[3], (O - 3, O + 7))

    for at in (FINE_X, FINE_Y, COEF_X, MID_IN):
        sent(at)

    received(MID_F)
    start_sweep(mid, m_src, m_a, (O - 2, O + 6))
    sweep(mid, m_src, m_a, m_b, (O - 1, O + 5))
    for ix in range(2):
        fold = row_residual(mid, m_src, m_b, O + 2 * ix) + row_residual(mid, m_src, m_b, O + 2 * ix + 1)
        c_src[2 + ix, OWN_C, :] = (fold[0] + fold[1])[pairs4]
    messages = []
    for e in sorted(range(-REACH, REACH + 1), key=lambda e: -abs(e)):
        for g in (1, -1, 0):
            if (g, e) != (0, 0):
                target = c_src.at[2 - 2 * g : 4 - 2 * g, OWN_C.start - 2 * e : OWN_C.stop - 2 * e, :]
                messages.append((c_src.at[2:4, OWN_C, :], target, (g, e)))
    exchange(COARSE_F, messages)

    def keep_mid(x, _):
        m_y[x, :, pairs4] = m_b[x, :, pairs4]
        return 0

    lax.fori_loop(O, O + 4, keep_mid, 0, unroll=True)
    messages = []
    for step in NEIGHBOURS:
        ax, ay, bx, by = spans(*step, 4, 3 if step in corners else 4, 2)
        messages.append((m_y.at[ax, :, ay, :], m_y.at[bx, :, by, :], step))
    exchange(MID_V, messages)

    received(COEF_Y)
    coef = [c_coef[k, :, 8:24, :].reshape(128, 64).T for k in range(4)]
    second_prev = c_coef[2, :, 7:23, :].reshape(128, 64).T
    second_next = c_coef[2, :, 9:25, :].reshape(128, 64).T
    column = lax.broadcasted_iota(jnp.int32, (64, 128), 1)
    level_row = lax.broadcasted_iota(jnp.int32, (64, 128), 0)
    cells = 2 * count_y
    cell = 2 * gy + lax.rem(column, 16) + (cells - 7)
    block = 2 * GROUP
    offset = 4 + cells - (cells // block) * block
    shut_up = (lax.rem(cell + 1 - offset + 2 * block, block) == 0) | (lax.rem(cell + 1, cells) == 0)
    shut_down = (lax.rem(cell - offset + 2 * block, block) == 0) | (lax.rem(cell, cells) == 0)
    up_x = jnp.where(lax.rem(column, 32) < 16, harmonic(coef[1], pltpu.roll(coef[1], 112, 1)), 0.0)
    down_x = pltpu.roll(up_x, 16, 1)
    up_y = jnp.where(shut_up, 0.0, harmonic(coef[2], second_next))
    down_y = jnp.where(shut_down, 0.0, harmonic(second_prev, coef[2]))
    up_z = jnp.where(level_row == 63, 0.0, harmonic(coef[3], next_of(coef[3], 0)))
    down_z = prev_of(up_z, 0)
    main = coef[0] + (up_x + down_x) + (up_y + down_y) + (up_z + down_z)
    for at, band in enumerate((up_x, down_x, up_y, down_y, -down_z, main, -up_z)):
        c_bands[at] = band

    def registers(at):
        return [c_bands[at, pl.ds(place, 8, stride=8), :] for place in range(8)]

    for at in range(4):
        for place, values in enumerate(registers(at)):
            c_weights[at, place] = values
    low, main, high = (registers(at) for at in (4, 5, 6))
    ahead, back = [reciprocal(main[0])], {6: reciprocal(main[6])}
    upto, onfrom = [main[0]], {6: main[6]}
    for i in range(1, 7):
        upto.append(main[i] - low[i] * high[i - 1] * ahead[i - 1])
        ahead.append(reciprocal(upto[i]))
        j = 6 - i
        onfrom[j] = main[j] - high[j] * low[j + 1] * back[j + 1]
        back[j] = reciprocal(onfrom[j])
    rise = [-high[i] * ahead[i] for i in range(7)]
    fall = [-low[i] * back[i] for i in range(7)]
    inverse = {}
    for j in range(7):
        inverse[j, j] = reciprocal(upto[j] + onfrom[j] - main[j])
        for i in range(j - 1, -1, -1):
            inverse[i, j] = rise[i] * inverse[i + 1, j]
        for i in range(j + 1, 7):
            inverse[i, j] = fall[i] * inverse[i - 1, j]
    from_last = [inverse[i, 0] * low[0] for i in range(7)]
    from_own = [inverse[i, 6] * high[6] for i in range(7)]

    def turned(values, by):
        return pltpu.roll(values, by % 8, 0) if by % 8 else values

    face_main = main[7] - low[7] * from_own[6] - high[7] * turned(from_last[0], -1)
    face_low = -low[7] * from_last[6]
    face_high = -high[7] * turned(from_own[0], -1)
    spread_by = {0: jnp.ones((8, 128), jnp.float32)}
    for far in (1, 2, 4):
        over = reciprocal(face_main)
        alpha = -face_low * turned(over, far)
        gamma = -face_high * turned(over, -far)
        face_main = face_main + alpha * turned(face_high, far) + gamma * turned(face_low, -far)
        face_low, face_high = alpha * turned(face_low, far), gamma * turned(face_high, -far)
        wider = dict(spread_by)
        for by, values in spread_by.items():
            for step, factor in ((far, alpha), (-far, gamma)):
                term = factor * turned(values, step)
                key = (by + step) % 8
                wider[key] = wider[key] + term if key in wider else term
        spread_by = wider
    over = reciprocal(face_main)
    own_by = [over * spread_by[by] for by in range(8)]
    next_by = [own_by[(by + 1) % 8] * turned(high[7], by + 1) for by in range(8)]
    for i in range(7):
        for j in range(7):
            c_inverse[7 * i + j] = inverse[i, j]
        c_inverse[49 + i] = from_last[i]
        c_inverse[56 + i] = from_own[i]
    for by in range(8):
        c_inverse[64 + by] = own_by[by]
        c_inverse[72 + by] = next_by[by]
        c_inverse[80 + by] = turned(own_by[by - 1], 1)
        c_inverse[88 + by] = turned(next_by[by - 1], 1)
    c_inverse[63] = low[7]

    def lines(values):
        inner = [total([c_inverse[7 * i + j] * values[j] for j in range(7)]) for i in range(7)]
        face = values[7] - c_inverse[63] * inner[6]
        faces = [turned(face, by) for by in range(8)]
        firsts = [turned(inner[0], by) for by in range(8)]

        def interface(at):
            terms = [c_inverse[at + by] * faces[by] for by in range(8)]
            return total(terms) - total([c_inverse[at + 8 + by] * firsts[by] for by in range(8)])

        here, before = interface(64), interface(80)
        return tuple(inner[i] - (c_inverse[49 + i] * before + c_inverse[56 + i] * here) for i in range(7)) + (here,)

    for at in (COEF_Y, MID_F, FINE_V):
        sent(at)

    received(COARSE_F)
    source = lax.dot_general(
        jnp.concatenate([fold_c] * 2, axis=1),
        jnp.concatenate(pieces(c_src[:, 8:24, :].reshape(128, 128), 2), axis=1),
        (((1,), (1,)), ((), ())),
        preferred_element_type=jnp.float32,
    )
    sources = [source[8 * place : 8 * place + 8] for place in range(8)]

    def turn(_, z):
        pushed = []
        for place in range(8):
            own = z[place]
            along_x = c_weights[0, place] * pltpu.roll(own, 112, 1) + c_weights[1, place] * pltpu.roll(own, 16, 1)
            along_y = c_weights[2, place] * next_of(own, 1) + c_weights[3, place] * prev_of(own, 1)
            pushed.append(sources[place] + (along_x + along_y))
        return lines(pushed)

    z = lax.fori_loop(0, KC - 1, turn, lines(sources))
    c_ext[...] = times_one_hot(jnp.concatenate(z, axis=0).T[0:96], fold_c, 2).reshape(6, 16, 128)

    received(MID_V)

    def raise_mid(x, _):
        rows = c_ext[x, 5:13, :]
        for along in range(2):
            for parity in range(2):
                m_a[2 * x + along, parity] = m_y[2 * x + along, parity] + rows
        return 0

    lax.fori_loop(0, 6, raise_mid, 0, unroll=True)
    sweep(mid, m_src, m_a, m_b, (O - 3, O + 7))
    sweep(mid, m_src, m_b, m_a, (O - 2, O + 6))

    received(FINE_V)

    def raise_fine(x, _):
        for parity in range(2):
            m_fold[x, pl.ds(parity, 4, stride=2), :] = m_a[O - 2 + x, parity, 1:5]
        rows = m_fold[x]
        for along in range(2):
            for parity in range(2):
                for half in range(2):
                    at = (2 * x + along, parity, half)
                    f_a[at] = f_x[at] + rows
        return 0

    lax.fori_loop(0, 8, raise_fine, 0, unroll=True)
    sweep(fine, f_src, f_a, f_b, (O - 2, O + 10))
    sweep(fine, f_src, f_b, f_a, (O - 1, O + 9))


    def in_order(field, result):
        def sort_back(x, _):
            for parity in range(2):
                for half in range(2):
                    f_rows[half, x, pl.ds(parity, 8, stride=2), :] = field[O + x, parity, half]
            return 0

        lax.fori_loop(0, 8, sort_back, 0, unroll=True)
        halves = [f_rows[half, :, O : O + 8, :].reshape(64, 128) for half in range(2)]
        result[...] = times_one_hot(jnp.concatenate(halves, axis=1), together[...], 2).reshape(8, 8, 256)

    in_order(f_a, pressure)

    def last(x, _):
        f_b[x] = row_residual(fine, f_src, f_a, x)
        return 0

    lax.fori_loop(O, O + 8, last, 0, unroll=True)
    in_order(f_b, residual)
    for at in (COARSE_F, MID_V):
        sent(at)


def publish(pressure, residual, pressure_h, residual_h, sem):
    copies = [
        pltpu.make_async_copy(pressure, pressure_h, sem.at[0]),
        pltpu.make_async_copy(residual, residual_h, sem.at[1]),
    ]
    for copy in copies:
        copy.start()
    for copy in copies:
        copy.wait()


def local(pressure_rhs, storage_fine, mobility_fine, storage_mid, mobility_mid, storage_coarse, mobility_coarse):
    count_x = lax.axis_size("gx")
    count_y = lax.axis_size("gy")
    f32 = jnp.float32
    fine = pltpu.VMEM((8 + 2 * O, 2, 2, 8, 128), f32)
    mid = pltpu.VMEM((4 + 2 * O, 2, 8, 128), f32)
    in_hbm = pl.BlockSpec(memory_space=pltpu.HBM)
    in_vmem = pl.BlockSpec(memory_space=pltpu.VMEM)
    arrays = (pressure_rhs, storage_fine, mobility_fine, storage_mid, mobility_mid, storage_coarse, mobility_coarse)
    result = pl.pallas_call(
        functools.partial(kernel, count_x, count_y),
        out_shape=(pltpu.VMEM(pressure_rhs.shape, f32),) * 2,
        in_specs=[in_hbm] * 7,
        out_specs=(in_vmem, in_vmem),
        scratch_shapes=[
            pltpu.VMEM((5, 8, 8, 256), f32),
            pltpu.VMEM((2, 40, 8, 128), f32),
            pltpu.VMEM((5, 8 + 2 * O, 2, 2, 8, 128), f32),
            *[fine] * 10,
            pltpu.VMEM((4, 4 + 2 * O, 2, 8, 128), f32),
            *[mid] * 11,
            pltpu.VMEM((8, 8, 128), f32),
            pltpu.VMEM((2, 8, 16, 128), f32),
            pltpu.VMEM((256, 256), jnp.bfloat16),
            pltpu.VMEM((4, 8, 32, 64), f32),
            pltpu.VMEM((8, 32, 128), f32),
            pltpu.VMEM((6, 16, 128), f32),
            pltpu.VMEM((4, 8, 8, 128), f32),
            pltpu.VMEM((7, 64, 128), f32),
            pltpu.VMEM((97, 8, 128), f32),
            pltpu.VMEM((1024, 128), f32),
            pltpu.VMEM((4096, 128), f32),
            pltpu.VMEM((4, 2, 2, 64), f32),
            pltpu.SemaphoreType.DMA((16,)),
            pltpu.SemaphoreType.DMA((EXCHANGES,)),
            pltpu.SemaphoreType.DMA((EXCHANGES,)),
        ],
        compiler_params=pltpu.CompilerParams(
            collective_id=0, has_side_effects=True, vmem_limit_bytes=32 * 1024 * 1024
        ),
    )(*[pltpu.with_memory_space_constraint(array, pltpu.HBM) for array in arrays])
    out = jax.ShapeDtypeStruct(pressure_rhs.shape, f32)
    return pl.pallas_call(
        publish,
        out_shape=(out, out),
        in_specs=[in_vmem] * 2,
        out_specs=(in_hbm, in_hbm),
        scratch_shapes=[pltpu.SemaphoreType.DMA((2,))],
        compiler_params=pltpu.CompilerParams(vmem_limit_bytes=16 * 1024 * 1024),
    )(*result)


def solution(mesh):
    placed = (
        P("gx", "gy", None),
        P("gx", "gy", None),
        P(None, "gx", "gy", None),
        P("gx", "gy", None),
        P(None, "gx", "gy", None),
        P("gx", "gy", None),
        P(None, "gx", "gy", None),
    )
    return jax.shard_map(
        local,
        mesh=mesh,
        in_specs=placed,
        out_specs=(P("gx", "gy", None), P("gx", "gy", None)),
        check_vma=False,
    )
```

```python
import functools

import jax
import jax.numpy as jnp
from jax import lax
from jax.experimental import pallas as pl
from jax.experimental.pallas import tpu as pltpu
from jax.sharding import PartitionSpec as P

KC = 6
GROUP = 8
REACH = 4
DAMPING = 2.0 / 3.0

MESH = pl.DeviceIdType.MESH

O = 4
OP = 2
M0, M2, STORE, SOURCE, M1 = range(5)
OWN_C = slice(15, 17)
FINE_X, FINE_Y, COEF_X, COEF_Y, MID_IN, MID_F, FINE_V, COARSE_F, MID_V = range(9)
EXCHANGES = 9
NEIGHBOURS = ((1, 0), (-1, 0), (1, 1), (1, -1), (-1, 1), (-1, -1), (0, 1), (0, -1))


def reciprocal(values):
    guess = pl.reciprocal(values, approx=True)
    return guess * (2.0 - values * guess)


def harmonic(left, right):
    return 2.0 * left * right * reciprocal(left + right)


def next_of(values, axis):
    return pltpu.roll(values, values.shape[axis] - 1, axis)


def prev_of(values, axis):
    return pltpu.roll(values, 1, axis)


def next_paired(values, axis, pairs):
    first, second = lax.slice_in_dim(values, 0, 1, axis=axis), lax.slice_in_dim(values, 1, 2, axis=axis)
    return jnp.concatenate([second, next_of(first, pairs)], axis=axis)


def prev_paired(values, axis, pairs):
    first, second = lax.slice_in_dim(values, 0, 1, axis=axis), lax.slice_in_dim(values, 1, 2, axis=axis)
    return jnp.concatenate([prev_of(second, pairs), first], axis=axis)


def next_y(values):
    return next_paired(values, 1, values.ndim - 2)


def prev_y(values):
    return prev_paired(values, 1, values.ndim - 2)


def next_z(values):
    return next_paired(values, 2, 4) if values.ndim == 5 else next_of(values, 3)


def prev_z(values):
    return prev_paired(values, 2, 4) if values.ndim == 5 else prev_of(values, 3)


def blocks(level, rows):
    first, last = rows
    most = 4 if len(level[0].shape) == 5 else 6
    count = -(-(last - first) // most)
    edges = [first + (last - first) * at // count for at in range(count + 1)]
    return [slice(*pair) for pair in zip(edges[:-1], edges[1:])]


def moved(rows, by):
    return slice(rows.start + by, rows.stop + by)


def one_hot(shape, test):
    row = lax.broadcasted_iota(jnp.int32, shape, 0)
    column = lax.broadcasted_iota(jnp.int32, shape, 1)
    return jnp.where(test(row, column), 1.0, 0.0).astype(jnp.bfloat16)


def pieces(values, count):
    parts = []
    for _ in range(count - 1):
        parts.append(values.astype(jnp.bfloat16))
        values = values - parts[-1].astype(jnp.float32)
    return parts + [values.astype(jnp.bfloat16)]


def times_one_hot(values, matrix, count):
    rows = values.shape[0]
    product = jnp.dot(jnp.concatenate(pieces(values, count), axis=0), matrix, preferred_element_type=jnp.float32)
    return total([product[at * rows : (at + 1) * rows] for at in range(count)])


def total(terms):
    while len(terms) > 1:
        pairs = [terms[i] + terms[i + 1] for i in range(0, len(terms) - 1, 2)]
        terms = pairs + terms[len(terms) - len(terms) % 2 :]
    return terms[0]


def source_span(step, first, n, width):
    return slice(first + n - width, first + n) if step > 0 else slice(first, first + (width if step < 0 else n))


def target_span(step, first, n, width):
    if step > 0:
        return slice(first - width, first)
    return slice(first + n, first + n + width) if step < 0 else slice(first, first + n)


def weights_x(level, mob, rows):
    for x in blocks(level, rows):
        level[0][x] = harmonic(mob[0][x], mob[0][moved(x, 1)])


def weights_yz(level, mob, rows, keep_y, keep_z):
    wx, wyu, wyd, wzu, wzd, diag, damp = level
    for x in blocks(level, rows):
        second = mob[1][x]
        up_y = harmonic(second, next_y(second)) * keep_y
        wyu[x] = up_y
        wyd[x] = prev_y(up_y)
        third = mob[2][x]
        up_z = harmonic(third, next_z(third)) * keep_z
        wzu[x] = up_z
        wzd[x] = prev_z(up_z)


def diagonals(level, store, rows):
    wx, wyu, wyd, wzu, wzd, diag, damp = level
    for x in blocks(level, rows):
        all_of_it = store[x] + (wx[x] + wx[moved(x, -1)]) + (wyu[x] + wyd[x]) + (wzu[x] + wzd[x])
        diag[x] = all_of_it
        damp[x] = DAMPING * reciprocal(all_of_it)


def residual_of(level, source, field, x):
    wx, wyu, wyd, wzu, wzd, diag, damp = level
    v = field[x]
    left = source[x] - diag[x] * v
    left = left + (wx[x] * field[moved(x, 1)] + wx[moved(x, -1)] * field[moved(x, -1)])
    left = left + (wyu[x] * next_y(v) + wyd[x] * prev_y(v))
    return left + (wzu[x] * next_z(v) + wzd[x] * prev_z(v))


def sweep(level, source, field, result, rows):
    damp = level[6]
    for x in blocks(level, rows):
        result[x] = field[x] + damp[x] * residual_of(level, source, field, x)


def start_sweep(level, source, result, rows):
    damp = level[6]
    for x in blocks(level, rows):
        result[x] = damp[x] * source[x]


def kernel(
    count_x,
    count_y,
    rhs_h,
    store_f_h,
    mob_f_h,
    store_m_h,
    mob_m_h,
    store_c_h,
    mob_c_h,
    pressure,
    residual,
    f_stage,
    f_mixed,
    f_in,
    f_wx,
    f_wyu,
    f_wyd,
    f_wzu,
    f_wzd,
    f_diag,
    f_damp,
    f_a,
    f_b,
    f_x,
    m_in,
    m_src,
    m_wx,
    m_wyu,
    m_wyd,
    m_wzu,
    m_wzd,
    m_diag,
    m_damp,
    m_a,
    m_b,
    m_y,
    m_fold,
    f_rows,
    together,
    c_coef,
    c_src,
    c_ext,
    c_weights,
    c_bands,
    c_inverse,
    meter,
    spare,
    c_spare,
    local_sem,
    send_sem,
    recv_sem,
):
    gx = lax.axis_index("gx")
    gy = lax.axis_index("gy")

    def stepped(at, step, count):
        to = at + step
        if step > 0:
            return jnp.where(to >= count, to - count, to)
        return jnp.where(to < 0, to + count, to) if step < 0 else at

    along_gx = {step: stepped(gx, step, count_x) for step in (-1, 0, 1)}
    along_gy = {step: stepped(gy, step, count_y) for step in range(-REACH, REACH + 1)}

    def beside(sx, sy):
        return {"gx": along_gx[sx], "gy": along_gy[sy]}

    def ahead_of(sx):
        return gx < count_x - 1 if sx > 0 else gx > 0

    barrier = pltpu.get_barrier_semaphore()

    def greet(steps):
        for step in steps:
            pl.semaphore_signal(barrier, inc=1, device_id=beside(*step), device_id_type=MESH)

    for side in (1, -1):

        @pl.when(ahead_of(side))
        def _():
            greet([step for step in NEIGHBOURS if step[0] == side])

    straight = [(0, e) for e in range(-REACH, REACH + 1) if e != 0]
    greet(straight)
    partners = len(straight) + jnp.where(gx > 0, 3, 0) + jnp.where(gx < count_x - 1, 3, 0)

    c_coef[:, 6:8] = jnp.ones((4, 2, 32, 64), jnp.float32)
    c_src[6:8] = jnp.zeros((2, 32, 128), jnp.float32)

    locals_ = []

    def bring(source, target):
        copy = pltpu.make_async_copy(source, target, local_sem.at[len(locals_)])
        copy.start()
        locals_.append(copy)
        return copy

    def exchange(at, messages):
        sizes = []
        for source, _, _ in messages:
            rows = 1
            for size in source.shape[:-1]:
                rows = rows * size
            sizes.append(rows)
        rows_of[at] = rows_of.get(at, 0) + sum(sizes)

        def send(side):
            for source, target, step in messages:
                if step[0] == side:
                    pltpu.make_async_remote_copy(
                        src_ref=source,
                        dst_ref=target,
                        send_sem=send_sem.at[at],
                        recv_sem=recv_sem.at[at],
                        device_id=beside(*step),
                        device_id_type=MESH,
                    ).start()

        for side in (1, -1):
            rows = sum(size for size, message in zip(sizes, messages) if message[2][0] == side)
            if rows == 0:
                continue
            first = spent[0]
            spent[0] += rows

            @pl.when(ahead_of(side))
            def _():
                send(side)

            @pl.when(jnp.logical_not(ahead_of(side)))
            def _():
                if at == COEF_X:
                    pltpu.make_async_copy(c_coef.at[:, 2:4, OWN_C, :], c_spare, send_sem.at[at]).start()
                else:
                    spare_to = spare.at[first : first + rows, :]
                    pltpu.make_async_copy(meter.at[0:rows, :], spare_to, send_sem.at[at]).start()

            @pl.when(jnp.logical_not(ahead_of(-side)))
            def _():
                for source, target, step in messages:
                    if step[0] == side:
                        pltpu.make_async_copy(source, target, recv_sem.at[at]).start()

        send(0)

    spent = [0]
    rows_of = {}

    def all_of(at):
        if at == COEF_X:
            return c_coef.at[:, 0:4, 0:2, :]
        if at == COEF_Y:
            return c_coef.at[:, 0:6, 0:16, :]
        return meter.at[0 : rows_of[at], :]

    def received(at):
        pltpu.make_async_copy(all_of(at), all_of(at), recv_sem.at[at]).wait()

    def sent(at):
        pltpu.make_async_copy(all_of(at), all_of(at), send_sem.at[at]).wait()

    own8, pairs8 = slice(O, O + 8), slice(OP, OP + 4)
    own4, pairs4 = slice(O, O + 4), slice(OP, OP + 2)
    fine_in = [
        bring(mob_f_h, f_stage.at[0:3]),
        bring(store_f_h, f_stage.at[3]),
        bring(rhs_h, f_stage.at[4]),
    ]
    coarse_in = [
        bring(store_c_h, c_coef.at[0, 2:4, OWN_C, :]),
        bring(mob_c_h, c_coef.at[1:4, 2:4, OWN_C, :]),
    ]
    mid_in = []
    for y in range(4):
        parity, pair = y % 2, OP + y // 2
        mid_in.append(bring(mob_m_h.at[:, :, y, :], m_in.at[0:3, own4, parity, pair, :]))
        mid_in.append(bring(store_m_h.at[:, y, :], m_in.at[3, own4, parity, pair, :]))
    f_src = f_in.at[SOURCE]

    def spans(sx, sy, n, wide_x, wide_y):
        return (
            source_span(sx, O, n, wide_x),
            source_span(sy, OP, n // 2, wide_y),
            target_span(sx, O, n, wide_x),
            target_span(sy, OP, n // 2, wide_y),
        )

    faces_x = [step for step in NEIGHBOURS if step[1] == 0]
    faces_y = [step for step in NEIGHBOURS if step[0] == 0]
    corners = [step for step in NEIGHBOURS if step[0] != 0 and step[1] != 0]

    apart = one_hot((256, 256), lambda row, column: row == 2 * (column % 128) + column // 128)
    for copy in fine_in:
        copy.wait()
    sorted_z = times_one_hot(f_stage[...].reshape(320, 256), apart, 2)
    for half in range(2):
        f_mixed[half] = sorted_z[:, 128 * half : 128 * half + 128].reshape(40, 8, 128)

    def sort_y(x, _):
        for at, to in enumerate((M0, M1, M2, STORE, SOURCE)):
            for parity in range(2):
                for half in range(2):
                    rows = f_mixed[half, 8 * at + x, pl.ds(parity, 4, stride=2), :]
                    f_in[to, O + x, parity, half, pairs8] = rows
        return 0

    lax.fori_loop(0, 8, sort_y, 0, unroll=True)
    pl.semaphore_wait(barrier, partners)

    def part(first, last, step, wide_x, wide_y, parity=slice(0, 2)):
        fields = slice(first, last + 1)
        ax, ay, bx, by = spans(*step, 8, wide_x, wide_y)
        return (f_in.at[fields, ax, parity, :, ay, :], f_in.at[fields, bx, parity, :, by, :], step)

    for copy in coarse_in:
        copy.wait()
    exchange(
        COEF_X,
        [
            (c_coef.at[:, 2:4, OWN_C, :], c_coef.at[:, 2 - 2 * sx : 4 - 2 * sx, OWN_C, :], (sx, sy))
            for sx, sy in faces_x
        ],
    )

    messages = []
    for step in faces_x:
        messages += [part(M0, M0, step, 3, 1), part(M2, M1, step, 2, 1)]
    for step in corners:
        nearest = slice(1, 2) if step[1] > 0 else slice(0, 1)
        messages += [part(M0, M0, step, 2, 1), part(M1, M1, step, 2, 1), part(M2, SOURCE, step, 1, 1, nearest)]
    exchange(FINE_X, messages)
    messages = []
    for step in faces_y:
        messages += [part(M0, SOURCE, step, 1, 1), part(M1, M1, step, 1, 2)]
    exchange(FINE_Y, messages)

    for copy in mid_in:
        copy.wait()
    messages = []
    for step in NEIGHBOURS:
        ax, ay, bx, by = spans(*step, 4, 3 if step in corners else 4, 2)
        messages.append((m_in.at[:, ax, :, ay, :], m_in.at[:, bx, :, by, :], step))
    exchange(MID_IN, messages)

    one = jnp.float32(1.0)
    nil = jnp.float32(0.0)
    keep_x = (jnp.where(gx == 0, nil, one), jnp.where(gx == count_x - 1, nil, one))

    def keep_yz(own, shape):
        def index(axis):
            return lax.broadcasted_iota(jnp.int32, shape, axis)

        parity, pair, lane = index(0), index(len(shape) - 2), index(len(shape) - 1)
        end = jnp.where(gy == 0, OP - 1, -1)
        other = jnp.where(gy == count_y - 1, OP + own // 2 - 1, -1)
        keep_y = jnp.where((parity == 1) & ((pair == end) | (pair == other)), 0.0, 1.0)
        last_z = (lane == 127) if len(shape) == 3 else (lane == 127) & (index(1) == 1)
        return keep_y, jnp.where(last_z, 0.0, 1.0)

    together[...] = one_hot((256, 256), lambda row, column: column == 2 * (row % 128) + row // 128)
    fold_c = one_hot((64, 128), lambda row, column: row // 8 + 8 * (row % 8) == column // 2)

    fine = (f_wx, f_wyu, f_wyd, f_wzu, f_wzd, f_diag, f_damp)
    f_mob = (f_in.at[M0], f_in.at[M1], f_in.at[M2])
    f_store = f_in.at[STORE]
    keep_y, keep_z = keep_yz(8, (2, 2, 8, 128))
    received(FINE_Y)
    weights_yz(fine, f_mob, (O, O + 8), keep_y, keep_z)
    weights_x(fine, f_mob, (O, O + 7))
    diagonals(fine, f_store, (O + 1, O + 7))
    start_sweep(fine, f_src, f_a, (O + 1, O + 7))
    received(COEF_X)
    messages = []
    for step in straight:
        target = c_coef.at[:, 0:6, OWN_C.start - 2 * step[1] : OWN_C.stop - 2 * step[1], :]
        messages.append((c_coef.at[:, 0:6, OWN_C, :], target, step))
    exchange(COEF_Y, messages)
    sweep(fine, f_src, f_a, f_b, (O + 2, O + 6))
    received(FINE_X)
    for rows in ((O - 3, O), (O + 7, O + 10)):
        weights_x(fine, f_mob, rows)
    f_wx[O - 1] = f_wx[O - 1] * keep_x[0]
    f_wx[O + 7] = f_wx[O + 7] * keep_x[1]
    for rows in ((O - 2, O), (O + 8, O + 10)):
        weights_yz(fine, f_mob, rows, keep_y, keep_z)
    for rows in ((O - 2, O + 1), (O + 7, O + 10)):
        diagonals(fine, f_store, rows)
        start_sweep(fine, f_src, f_a, rows)
    for rows in ((O - 1, O + 2), (O + 6, O + 9)):
        sweep(fine, f_src, f_a, f_b, rows)

    for x in blocks(fine, (O, O + 8)):
        left = residual_of(fine, f_src, f_b, x)
        for pair in range(2):
            both = left[2 * pair] + left[2 * pair + 1]
            m_fold[(x.start - O) // 2 + pair] = (both[0, 0] + both[0, 1]) + (both[1, 0] + both[1, 1])
    for x in range(4):
        for parity in range(2):
            m_src[O + x, parity, pairs4] = m_fold[x, pl.ds(OP + parity, 2, stride=2), :]
    messages = []
    for step in NEIGHBOURS:
        ax, ay, bx, by = spans(*step, 4, 2 if step in corners else 3, 1 if step in corners else 2)
        messages.append((m_src.at[ax, :, ay, :], m_src.at[bx, :, by, :], step))
    exchange(MID_F, messages)

    def keep_fine(x, _):
        f_x[x, :, :, pairs8] = f_b[x, :, :, pairs8]
        return 0

    lax.fori_loop(O, O + 8, keep_fine, 0, unroll=True)
    messages = []
    for step in NEIGHBOURS:
        ax, ay, bx, by = spans(*step, 8, 2 if step in corners else 3, 1 if step in corners else 2)
        messages.append((f_x.at[ax, :, :, ay, :], f_x.at[bx, :, :, by, :], step))
    exchange(FINE_V, messages)

    mid = (m_wx, m_wyu, m_wyd, m_wzu, m_wzd, m_diag, m_damp)
    m_mob = (m_in.at[0], m_in.at[1], m_in.at[2])
    keep_y, keep_z = keep_yz(4, (2, 8, 128))
    received(MID_IN)
    weights_x(mid, m_mob, (O - 4, O + 7))
    m_wx[O - 1] = m_wx[O - 1] * keep_x[0]
    m_wx[O + 3] = m_wx[O + 3] * keep_x[1]
    weights_yz(mid, m_mob, (O - 3, O + 7), keep_y, keep_z)
    diagonals(mid, m_in.at[3], (O - 3, O + 7))

    for at in (FINE_X, FINE_Y, COEF_X, MID_IN):
        sent(at)

    received(MID_F)
    start_sweep(mid, m_src, m_a, (O - 2, O + 6))
    sweep(mid, m_src, m_a, m_b, (O - 1, O + 5))
    left = residual_of(mid, m_src, m_b, own4)
    for ix in range(2):
        fold = left[2 * ix] + left[2 * ix + 1]
        c_src[2 + ix, OWN_C, :] = (fold[0] + fold[1])[pairs4]
    messages = []
    for e in sorted(range(-REACH, REACH + 1), key=lambda e: -abs(e)):
        for g in (1, -1, 0):
            if (g, e) != (0, 0):
                target = c_src.at[2 - 2 * g : 4 - 2 * g, OWN_C.start - 2 * e : OWN_C.stop - 2 * e, :]
                messages.append((c_src.at[2:4, OWN_C, :], target, (g, e)))
    exchange(COARSE_F, messages)

    def keep_mid(x, _):
        m_y[x, :, pairs4] = m_b[x, :, pairs4]
        return 0

    lax.fori_loop(O, O + 4, keep_mid, 0, unroll=True)
    messages = []
    for step in NEIGHBOURS:
        ax, ay, bx, by = spans(*step, 4, 3 if step in corners else 4, 2)
        messages.append((m_y.at[ax, :, ay, :], m_y.at[bx, :, by, :], step))
    exchange(MID_V, messages)

    received(COEF_Y)
    coef = [c_coef[k, :, 8:24, :].reshape(128, 64).T for k in range(4)]
    second_prev = c_coef[2, :, 7:23, :].reshape(128, 64).T
    second_next = c_coef[2, :, 9:25, :].reshape(128, 64).T
    column = lax.broadcasted_iota(jnp.int32, (64, 128), 1)
    level_row = lax.broadcasted_iota(jnp.int32, (64, 128), 0)
    cells = 2 * count_y
    cell = 2 * gy + lax.rem(column, 16) + (cells - 7)
    block = 2 * GROUP
    offset = 4 + cells - (cells // block) * block
    shut_up = (lax.rem(cell + 1 - offset + 2 * block, block) == 0) | (lax.rem(cell + 1, cells) == 0)
    shut_down = (lax.rem(cell - offset + 2 * block, block) == 0) | (lax.rem(cell, cells) == 0)
    up_x = jnp.where(lax.rem(column, 32) < 16, harmonic(coef[1], pltpu.roll(coef[1], 112, 1)), 0.0)
    down_x = pltpu.roll(up_x, 16, 1)
    up_y = jnp.where(shut_up, 0.0, harmonic(coef[2], second_next))
    down_y = jnp.where(shut_down, 0.0, harmonic(second_prev, coef[2]))
    up_z = jnp.where(level_row == 63, 0.0, harmonic(coef[3], next_of(coef[3], 0)))
    down_z = prev_of(up_z, 0)
    main = coef[0] + (up_x + down_x) + (up_y + down_y) + (up_z + down_z)
    for at, band in enumerate((up_x, down_x, up_y, down_y, -down_z, main, -up_z)):
        c_bands[at] = band

    def registers(at):
        return [c_bands[at, pl.ds(place, 8, stride=8), :] for place in range(8)]

    for at in range(4):
        for place, values in enumerate(registers(at)):
            c_weights[at, place] = values
    low, main, high = (registers(at) for at in (4, 5, 6))
    ahead, back = [reciprocal(main[0])], {6: reciprocal(main[6])}
    upto, onfrom = [main[0]], {6: main[6]}
    for i in range(1, 7):
        upto.append(main[i] - low[i] * high[i - 1] * ahead[i - 1])
        ahead.append(reciprocal(upto[i]))
        j = 6 - i
        onfrom[j] = main[j] - high[j] * low[j + 1] * back[j + 1]
        back[j] = reciprocal(onfrom[j])
    rise = [-high[i] * ahead[i] for i in range(7)]
    fall = [-low[i] * back[i] for i in range(7)]
    inverse = {}
    for j in range(7):
        inverse[j, j] = reciprocal(upto[j] + onfrom[j] - main[j])
        for i in range(j - 1, -1, -1):
            inverse[i, j] = rise[i] * inverse[i + 1, j]
        for i in range(j + 1, 7):
            inverse[i, j] = fall[i] * inverse[i - 1, j]
    from_last = [inverse[i, 0] * low[0] for i in range(7)]
    from_own = [inverse[i, 6] * high[6] for i in range(7)]

    def turned(values, by):
        return pltpu.roll(values, by % 8, 0) if by % 8 else values

    face_main = main[7] - low[7] * from_own[6] - high[7] * turned(from_last[0], -1)
    face_low = -low[7] * from_last[6]
    face_high = -high[7] * turned(from_own[0], -1)
    spread_by = {0: jnp.ones((8, 128), jnp.float32)}
    for far in (1, 2, 4):
        over = reciprocal(face_main)
        alpha = -face_low * turned(over, far)
        gamma = -face_high * turned(over, -far)
        face_main = face_main + alpha * turned(face_high, far) + gamma * turned(face_low, -far)
        face_low, face_high = alpha * turned(face_low, far), gamma * turned(face_high, -far)
        wider = dict(spread_by)
        for by, values in spread_by.items():
            for step, factor in ((far, alpha), (-far, gamma)):
                term = factor * turned(values, step)
                key = (by + step) % 8
                wider[key] = wider[key] + term if key in wider else term
        spread_by = wider
    over = reciprocal(face_main)
    own_by = [over * spread_by[by] for by in range(8)]
    next_by = [own_by[(by + 1) % 8] * turned(high[7], by + 1) for by in range(8)]
    for i in range(7):
        for j in range(7):
            c_inverse[7 * i + j] = inverse[i, j]
        c_inverse[49 + i] = from_last[i]
        c_inverse[56 + i] = from_own[i]
    for by in range(8):
        c_inverse[64 + by] = own_by[by]
        c_inverse[72 + by] = next_by[by]
        c_inverse[80 + by] = turned(own_by[by - 1], 1)
        c_inverse[88 + by] = turned(next_by[by - 1], 1)
    c_inverse[63] = low[7]

    def lines(values):
        inner = [total([c_inverse[7 * i + j] * values[j] for j in range(7)]) for i in range(7)]
        face = values[7] - c_inverse[63] * inner[6]
        faces = [turned(face, by) for by in range(8)]
        firsts = [turned(inner[0], by) for by in range(8)]

        def interface(at):
            terms = [c_inverse[at + by] * faces[by] for by in range(8)]
            return total(terms) - total([c_inverse[at + 8 + by] * firsts[by] for by in range(8)])

        here, before = interface(64), interface(80)
        return tuple(inner[i] - (c_inverse[49 + i] * before + c_inverse[56 + i] * here) for i in range(7)) + (here,)

    for at in (COEF_Y, MID_F, FINE_V):
        sent(at)

    received(COARSE_F)
    source = lax.dot_general(
        jnp.concatenate([fold_c] * 2, axis=1),
        jnp.concatenate(pieces(c_src[:, 8:24, :].reshape(128, 128), 2), axis=1),
        (((1,), (1,)), ((), ())),
        preferred_element_type=jnp.float32,
    )
    sources = [source[8 * place : 8 * place + 8] for place in range(8)]

    def turn(_, z):
        pushed = []
        for place in range(8):
            own = z[place]
            along_x = c_weights[0, place] * pltpu.roll(own, 112, 1) + c_weights[1, place] * pltpu.roll(own, 16, 1)
            along_y = c_weights[2, place] * next_of(own, 1) + c_weights[3, place] * prev_of(own, 1)
            pushed.append(sources[place] + (along_x + along_y))
        return lines(pushed)

    z = lax.fori_loop(0, KC - 1, turn, lines(sources))
    c_ext[...] = times_one_hot(jnp.concatenate(z, axis=0).T[0:96], fold_c, 2).reshape(6, 16, 128)

    received(MID_V)

    def raise_mid(x, _):
        rows = c_ext[x, 5:13, :]
        for along in range(2):
            for parity in range(2):
                m_a[2 * x + along, parity] = m_y[2 * x + along, parity] + rows
        return 0

    lax.fori_loop(0, 6, raise_mid, 0, unroll=True)
    sweep(mid, m_src, m_a, m_b, (O - 3, O + 7))
    sweep(mid, m_src, m_b, m_a, (O - 2, O + 6))

    received(FINE_V)

    def raise_fine(x, _):
        for parity in range(2):
            m_fold[x, pl.ds(parity, 4, stride=2), :] = m_a[O - 2 + x, parity, 1:5]
        rows = m_fold[x]
        for along in range(2):
            for parity in range(2):
                for half in range(2):
                    at = (2 * x + along, parity, half)
                    f_a[at] = f_x[at] + rows
        return 0

    lax.fori_loop(0, 8, raise_fine, 0, unroll=True)
    sweep(fine, f_src, f_a, f_b, (O - 2, O + 10))
    sweep(fine, f_src, f_b, f_a, (O - 1, O + 9))


    def in_order(field, result):
        def sort_back(x, _):
            for parity in range(2):
                for half in range(2):
                    f_rows[half, x, pl.ds(parity, 8, stride=2), :] = field[O + x, parity, half]
            return 0

        lax.fori_loop(0, 8, sort_back, 0, unroll=True)
        halves = [f_rows[half, :, O : O + 8, :].reshape(64, 128) for half in range(2)]
        result[...] = times_one_hot(jnp.concatenate(halves, axis=1), together[...], 2).reshape(8, 8, 256)

    in_order(f_a, pressure)

    for x in blocks(fine, (O, O + 8)):
        f_b[x] = residual_of(fine, f_src, f_a, x)
    in_order(f_b, residual)
    for at in (COARSE_F, MID_V):
        sent(at)


def publish(pressure, residual, pressure_h, residual_h, sem):
    copies = [
        pltpu.make_async_copy(pressure, pressure_h, sem.at[0]),
        pltpu.make_async_copy(residual, residual_h, sem.at[1]),
    ]
    for copy in copies:
        copy.start()
    for copy in copies:
        copy.wait()


def local(pressure_rhs, storage_fine, mobility_fine, storage_mid, mobility_mid, storage_coarse, mobility_coarse):
    count_x = lax.axis_size("gx")
    count_y = lax.axis_size("gy")
    f32 = jnp.float32
    fine = pltpu.VMEM((8 + 2 * O, 2, 2, 8, 128), f32)
    mid = pltpu.VMEM((4 + 2 * O, 2, 8, 128), f32)
    in_hbm = pl.BlockSpec(memory_space=pltpu.HBM)
    in_vmem = pl.BlockSpec(memory_space=pltpu.VMEM)
    arrays = (pressure_rhs, storage_fine, mobility_fine, storage_mid, mobility_mid, storage_coarse, mobility_coarse)
    result = pl.pallas_call(
        functools.partial(kernel, count_x, count_y),
        out_shape=(pltpu.VMEM(pressure_rhs.shape, f32),) * 2,
        in_specs=[in_hbm] * 7,
        out_specs=(in_vmem, in_vmem),
        scratch_shapes=[
            pltpu.VMEM((5, 8, 8, 256), f32),
            pltpu.VMEM((2, 40, 8, 128), f32),
            pltpu.VMEM((5, 8 + 2 * O, 2, 2, 8, 128), f32),
            *[fine] * 10,
            pltpu.VMEM((4, 4 + 2 * O, 2, 8, 128), f32),
            *[mid] * 11,
            pltpu.VMEM((8, 8, 128), f32),
            pltpu.VMEM((2, 8, 16, 128), f32),
            pltpu.VMEM((256, 256), jnp.bfloat16),
            pltpu.VMEM((4, 8, 32, 64), f32),
            pltpu.VMEM((8, 32, 128), f32),
            pltpu.VMEM((6, 16, 128), f32),
            pltpu.VMEM((4, 8, 8, 128), f32),
            pltpu.VMEM((7, 64, 128), f32),
            pltpu.VMEM((97, 8, 128), f32),
            pltpu.VMEM((1024, 128), f32),
            pltpu.VMEM((4096, 128), f32),
            pltpu.VMEM((4, 2, 2, 64), f32),
            pltpu.SemaphoreType.DMA((16,)),
            pltpu.SemaphoreType.DMA((EXCHANGES,)),
            pltpu.SemaphoreType.DMA((EXCHANGES,)),
        ],
        compiler_params=pltpu.CompilerParams(
            collective_id=0, has_side_effects=True, vmem_limit_bytes=32 * 1024 * 1024
        ),
    )(*[pltpu.with_memory_space_constraint(array, pltpu.HBM) for array in arrays])
    out = jax.ShapeDtypeStruct(pressure_rhs.shape, f32)
    return pl.pallas_call(
        publish,
        out_shape=(out, out),
        in_specs=[in_vmem] * 2,
        out_specs=(in_hbm, in_hbm),
        scratch_shapes=[pltpu.SemaphoreType.DMA((2,))],
        compiler_params=pltpu.CompilerParams(vmem_limit_bytes=16 * 1024 * 1024),
    )(*result)


def solution(mesh):
    placed = (
        P("gx", "gy", None),
        P("gx", "gy", None),
        P(None, "gx", "gy", None),
        P("gx", "gy", None),
        P(None, "gx", "gy", None),
        P("gx", "gy", None),
        P(None, "gx", "gy", None),
    )
    return jax.shard_map(
        local,
        mesh=mesh,
        in_specs=placed,
        out_specs=(P("gx", "gy", None), P("gx", "gy", None)),
        check_vma=False,
    )
```

```python
import functools

import jax
import jax.numpy as jnp
from jax import lax
from jax.experimental import pallas as pl
from jax.experimental.pallas import tpu as pltpu
from jax.sharding import PartitionSpec as P

KC = 6
GROUP = 8
REACH = 4
DAMPING = 2.0 / 3.0

MESH = pl.DeviceIdType.MESH

O = 4
OP = 2
M0, M2, STORE, SOURCE, M1 = range(5)
OWN_C = slice(15, 17)
FINE_X, FINE_Y, COEF_X, COEF_Y, MID_IN, MID_F, FINE_V, COARSE_F, MID_V = range(9)
EXCHANGES = 9
NEIGHBOURS = ((1, 0), (-1, 0), (1, 1), (1, -1), (-1, 1), (-1, -1), (0, 1), (0, -1))


def reciprocal(values):
    guess = pl.reciprocal(values, approx=True)
    return guess * (2.0 - values * guess)


def harmonic(left, right):
    return 2.0 * left * right * reciprocal(left + right)


def next_of(values, axis):
    return pltpu.roll(values, values.shape[axis] - 1, axis)


def prev_of(values, axis):
    return pltpu.roll(values, 1, axis)


def next_paired(values, axis, pairs):
    first, second = lax.slice_in_dim(values, 0, 1, axis=axis), lax.slice_in_dim(values, 1, 2, axis=axis)
    return jnp.concatenate([second, next_of(first, pairs)], axis=axis)


def prev_paired(values, axis, pairs):
    first, second = lax.slice_in_dim(values, 0, 1, axis=axis), lax.slice_in_dim(values, 1, 2, axis=axis)
    return jnp.concatenate([prev_of(second, pairs), first], axis=axis)


def next_y(values):
    return next_paired(values, 1, values.ndim - 2)


def prev_y(values):
    return prev_paired(values, 1, values.ndim - 2)


def next_z(values):
    return next_paired(values, 2, 4) if values.ndim == 5 else next_of(values, 3)


def prev_z(values):
    return prev_paired(values, 2, 4) if values.ndim == 5 else prev_of(values, 3)


def blocks(level, rows):
    first, last = rows
    most = 4 if len(level[0].shape) == 5 else 6
    count = -(-(last - first) // most)
    edges = [first + (last - first) * at // count for at in range(count + 1)]
    return [slice(*pair) for pair in zip(edges[:-1], edges[1:])]


def moved(rows, by):
    return slice(rows.start + by, rows.stop + by)


def one_hot(shape, test):
    row = lax.broadcasted_iota(jnp.int32, shape, 0)
    column = lax.broadcasted_iota(jnp.int32, shape, 1)
    return jnp.where(test(row, column), 1.0, 0.0).astype(jnp.bfloat16)


def pieces(values, count):
    parts = []
    for _ in range(count - 1):
        parts.append(values.astype(jnp.bfloat16))
        values = values - parts[-1].astype(jnp.float32)
    return parts + [values.astype(jnp.bfloat16)]


def times_one_hot(values, matrix, count):
    rows = values.shape[0]
    product = jnp.dot(jnp.concatenate(pieces(values, count), axis=0), matrix, preferred_element_type=jnp.float32)
    return total([product[at * rows : (at + 1) * rows] for at in range(count)])


def total(terms):
    while len(terms) > 1:
        pairs = [terms[i] + terms[i + 1] for i in range(0, len(terms) - 1, 2)]
        terms = pairs + terms[len(terms) - len(terms) % 2 :]
    return terms[0]


def source_span(step, first, n, width):
    return slice(first + n - width, first + n) if step > 0 else slice(first, first + (width if step < 0 else n))


def target_span(step, first, n, width):
    if step > 0:
        return slice(first - width, first)
    return slice(first + n, first + n + width) if step < 0 else slice(first, first + n)


def weights_x(level, mob, rows):
    for x in blocks(level, rows):
        level[0][x] = harmonic(mob[0][x], mob[0][moved(x, 1)])


def weights_yz(level, mob, rows, keep_y, keep_z):
    wx, wyu, wyd, wzu, wzd, diag, damp = level
    for x in blocks(level, rows):
        second = mob[1][x]
        up_y = harmonic(second, next_y(second)) * keep_y
        wyu[x] = up_y
        wyd[x] = prev_y(up_y)
        third = mob[2][x]
        up_z = harmonic(third, next_z(third)) * keep_z
        wzu[x] = up_z
        wzd[x] = prev_z(up_z)


def diagonals(level, store, rows):
    wx, wyu, wyd, wzu, wzd, diag, damp = level
    for x in blocks(level, rows):
        all_of_it = store[x] + (wx[x] + wx[moved(x, -1)]) + (wyu[x] + wyd[x]) + (wzu[x] + wzd[x])
        diag[x] = all_of_it
        damp[x] = DAMPING * reciprocal(all_of_it)


def residual_of(level, source, field, x):
    wx, wyu, wyd, wzu, wzd, diag, damp = level
    v = field[x]
    left = source[x] - diag[x] * v
    left = left + (wx[x] * field[moved(x, 1)] + wx[moved(x, -1)] * field[moved(x, -1)])
    left = left + (wyu[x] * next_y(v) + wyd[x] * prev_y(v))
    return left + (wzu[x] * next_z(v) + wzd[x] * prev_z(v))


def sweep(level, source, field, result, rows):
    damp = level[6]
    for x in blocks(level, rows):
        result[x] = field[x] + damp[x] * residual_of(level, source, field, x)


def start_sweep(level, source, result, rows):
    damp = level[6]
    for x in blocks(level, rows):
        result[x] = damp[x] * source[x]


def kernel(
    count_x,
    count_y,
    rhs_h,
    store_f_h,
    mob_f_h,
    store_m_h,
    mob_m_h,
    store_c_h,
    mob_c_h,
    pressure,
    residual,
    f_stage,
    f_mixed,
    f_in,
    f_wx,
    f_wyu,
    f_wyd,
    f_wzu,
    f_wzd,
    f_diag,
    f_damp,
    f_a,
    f_b,
    f_x,
    m_in,
    m_src,
    m_wx,
    m_wyu,
    m_wyd,
    m_wzu,
    m_wzd,
    m_diag,
    m_damp,
    m_a,
    m_b,
    m_y,
    m_fold,
    f_rows,
    together,
    c_coef,
    c_src,
    c_ext,
    c_weights,
    c_bands,
    c_inverse,
    meter,
    spare,
    c_spare,
    local_sem,
    send_sem,
    recv_sem,
):
    gx = lax.axis_index("gx")
    gy = lax.axis_index("gy")

    def stepped(at, step, count):
        to = at + step
        if step > 0:
            return jnp.where(to >= count, to - count, to)
        return jnp.where(to < 0, to + count, to) if step < 0 else at

    along_gx = {step: stepped(gx, step, count_x) for step in (-1, 0, 1)}
    along_gy = {step: stepped(gy, step, count_y) for step in range(-REACH, REACH + 1)}

    def beside(sx, sy):
        return {"gx": along_gx[sx], "gy": along_gy[sy]}

    def ahead_of(sx):
        return gx < count_x - 1 if sx > 0 else gx > 0

    barrier = pltpu.get_barrier_semaphore()

    def greet(steps):
        for step in steps:
            pl.semaphore_signal(barrier, inc=1, device_id=beside(*step), device_id_type=MESH)

    for side in (1, -1):

        @pl.when(ahead_of(side))
        def _():
            greet([step for step in NEIGHBOURS if step[0] == side])

    straight = [(0, e) for e in range(-REACH, REACH + 1) if e != 0]
    greet(straight)
    partners = len(straight) + jnp.where(gx > 0, 3, 0) + jnp.where(gx < count_x - 1, 3, 0)

    c_coef[:, 6:8] = jnp.ones((4, 2, 32, 64), jnp.float32)
    c_src[6:8] = jnp.zeros((2, 32, 128), jnp.float32)

    locals_ = []

    def bring(source, target):
        copy = pltpu.make_async_copy(source, target, local_sem.at[len(locals_)])
        copy.start()
        locals_.append(copy)
        return copy

    def exchange(at, messages):
        sizes = []
        for source, _, _ in messages:
            rows = 1
            for size in source.shape[:-1]:
                rows = rows * size
            sizes.append(rows)
        rows_of[at] = rows_of.get(at, 0) + sum(sizes)

        def send(side):
            for source, target, step in messages:
                if step[0] == side:
                    pltpu.make_async_remote_copy(
                        src_ref=source,
                        dst_ref=target,
                        send_sem=send_sem.at[at],
                        recv_sem=recv_sem.at[at],
                        device_id=beside(*step),
                        device_id_type=MESH,
                    ).start()

        for side in (1, -1):
            rows = sum(size for size, message in zip(sizes, messages) if message[2][0] == side)
            if rows == 0:
                continue
            first = spent[0]
            spent[0] += rows

            @pl.when(ahead_of(side))
            def _():
                send(side)

            @pl.when(jnp.logical_not(ahead_of(side)))
            def _():
                if at == COEF_X:
                    pltpu.make_async_copy(c_coef.at[:, 2:4, OWN_C, :], c_spare, send_sem.at[at]).start()
                else:
                    spare_to = spare.at[first : first + rows, :]
                    pltpu.make_async_copy(meter.at[0:rows, :], spare_to, send_sem.at[at]).start()

            @pl.when(jnp.logical_not(ahead_of(-side)))
            def _():
                for source, target, step in messages:
                    if step[0] == side:
                        pltpu.make_async_copy(source, target, recv_sem.at[at]).start()

        send(0)

    spent = [0]
    rows_of = {}

    def all_of(at):
        if at == COEF_X:
            return c_coef.at[:, 0:4, 0:2, :]
        if at == COEF_Y:
            return c_coef.at[:, 0:6, 0:16, :]
        return meter.at[0 : rows_of[at], :]

    def received(at):
        pltpu.make_async_copy(all_of(at), all_of(at), recv_sem.at[at]).wait()

    def sent(at):
        pltpu.make_async_copy(all_of(at), all_of(at), send_sem.at[at]).wait()

    own8, pairs8 = slice(O, O + 8), slice(OP, OP + 4)
    own4, pairs4 = slice(O, O + 4), slice(OP, OP + 2)
    fine_in = [
        bring(mob_f_h, f_stage.at[0:3]),
        bring(store_f_h, f_stage.at[3]),
        bring(rhs_h, f_stage.at[4]),
    ]
    coarse_in = [
        bring(store_c_h, c_coef.at[0, 2:4, OWN_C, :]),
        bring(mob_c_h, c_coef.at[1:4, 2:4, OWN_C, :]),
    ]
    mid_in = []
    for y in range(4):
        parity, pair = y % 2, OP + y // 2
        mid_in.append(bring(mob_m_h.at[:, :, y, :], m_in.at[0:3, own4, parity, pair, :]))
        mid_in.append(bring(store_m_h.at[:, y, :], m_in.at[3, own4, parity, pair, :]))
    f_src = f_in.at[SOURCE]

    def spans(sx, sy, n, wide_x, wide_y):
        return (
            source_span(sx, O, n, wide_x),
            source_span(sy, OP, n // 2, wide_y),
            target_span(sx, O, n, wide_x),
            target_span(sy, OP, n // 2, wide_y),
        )

    faces_x = [step for step in NEIGHBOURS if step[1] == 0]
    faces_y = [step for step in NEIGHBOURS if step[0] == 0]
    corners = [step for step in NEIGHBOURS if step[0] != 0 and step[1] != 0]

    apart = one_hot((256, 256), lambda row, column: row == 2 * (column % 128) + column // 128)
    for copy in fine_in:
        copy.wait()
    sorted_z = times_one_hot(f_stage[...].reshape(320, 256), apart, 2)
    for half in range(2):
        f_mixed[half] = sorted_z[:, 128 * half : 128 * half + 128].reshape(40, 8, 128)

    def sort_y(x, _):
        for at, to in enumerate((M0, M1, M2, STORE, SOURCE)):
            for parity in range(2):
                for half in range(2):
                    rows = f_mixed[half, 8 * at + x, pl.ds(parity, 4, stride=2), :]
                    f_in[to, O + x, parity, half, pairs8] = rows
        return 0

    lax.fori_loop(0, 8, sort_y, 0, unroll=True)
    pl.semaphore_wait(barrier, partners)

    def part(first, last, step, wide_x, wide_y, parity=slice(0, 2)):
        fields = slice(first, last + 1)
        ax, ay, bx, by = spans(*step, 8, wide_x, wide_y)
        return (f_in.at[fields, ax, parity, :, ay, :], f_in.at[fields, bx, parity, :, by, :], step)

    for copy in coarse_in:
        copy.wait()
    exchange(
        COEF_X,
        [
            (c_coef.at[:, 2:4, OWN_C, :], c_coef.at[:, 2 - 2 * sx : 4 - 2 * sx, OWN_C, :], (sx, sy))
            for sx, sy in faces_x
        ],
    )

    messages = []
    for step in faces_x:
        messages += [part(M0, M0, step, 3, 1), part(M2, M1, step, 2, 1)]
    for step in corners:
        nearest = slice(1, 2) if step[1] > 0 else slice(0, 1)
        messages += [part(M0, M0, step, 2, 1), part(M1, M1, step, 2, 1), part(M2, SOURCE, step, 1, 1, nearest)]
    exchange(FINE_X, messages)
    messages = []
    for step in faces_y:
        messages += [part(M0, SOURCE, step, 1, 1), part(M1, M1, step, 1, 2)]
    exchange(FINE_Y, messages)

    for copy in mid_in:
        copy.wait()
    messages = []

    def mid_part(first, last, step, wide_x, wide_y, beyond_y=0):
        fields = slice(first, last + 1)
        ax, ay, bx, by = spans(*step, 4, wide_x, wide_y)
        if beyond_y and step[1] > 0:
            ay, by = slice(ay.start, ay.stop - beyond_y), slice(by.start, by.stop - beyond_y)
        elif beyond_y:
            ay, by = slice(ay.start + beyond_y, ay.stop), slice(by.start + beyond_y, by.stop)
        return (m_in.at[fields, ax, :, ay, :], m_in.at[fields, bx, :, by, :], step)

    for step in faces_x:
        messages += [mid_part(0, 0, step, 4, 1), mid_part(1, 3, step, 3, 1)]
    for step in corners:
        messages += [mid_part(0, 1, step, 3, 1), mid_part(0, 1, step, 1, 2, 1), mid_part(2, 3, step, 2, 1)]
    for step in faces_y:
        messages.append(mid_part(0, 3, step, 4, 2))
    exchange(MID_IN, messages)

    one = jnp.float32(1.0)
    nil = jnp.float32(0.0)
    keep_x = (jnp.where(gx == 0, nil, one), jnp.where(gx == count_x - 1, nil, one))

    def keep_yz(own, shape):
        def index(axis):
            return lax.broadcasted_iota(jnp.int32, shape, axis)

        parity, pair, lane = index(0), index(len(shape) - 2), index(len(shape) - 1)
        end = jnp.where(gy == 0, OP - 1, -1)
        other = jnp.where(gy == count_y - 1, OP + own // 2 - 1, -1)
        keep_y = jnp.where((parity == 1) & ((pair == end) | (pair == other)), 0.0, 1.0)
        last_z = (lane == 127) if len(shape) == 3 else (lane == 127) & (index(1) == 1)
        return keep_y, jnp.where(last_z, 0.0, 1.0)

    together[...] = one_hot((256, 256), lambda row, column: column == 2 * (row % 128) + row // 128)
    fold_c = one_hot((64, 128), lambda row, column: row // 8 + 8 * (row % 8) == column // 2)

    fine = (f_wx, f_wyu, f_wyd, f_wzu, f_wzd, f_diag, f_damp)
    f_mob = (f_in.at[M0], f_in.at[M1], f_in.at[M2])
    f_store = f_in.at[STORE]
    keep_y, keep_z = keep_yz(8, (2, 2, 8, 128))
    received(FINE_Y)
    weights_yz(fine, f_mob, (O, O + 8), keep_y, keep_z)
    weights_x(fine, f_mob, (O, O + 7))
    diagonals(fine, f_store, (O + 1, O + 7))
    start_sweep(fine, f_src, f_a, (O + 1, O + 7))
    received(COEF_X)
    messages = []
    for step in straight:
        target = c_coef.at[:, 0:6, OWN_C.start - 2 * step[1] : OWN_C.stop - 2 * step[1], :]
        messages.append((c_coef.at[:, 0:6, OWN_C, :], target, step))
    exchange(COEF_Y, messages)
    sweep(fine, f_src, f_a, f_b, (O + 2, O + 6))
    received(FINE_X)
    for rows in ((O - 3, O), (O + 7, O + 10)):
        weights_x(fine, f_mob, rows)
    f_wx[O - 1] = f_wx[O - 1] * keep_x[0]
    f_wx[O + 7] = f_wx[O + 7] * keep_x[1]
    for rows in ((O - 2, O), (O + 8, O + 10)):
        weights_yz(fine, f_mob, rows, keep_y, keep_z)
    for rows in ((O - 2, O + 1), (O + 7, O + 10)):
        diagonals(fine, f_store, rows)
        start_sweep(fine, f_src, f_a, rows)
    for rows in ((O - 1, O + 2), (O + 6, O + 9)):
        sweep(fine, f_src, f_a, f_b, rows)

    for x in blocks(fine, (O, O + 8)):
        left = residual_of(fine, f_src, f_b, x)
        for pair in range(2):
            both = left[2 * pair] + left[2 * pair + 1]
            m_fold[(x.start - O) // 2 + pair] = (both[0, 0] + both[0, 1]) + (both[1, 0] + both[1, 1])
    for x in range(4):
        for parity in range(2):
            m_src[O + x, parity, pairs4] = m_fold[x, pl.ds(OP + parity, 2, stride=2), :]
    messages = []
    for step in NEIGHBOURS:
        ax, ay, bx, by = spans(*step, 4, 2 if step in corners else 3, 1 if step in corners else 2)
        messages.append((m_src.at[ax, :, ay, :], m_src.at[bx, :, by, :], step))
    exchange(MID_F, messages)

    def keep_fine(x, _):
        f_x[x, :, :, pairs8] = f_b[x, :, :, pairs8]
        return 0

    lax.fori_loop(O, O + 8, keep_fine, 0, unroll=True)
    messages = []
    for step in NEIGHBOURS:
        ax, ay, bx, by = spans(*step, 8, 2 if step in corners else 3, 1 if step in corners else 2)
        messages.append((f_x.at[ax, :, :, ay, :], f_x.at[bx, :, :, by, :], step))
    exchange(FINE_V, messages)

    mid = (m_wx, m_wyu, m_wyd, m_wzu, m_wzd, m_diag, m_damp)
    m_mob = (m_in.at[0], m_in.at[1], m_in.at[2])
    keep_y, keep_z = keep_yz(4, (2, 8, 128))
    received(MID_IN)
    weights_x(mid, m_mob, (O - 4, O + 7))
    m_wx[O - 1] = m_wx[O - 1] * keep_x[0]
    m_wx[O + 3] = m_wx[O + 3] * keep_x[1]
    weights_yz(mid, m_mob, (O - 3, O + 7), keep_y, keep_z)
    diagonals(mid, m_in.at[3], (O - 3, O + 7))

    for at in (FINE_X, FINE_Y, COEF_X, MID_IN):
        sent(at)

    received(MID_F)
    start_sweep(mid, m_src, m_a, (O - 2, O + 6))
    sweep(mid, m_src, m_a, m_b, (O - 1, O + 5))
    left = residual_of(mid, m_src, m_b, own4)
    for ix in range(2):
        fold = left[2 * ix] + left[2 * ix + 1]
        c_src[2 + ix, OWN_C, :] = (fold[0] + fold[1])[pairs4]
    messages = []
    for e in sorted(range(-REACH, REACH + 1), key=lambda e: -abs(e)):
        for g in (1, -1, 0):
            if (g, e) != (0, 0):
                target = c_src.at[2 - 2 * g : 4 - 2 * g, OWN_C.start - 2 * e : OWN_C.stop - 2 * e, :]
                messages.append((c_src.at[2:4, OWN_C, :], target, (g, e)))
    exchange(COARSE_F, messages)

    def keep_mid(x, _):
        m_y[x, :, pairs4] = m_b[x, :, pairs4]
        return 0

    lax.fori_loop(O, O + 4, keep_mid, 0, unroll=True)
    messages = []
    for step in NEIGHBOURS:
        ax, ay, bx, by = spans(*step, 4, 3 if step in corners else 4, 2)
        messages.append((m_y.at[ax, :, ay, :], m_y.at[bx, :, by, :], step))
    exchange(MID_V, messages)

    received(COEF_Y)
    coef = [c_coef[k, :, 8:24, :].reshape(128, 64).T for k in range(4)]
    second_prev = c_coef[2, :, 7:23, :].reshape(128, 64).T
    second_next = c_coef[2, :, 9:25, :].reshape(128, 64).T
    column = lax.broadcasted_iota(jnp.int32, (64, 128), 1)
    level_row = lax.broadcasted_iota(jnp.int32, (64, 128), 0)
    cells = 2 * count_y
    cell = 2 * gy + lax.rem(column, 16) + (cells - 7)
    block = 2 * GROUP
    offset = 4 + cells - (cells // block) * block
    shut_up = (lax.rem(cell + 1 - offset + 2 * block, block) == 0) | (lax.rem(cell + 1, cells) == 0)
    shut_down = (lax.rem(cell - offset + 2 * block, block) == 0) | (lax.rem(cell, cells) == 0)
    up_x = jnp.where(lax.rem(column, 32) < 16, harmonic(coef[1], pltpu.roll(coef[1], 112, 1)), 0.0)
    down_x = pltpu.roll(up_x, 16, 1)
    up_y = jnp.where(shut_up, 0.0, harmonic(coef[2], second_next))
    down_y = jnp.where(shut_down, 0.0, harmonic(second_prev, coef[2]))
    up_z = jnp.where(level_row == 63, 0.0, harmonic(coef[3], next_of(coef[3], 0)))
    down_z = prev_of(up_z, 0)
    main = coef[0] + (up_x + down_x) + (up_y + down_y) + (up_z + down_z)
    for at, band in enumerate((up_x, down_x, up_y, down_y, -down_z, main, -up_z)):
        c_bands[at] = band

    def registers(at):
        return [c_bands[at, pl.ds(place, 8, stride=8), :] for place in range(8)]

    for at in range(4):
        for place, values in enumerate(registers(at)):
            c_weights[at, place] = values
    low, main, high = (registers(at) for at in (4, 5, 6))
    ahead, back = [reciprocal(main[0])], {6: reciprocal(main[6])}
    upto, onfrom = [main[0]], {6: main[6]}
    for i in range(1, 7):
        upto.append(main[i] - low[i] * high[i - 1] * ahead[i - 1])
        ahead.append(reciprocal(upto[i]))
        j = 6 - i
        onfrom[j] = main[j] - high[j] * low[j + 1] * back[j + 1]
        back[j] = reciprocal(onfrom[j])
    rise = [-high[i] * ahead[i] for i in range(7)]
    fall = [-low[i] * back[i] for i in range(7)]
    inverse = {}
    for j in range(7):
        inverse[j, j] = reciprocal(upto[j] + onfrom[j] - main[j])
        for i in range(j - 1, -1, -1):
            inverse[i, j] = rise[i] * inverse[i + 1, j]
        for i in range(j + 1, 7):
            inverse[i, j] = fall[i] * inverse[i - 1, j]
    from_last = [inverse[i, 0] * low[0] for i in range(7)]
    from_own = [inverse[i, 6] * high[6] for i in range(7)]

    def turned(values, by):
        return pltpu.roll(values, by % 8, 0) if by % 8 else values

    face_main = main[7] - low[7] * from_own[6] - high[7] * turned(from_last[0], -1)
    face_low = -low[7] * from_last[6]
    face_high = -high[7] * turned(from_own[0], -1)
    spread_by = {0: jnp.ones((8, 128), jnp.float32)}
    for far in (1, 2, 4):
        over = reciprocal(face_main)
        alpha = -face_low * turned(over, far)
        gamma = -face_high * turned(over, -far)
        face_main = face_main + alpha * turned(face_high, far) + gamma * turned(face_low, -far)
        face_low, face_high = alpha * turned(face_low, far), gamma * turned(face_high, -far)
        wider = dict(spread_by)
        for by, values in spread_by.items():
            for step, factor in ((far, alpha), (-far, gamma)):
                term = factor * turned(values, step)
                key = (by + step) % 8
                wider[key] = wider[key] + term if key in wider else term
        spread_by = wider
    over = reciprocal(face_main)
    own_by = [over * spread_by[by] for by in range(8)]
    next_by = [own_by[(by + 1) % 8] * turned(high[7], by + 1) for by in range(8)]
    for i in range(7):
        for j in range(7):
            c_inverse[7 * i + j] = inverse[i, j]
        c_inverse[49 + i] = from_last[i]
        c_inverse[56 + i] = from_own[i]
    for by in range(8):
        c_inverse[64 + by] = own_by[by]
        c_inverse[72 + by] = next_by[by]
        c_inverse[80 + by] = turned(own_by[by - 1], 1)
        c_inverse[88 + by] = turned(next_by[by - 1], 1)
    c_inverse[63] = low[7]

    def lines(values):
        inner = [total([c_inverse[7 * i + j] * values[j] for j in range(7)]) for i in range(7)]
        face = values[7] - c_inverse[63] * inner[6]
        faces = [turned(face, by) for by in range(8)]
        firsts = [turned(inner[0], by) for by in range(8)]

        def interface(at):
            terms = [c_inverse[at + by] * faces[by] for by in range(8)]
            return total(terms) - total([c_inverse[at + 8 + by] * firsts[by] for by in range(8)])

        here, before = interface(64), interface(80)
        return tuple(inner[i] - (c_inverse[49 + i] * before + c_inverse[56 + i] * here) for i in range(7)) + (here,)

    for at in (COEF_Y, MID_F, FINE_V):
        sent(at)

    received(COARSE_F)
    source = lax.dot_general(
        jnp.concatenate([fold_c] * 2, axis=1),
        jnp.concatenate(pieces(c_src[:, 8:24, :].reshape(128, 128), 2), axis=1),
        (((1,), (1,)), ((), ())),
        preferred_element_type=jnp.float32,
    )
    sources = [source[8 * place : 8 * place + 8] for place in range(8)]

    def turn(_, z):
        pushed = []
        for place in range(8):
            own = z[place]
            along_x = c_weights[0, place] * pltpu.roll(own, 112, 1) + c_weights[1, place] * pltpu.roll(own, 16, 1)
            along_y = c_weights[2, place] * next_of(own, 1) + c_weights[3, place] * prev_of(own, 1)
            pushed.append(sources[place] + (along_x + along_y))
        return lines(pushed)

    z = lax.fori_loop(0, KC - 1, turn, lines(sources))
    c_ext[...] = times_one_hot(jnp.concatenate(z, axis=0).T[0:96], fold_c, 2).reshape(6, 16, 128)

    received(MID_V)

    def raise_mid(x, _):
        rows = c_ext[x, 5:13, :]
        for along in range(2):
            for parity in range(2):
                m_a[2 * x + along, parity] = m_y[2 * x + along, parity] + rows
        return 0

    lax.fori_loop(0, 6, raise_mid, 0, unroll=True)
    sweep(mid, m_src, m_a, m_b, (O - 3, O + 7))
    sweep(mid, m_src, m_b, m_a, (O - 2, O + 6))

    received(FINE_V)

    def raise_fine(x, _):
        for parity in range(2):
            m_fold[x, pl.ds(parity, 4, stride=2), :] = m_a[O - 2 + x, parity, 1:5]
        rows = m_fold[x]
        for along in range(2):
            for parity in range(2):
                for half in range(2):
                    at = (2 * x + along, parity, half)
                    f_a[at] = f_x[at] + rows
        return 0

    lax.fori_loop(0, 8, raise_fine, 0, unroll=True)
    sweep(fine, f_src, f_a, f_b, (O - 2, O + 10))
    sweep(fine, f_src, f_b, f_a, (O - 1, O + 9))


    def in_order(field, result):
        def sort_back(x, _):
            for parity in range(2):
                for half in range(2):
                    f_rows[half, x, pl.ds(parity, 8, stride=2), :] = field[O + x, parity, half]
            return 0

        lax.fori_loop(0, 8, sort_back, 0, unroll=True)
        halves = [f_rows[half, :, O : O + 8, :].reshape(64, 128) for half in range(2)]
        result[...] = times_one_hot(jnp.concatenate(halves, axis=1), together[...], 2).reshape(8, 8, 256)

    in_order(f_a, pressure)

    for x in blocks(fine, (O, O + 8)):
        f_b[x] = residual_of(fine, f_src, f_a, x)
    in_order(f_b, residual)
    for at in (COARSE_F, MID_V):
        sent(at)


def publish(pressure, residual, pressure_h, residual_h, sem):
    copies = [
        pltpu.make_async_copy(pressure, pressure_h, sem.at[0]),
        pltpu.make_async_copy(residual, residual_h, sem.at[1]),
    ]
    for copy in copies:
        copy.start()
    for copy in copies:
        copy.wait()


def local(pressure_rhs, storage_fine, mobility_fine, storage_mid, mobility_mid, storage_coarse, mobility_coarse):
    count_x = lax.axis_size("gx")
    count_y = lax.axis_size("gy")
    f32 = jnp.float32
    fine = pltpu.VMEM((8 + 2 * O, 2, 2, 8, 128), f32)
    mid = pltpu.VMEM((4 + 2 * O, 2, 8, 128), f32)
    in_hbm = pl.BlockSpec(memory_space=pltpu.HBM)
    in_vmem = pl.BlockSpec(memory_space=pltpu.VMEM)
    arrays = (pressure_rhs, storage_fine, mobility_fine, storage_mid, mobility_mid, storage_coarse, mobility_coarse)
    result = pl.pallas_call(
        functools.partial(kernel, count_x, count_y),
        out_shape=(pltpu.VMEM(pressure_rhs.shape, f32),) * 2,
        in_specs=[in_hbm] * 7,
        out_specs=(in_vmem, in_vmem),
        scratch_shapes=[
            pltpu.VMEM((5, 8, 8, 256), f32),
            pltpu.VMEM((2, 40, 8, 128), f32),
            pltpu.VMEM((5, 8 + 2 * O, 2, 2, 8, 128), f32),
            *[fine] * 10,
            pltpu.VMEM((4, 4 + 2 * O, 2, 8, 128), f32),
            *[mid] * 11,
            pltpu.VMEM((8, 8, 128), f32),
            pltpu.VMEM((2, 8, 16, 128), f32),
            pltpu.VMEM((256, 256), jnp.bfloat16),
            pltpu.VMEM((4, 8, 32, 64), f32),
            pltpu.VMEM((8, 32, 128), f32),
            pltpu.VMEM((6, 16, 128), f32),
            pltpu.VMEM((4, 8, 8, 128), f32),
            pltpu.VMEM((7, 64, 128), f32),
            pltpu.VMEM((97, 8, 128), f32),
            pltpu.VMEM((1024, 128), f32),
            pltpu.VMEM((4096, 128), f32),
            pltpu.VMEM((4, 2, 2, 64), f32),
            pltpu.SemaphoreType.DMA((16,)),
            pltpu.SemaphoreType.DMA((EXCHANGES,)),
            pltpu.SemaphoreType.DMA((EXCHANGES,)),
        ],
        compiler_params=pltpu.CompilerParams(
            collective_id=0, has_side_effects=True, vmem_limit_bytes=32 * 1024 * 1024
        ),
    )(*[pltpu.with_memory_space_constraint(array, pltpu.HBM) for array in arrays])
    out = jax.ShapeDtypeStruct(pressure_rhs.shape, f32)
    return pl.pallas_call(
        publish,
        out_shape=(out, out),
        in_specs=[in_vmem] * 2,
        out_specs=(in_hbm, in_hbm),
        scratch_shapes=[pltpu.SemaphoreType.DMA((2,))],
        compiler_params=pltpu.CompilerParams(vmem_limit_bytes=16 * 1024 * 1024),
    )(*result)


def solution(mesh):
    placed = (
        P("gx", "gy", None),
        P("gx", "gy", None),
        P(None, "gx", "gy", None),
        P("gx", "gy", None),
        P(None, "gx", "gy", None),
        P("gx", "gy", None),
        P(None, "gx", "gy", None),
    )
    return jax.shard_map(
        local,
        mesh=mesh,
        in_specs=placed,
        out_specs=(P("gx", "gy", None), P("gx", "gy", None)),
        check_vma=False,
    )
```

```python
import functools

import jax
import jax.numpy as jnp
from jax import lax
from jax.experimental import pallas as pl
from jax.experimental.pallas import tpu as pltpu
from jax.sharding import PartitionSpec as P

KC = 6
GROUP = 8
REACH = 4
DAMPING = 2.0 / 3.0

MESH = pl.DeviceIdType.MESH

O = 4
OP = 2
M0, M2, STORE, SOURCE, M1 = range(5)
OWN_C = slice(15, 17)
FINE_X, FINE_Y, COEF_X, COEF_Y, MID_IN, MID_F, FINE_V, COARSE_F, MID_V, MID_OUT = range(10)
EXCHANGES = 10
NEIGHBOURS = ((1, 0), (-1, 0), (1, 1), (1, -1), (-1, 1), (-1, -1), (0, 1), (0, -1))


def reciprocal(values):
    guess = pl.reciprocal(values, approx=True)
    return guess * (2.0 - values * guess)


def harmonic(left, right):
    return 2.0 * left * right * reciprocal(left + right)


def next_of(values, axis):
    return pltpu.roll(values, values.shape[axis] - 1, axis)


def prev_of(values, axis):
    return pltpu.roll(values, 1, axis)


def next_paired(values, axis, pairs):
    first, second = lax.slice_in_dim(values, 0, 1, axis=axis), lax.slice_in_dim(values, 1, 2, axis=axis)
    return jnp.concatenate([second, next_of(first, pairs)], axis=axis)


def prev_paired(values, axis, pairs):
    first, second = lax.slice_in_dim(values, 0, 1, axis=axis), lax.slice_in_dim(values, 1, 2, axis=axis)
    return jnp.concatenate([prev_of(second, pairs), first], axis=axis)


def next_y(values):
    return next_paired(values, 1, values.ndim - 2)


def prev_y(values):
    return prev_paired(values, 1, values.ndim - 2)


def next_z(values):
    return next_paired(values, 2, 4) if values.ndim == 5 else next_of(values, 3)


def prev_z(values):
    return prev_paired(values, 2, 4) if values.ndim == 5 else prev_of(values, 3)


def blocks(level, rows):
    first, last = rows
    most = 4 if len(level[0].shape) == 5 else 6
    count = -(-(last - first) // most)
    edges = [first + (last - first) * at // count for at in range(count + 1)]
    return [slice(*pair) for pair in zip(edges[:-1], edges[1:])]


def moved(rows, by):
    return slice(rows.start + by, rows.stop + by)


def one_hot(shape, test):
    row = lax.broadcasted_iota(jnp.int32, shape, 0)
    column = lax.broadcasted_iota(jnp.int32, shape, 1)
    return jnp.where(test(row, column), 1.0, 0.0).astype(jnp.bfloat16)


def pieces(values, count):
    parts = []
    for _ in range(count - 1):
        parts.append(values.astype(jnp.bfloat16))
        values = values - parts[-1].astype(jnp.float32)
    return parts + [values.astype(jnp.bfloat16)]


def times_one_hot(values, matrix, count):
    rows = values.shape[0]
    product = jnp.dot(jnp.concatenate(pieces(values, count), axis=0), matrix, preferred_element_type=jnp.float32)
    return total([product[at * rows : (at + 1) * rows] for at in range(count)])


def total(terms):
    while len(terms) > 1:
        pairs = [terms[i] + terms[i + 1] for i in range(0, len(terms) - 1, 2)]
        terms = pairs + terms[len(terms) - len(terms) % 2 :]
    return terms[0]


def source_span(step, first, n, width):
    return slice(first + n - width, first + n) if step > 0 else slice(first, first + (width if step < 0 else n))


def target_span(step, first, n, width):
    if step > 0:
        return slice(first - width, first)
    return slice(first + n, first + n + width) if step < 0 else slice(first, first + n)


def weights_x(level, mob, rows):
    for x in blocks(level, rows):
        level[0][x] = harmonic(mob[0][x], mob[0][moved(x, 1)])


def weights_yz(level, mob, rows, keep_y, keep_z):
    wx, wyu, wyd, wzu, wzd, diag, damp = level
    for x in blocks(level, rows):
        second = mob[1][x]
        up_y = harmonic(second, next_y(second)) * keep_y
        wyu[x] = up_y
        wyd[x] = prev_y(up_y)
        third = mob[2][x]
        up_z = harmonic(third, next_z(third)) * keep_z
        wzu[x] = up_z
        wzd[x] = prev_z(up_z)


def diagonals(level, store, rows):
    wx, wyu, wyd, wzu, wzd, diag, damp = level
    for x in blocks(level, rows):
        all_of_it = store[x] + (wx[x] + wx[moved(x, -1)]) + (wyu[x] + wyd[x]) + (wzu[x] + wzd[x])
        diag[x] = all_of_it
        damp[x] = DAMPING * reciprocal(all_of_it)


def residual_of(level, source, field, x):
    wx, wyu, wyd, wzu, wzd, diag, damp = level
    v = field[x]
    left = source[x] - diag[x] * v
    left = left + (wx[x] * field[moved(x, 1)] + wx[moved(x, -1)] * field[moved(x, -1)])
    left = left + (wyu[x] * next_y(v) + wyd[x] * prev_y(v))
    return left + (wzu[x] * next_z(v) + wzd[x] * prev_z(v))


def sweep(level, source, field, result, rows):
    damp = level[6]
    for x in blocks(level, rows):
        result[x] = field[x] + damp[x] * residual_of(level, source, field, x)


def start_sweep(level, source, result, rows):
    damp = level[6]
    for x in blocks(level, rows):
        result[x] = damp[x] * source[x]


def kernel(
    count_x,
    count_y,
    rhs_h,
    store_f_h,
    mob_f_h,
    store_m_h,
    mob_m_h,
    store_c_h,
    mob_c_h,
    pressure,
    residual,
    f_stage,
    f_mixed,
    f_in,
    f_wx,
    f_wyu,
    f_wyd,
    f_wzu,
    f_wzd,
    f_diag,
    f_damp,
    f_a,
    f_b,
    f_x,
    m_in,
    m_wide,
    m_src,
    m_wx,
    m_wyu,
    m_wyd,
    m_wzu,
    m_wzd,
    m_diag,
    m_damp,
    m_a,
    m_b,
    m_y,
    m_fold,
    f_rows,
    together,
    c_coef,
    c_src,
    c_ext,
    c_weights,
    c_bands,
    c_inverse,
    meter,
    spare,
    c_spare,
    local_sem,
    send_sem,
    recv_sem,
):
    gx = lax.axis_index("gx")
    gy = lax.axis_index("gy")

    def stepped(at, step, count):
        to = at + step
        if step > 0:
            return jnp.where(to >= count, to - count, to)
        return jnp.where(to < 0, to + count, to) if step < 0 else at

    along_gx = {step: stepped(gx, step, count_x) for step in (-1, 0, 1)}
    along_gy = {step: stepped(gy, step, count_y) for step in range(-REACH, REACH + 1)}

    def beside(sx, sy):
        return {"gx": along_gx[sx], "gy": along_gy[sy]}

    def ahead_of(sx):
        return gx < count_x - 1 if sx > 0 else gx > 0

    barrier = pltpu.get_barrier_semaphore()

    def greet(steps):
        for step in steps:
            pl.semaphore_signal(barrier, inc=1, device_id=beside(*step), device_id_type=MESH)

    for side in (1, -1):

        @pl.when(ahead_of(side))
        def _():
            greet([step for step in NEIGHBOURS if step[0] == side])

    straight = [(0, e) for e in range(-REACH, REACH + 1) if e != 0]
    greet(straight)
    partners = len(straight) + jnp.where(gx > 0, 3, 0) + jnp.where(gx < count_x - 1, 3, 0)

    c_coef[:, 6:8] = jnp.ones((4, 2, 32, 64), jnp.float32)
    c_src[6:8] = jnp.zeros((2, 32, 128), jnp.float32)

    locals_ = []

    def bring(source, target):
        copy = pltpu.make_async_copy(source, target, local_sem.at[len(locals_)])
        copy.start()
        locals_.append(copy)
        return copy

    def exchange(at, messages):
        sizes = []
        for source, _, _ in messages:
            rows = 1
            for size in source.shape[:-1]:
                rows = rows * size
            sizes.append(rows)
        rows_of[at] = rows_of.get(at, 0) + sum(sizes)

        def send(side):
            for source, target, step in messages:
                if step[0] == side:
                    pltpu.make_async_remote_copy(
                        src_ref=source,
                        dst_ref=target,
                        send_sem=send_sem.at[at],
                        recv_sem=recv_sem.at[at],
                        device_id=beside(*step),
                        device_id_type=MESH,
                    ).start()

        for side in (1, -1):
            rows = sum(size for size, message in zip(sizes, messages) if message[2][0] == side)
            if rows == 0:
                continue
            first = spent[0]
            spent[0] += rows

            @pl.when(ahead_of(side))
            def _():
                send(side)

            @pl.when(jnp.logical_not(ahead_of(side)))
            def _():
                if at == COEF_X:
                    pltpu.make_async_copy(c_coef.at[:, 2:4, OWN_C, :], c_spare, send_sem.at[at]).start()
                else:
                    spare_to = spare.at[first : first + rows, :]
                    pltpu.make_async_copy(meter.at[0:rows, :], spare_to, send_sem.at[at]).start()

            @pl.when(jnp.logical_not(ahead_of(-side)))
            def _():
                for source, target, step in messages:
                    if step[0] == side:
                        pltpu.make_async_copy(source, target, recv_sem.at[at]).start()

        send(0)

    spent = [0]
    rows_of = {}

    def all_of(at):
        if at == COEF_X:
            return c_coef.at[:, 0:4, 0:2, :]
        if at == COEF_Y:
            return c_coef.at[:, 0:6, 0:16, :]
        return meter.at[0 : rows_of[at], :]

    def received(at):
        pltpu.make_async_copy(all_of(at), all_of(at), recv_sem.at[at]).wait()

    def sent(at):
        pltpu.make_async_copy(all_of(at), all_of(at), send_sem.at[at]).wait()

    own8, pairs8 = slice(O, O + 8), slice(OP, OP + 4)
    own4, pairs4 = slice(O, O + 4), slice(OP, OP + 2)
    fine_in = [
        bring(mob_f_h, f_stage.at[0:3]),
        bring(store_f_h, f_stage.at[3]),
        bring(rhs_h, f_stage.at[4]),
    ]
    coarse_in = [
        bring(store_c_h, c_coef.at[0, 2:4, OWN_C, :]),
        bring(mob_c_h, c_coef.at[1:4, 2:4, OWN_C, :]),
    ]
    mid_in = []
    for y in range(4):
        parity, pair = y % 2, OP + y // 2
        mid_in.append(bring(mob_m_h.at[:, :, y, :], m_in.at[0:3, own4, parity, pair, :]))
        mid_in.append(bring(store_m_h.at[:, y, :], m_in.at[3, own4, parity, pair, :]))
    f_src = f_in.at[SOURCE]

    def spans(sx, sy, n, wide_x, wide_y):
        return (
            source_span(sx, O, n, wide_x),
            source_span(sy, OP, n // 2, wide_y),
            target_span(sx, O, n, wide_x),
            target_span(sy, OP, n // 2, wide_y),
        )

    faces_x = [step for step in NEIGHBOURS if step[1] == 0]
    faces_y = [step for step in NEIGHBOURS if step[0] == 0]
    corners = [step for step in NEIGHBOURS if step[0] != 0 and step[1] != 0]

    apart = one_hot((256, 256), lambda row, column: row == 2 * (column % 128) + column // 128)
    for copy in fine_in:
        copy.wait()
    sorted_z = times_one_hot(f_stage[...].reshape(320, 256), apart, 2)
    for half in range(2):
        f_mixed[half] = sorted_z[:, 128 * half : 128 * half + 128].reshape(40, 8, 128)

    def sort_y(x, _):
        for at, to in enumerate((M0, M1, M2, STORE, SOURCE)):
            for parity in range(2):
                for half in range(2):
                    rows = f_mixed[half, 8 * at + x, pl.ds(parity, 4, stride=2), :]
                    f_in[to, O + x, parity, half, pairs8] = rows
        return 0

    lax.fori_loop(0, 8, sort_y, 0, unroll=True)
    pl.semaphore_wait(barrier, partners)

    def part(first, last, step, wide_x, wide_y, parity=slice(0, 2)):
        fields = slice(first, last + 1)
        ax, ay, bx, by = spans(*step, 8, wide_x, wide_y)
        return (f_in.at[fields, ax, parity, :, ay, :], f_in.at[fields, bx, parity, :, by, :], step)

    for copy in coarse_in:
        copy.wait()
    exchange(
        COEF_X,
        [
            (c_coef.at[:, 2:4, OWN_C, :], c_coef.at[:, 2 - 2 * sx : 4 - 2 * sx, OWN_C, :], (sx, sy))
            for sx, sy in faces_x
        ],
    )

    messages = []
    for step in faces_x:
        messages += [part(M0, M0, step, 3, 1), part(M2, M1, step, 2, 1)]
    for step in corners:
        nearest = slice(1, 2) if step[1] > 0 else slice(0, 1)
        messages += [part(M0, M0, step, 2, 1), part(M1, M1, step, 2, 1), part(M2, SOURCE, step, 1, 1, nearest)]
    exchange(FINE_X, messages)
    messages = []
    for step in faces_y:
        messages += [part(M0, SOURCE, step, 1, 1), part(M1, M1, step, 1, 2)]
    exchange(FINE_Y, messages)

    for copy in mid_in:
        copy.wait()
    messages = []

    def without(span, step, beyond):
        return slice(span.start, span.stop - beyond) if step > 0 else slice(span.start + beyond, span.stop)

    def mid_part(first, last, step, wide_x, wide_y, beyond_x=0, beyond_y=0):
        fields = slice(first, last + 1)
        ax, ay, bx, by = spans(*step, 4, wide_x, wide_y)
        if beyond_x:
            ax, bx = without(ax, step[0], beyond_x), without(bx, step[0], beyond_x)
        if beyond_y:
            ay, by = without(ay, step[1], beyond_y), without(by, step[1], beyond_y)
        landing = m_wide if beyond_x or beyond_y else m_in
        if landing is m_wide:
            late.append((fields, bx, slice(0, 2), by))
        return (m_in.at[fields, ax, :, ay, :], landing.at[fields, bx, :, by, :], step)

    late = []
    outer = []
    for step in faces_x:
        messages += [mid_part(0, 0, step, 3, 1), mid_part(1, 3, step, 2, 1)]
        outer += [mid_part(0, 0, step, 4, 1, 3), mid_part(1, 3, step, 3, 1, 2)]
    for step in corners:
        messages += [mid_part(0, 1, step, 2, 1), mid_part(2, 3, step, 1, 1)]
        outer += [mid_part(0, 1, step, 3, 1, 2), mid_part(0, 1, step, 1, 2, 0, 1), mid_part(2, 3, step, 2, 1, 1)]
    for step in faces_y:
        messages.append(mid_part(0, 3, step, 4, 2))
    exchange(MID_IN, messages)

    one = jnp.float32(1.0)
    nil = jnp.float32(0.0)
    keep_x = (jnp.where(gx == 0, nil, one), jnp.where(gx == count_x - 1, nil, one))

    def keep_yz(own, shape):
        def index(axis):
            return lax.broadcasted_iota(jnp.int32, shape, axis)

        parity, pair, lane = index(0), index(len(shape) - 2), index(len(shape) - 1)
        end = jnp.where(gy == 0, OP - 1, -1)
        other = jnp.where(gy == count_y - 1, OP + own // 2 - 1, -1)
        keep_y = jnp.where((parity == 1) & ((pair == end) | (pair == other)), 0.0, 1.0)
        last_z = (lane == 127) if len(shape) == 3 else (lane == 127) & (index(1) == 1)
        return keep_y, jnp.where(last_z, 0.0, 1.0)

    together[...] = one_hot((256, 256), lambda row, column: column == 2 * (row % 128) + row // 128)
    fold_c = one_hot((64, 128), lambda row, column: row // 8 + 8 * (row % 8) == column // 2)

    fine = (f_wx, f_wyu, f_wyd, f_wzu, f_wzd, f_diag, f_damp)
    f_mob = (f_in.at[M0], f_in.at[M1], f_in.at[M2])
    f_store = f_in.at[STORE]
    keep_y, keep_z = keep_yz(8, (2, 2, 8, 128))
    received(FINE_Y)
    weights_yz(fine, f_mob, (O, O + 8), keep_y, keep_z)
    weights_x(fine, f_mob, (O, O + 7))
    diagonals(fine, f_store, (O + 1, O + 7))
    start_sweep(fine, f_src, f_a, (O + 1, O + 7))
    received(COEF_X)
    messages = []
    for step in straight:
        target = c_coef.at[:, 0:6, OWN_C.start - 2 * step[1] : OWN_C.stop - 2 * step[1], :]
        messages.append((c_coef.at[:, 0:6, OWN_C, :], target, step))
    exchange(COEF_Y, messages)
    sweep(fine, f_src, f_a, f_b, (O + 2, O + 6))
    received(FINE_X)
    for rows in ((O - 3, O), (O + 7, O + 10)):
        weights_x(fine, f_mob, rows)
    f_wx[O - 1] = f_wx[O - 1] * keep_x[0]
    f_wx[O + 7] = f_wx[O + 7] * keep_x[1]
    for rows in ((O - 2, O), (O + 8, O + 10)):
        weights_yz(fine, f_mob, rows, keep_y, keep_z)
    for rows in ((O - 2, O + 1), (O + 7, O + 10)):
        diagonals(fine, f_store, rows)
        start_sweep(fine, f_src, f_a, rows)
    for rows in ((O - 1, O + 2), (O + 6, O + 9)):
        sweep(fine, f_src, f_a, f_b, rows)

    for x in blocks(fine, (O, O + 8)):
        left = residual_of(fine, f_src, f_b, x)
        for pair in range(2):
            both = left[2 * pair] + left[2 * pair + 1]
            m_fold[(x.start - O) // 2 + pair] = (both[0, 0] + both[0, 1]) + (both[1, 0] + both[1, 1])
    for x in range(4):
        for parity in range(2):
            m_src[O + x, parity, pairs4] = m_fold[x, pl.ds(OP + parity, 2, stride=2), :]
    messages = []
    for step in NEIGHBOURS:
        ax, ay, bx, by = spans(*step, 4, 2 if step in corners else 3, 1 if step in corners else 2)
        messages.append((m_src.at[ax, :, ay, :], m_src.at[bx, :, by, :], step))
    exchange(MID_F, messages)
    exchange(MID_OUT, outer)

    def keep_fine(x, _):
        f_x[x, :, :, pairs8] = f_b[x, :, :, pairs8]
        return 0

    lax.fori_loop(O, O + 8, keep_fine, 0, unroll=True)
    messages = []
    for step in NEIGHBOURS:
        ax, ay, bx, by = spans(*step, 8, 2 if step in corners else 3, 1 if step in corners else 2)
        messages.append((f_x.at[ax, :, :, ay, :], f_x.at[bx, :, :, by, :], step))
    exchange(FINE_V, messages)

    mid = (m_wx, m_wyu, m_wyd, m_wzu, m_wzd, m_diag, m_damp)
    m_mob = (m_in.at[0], m_in.at[1], m_in.at[2])
    keep_y, keep_z = keep_yz(4, (2, 8, 128))

    def mid_weights(reach):
        weights_x(mid, m_mob, (O - 1 - reach, O + 4 + reach))
        m_wx[O - 1] = m_wx[O - 1] * keep_x[0]
        m_wx[O + 3] = m_wx[O + 3] * keep_x[1]
        weights_yz(mid, m_mob, (O - reach, O + 4 + reach), keep_y, keep_z)
        diagonals(mid, m_in.at[3], (O - reach, O + 4 + reach))

    received(MID_IN)
    mid_weights(2)
    for at in (FINE_X, FINE_Y, COEF_X, MID_IN):
        sent(at)

    received(MID_F)
    start_sweep(mid, m_src, m_a, (O - 2, O + 6))
    sweep(mid, m_src, m_a, m_b, (O - 1, O + 5))
    left = residual_of(mid, m_src, m_b, own4)
    for ix in range(2):
        fold = left[2 * ix] + left[2 * ix + 1]
        c_src[2 + ix, OWN_C, :] = (fold[0] + fold[1])[pairs4]
    messages = []
    for e in sorted(range(-REACH, REACH + 1), key=lambda e: -abs(e)):
        for g in (1, -1, 0):
            if (g, e) != (0, 0):
                target = c_src.at[2 - 2 * g : 4 - 2 * g, OWN_C.start - 2 * e : OWN_C.stop - 2 * e, :]
                messages.append((c_src.at[2:4, OWN_C, :], target, (g, e)))
    exchange(COARSE_F, messages)

    def keep_mid(x, _):
        m_y[x, :, pairs4] = m_b[x, :, pairs4]
        return 0

    lax.fori_loop(O, O + 4, keep_mid, 0, unroll=True)
    messages = []
    for step in NEIGHBOURS:
        ax, ay, bx, by = spans(*step, 4, 3 if step in corners else 4, 2)
        messages.append((m_y.at[ax, :, ay, :], m_y.at[bx, :, by, :], step))
    exchange(MID_V, messages)

    received(COEF_Y)
    coef = [c_coef[k, :, 8:24, :].reshape(128, 64).T for k in range(4)]
    second_prev = c_coef[2, :, 7:23, :].reshape(128, 64).T
    second_next = c_coef[2, :, 9:25, :].reshape(128, 64).T
    column = lax.broadcasted_iota(jnp.int32, (64, 128), 1)
    level_row = lax.broadcasted_iota(jnp.int32, (64, 128), 0)
    cells = 2 * count_y
    cell = 2 * gy + lax.rem(column, 16) + (cells - 7)
    block = 2 * GROUP
    offset = 4 + cells - (cells // block) * block
    shut_up = (lax.rem(cell + 1 - offset + 2 * block, block) == 0) | (lax.rem(cell + 1, cells) == 0)
    shut_down = (lax.rem(cell - offset + 2 * block, block) == 0) | (lax.rem(cell, cells) == 0)
    up_x = jnp.where(lax.rem(column, 32) < 16, harmonic(coef[1], pltpu.roll(coef[1], 112, 1)), 0.0)
    down_x = pltpu.roll(up_x, 16, 1)
    up_y = jnp.where(shut_up, 0.0, harmonic(coef[2], second_next))
    down_y = jnp.where(shut_down, 0.0, harmonic(second_prev, coef[2]))
    up_z = jnp.where(level_row == 63, 0.0, harmonic(coef[3], next_of(coef[3], 0)))
    down_z = prev_of(up_z, 0)
    main = coef[0] + (up_x + down_x) + (up_y + down_y) + (up_z + down_z)
    for at, band in enumerate((up_x, down_x, up_y, down_y, -down_z, main, -up_z)):
        c_bands[at] = band

    def registers(at):
        return [c_bands[at, pl.ds(place, 8, stride=8), :] for place in range(8)]

    for at in range(4):
        for place, values in enumerate(registers(at)):
            c_weights[at, place] = values
    low, main, high = (registers(at) for at in (4, 5, 6))
    ahead, back = [reciprocal(main[0])], {6: reciprocal(main[6])}
    upto, onfrom = [main[0]], {6: main[6]}
    for i in range(1, 7):
        upto.append(main[i] - low[i] * high[i - 1] * ahead[i - 1])
        ahead.append(reciprocal(upto[i]))
        j = 6 - i
        onfrom[j] = main[j] - high[j] * low[j + 1] * back[j + 1]
        back[j] = reciprocal(onfrom[j])
    rise = [-high[i] * ahead[i] for i in range(7)]
    fall = [-low[i] * back[i] for i in range(7)]
    inverse = {}
    for j in range(7):
        inverse[j, j] = reciprocal(upto[j] + onfrom[j] - main[j])
        for i in range(j - 1, -1, -1):
            inverse[i, j] = rise[i] * inverse[i + 1, j]
        for i in range(j + 1, 7):
            inverse[i, j] = fall[i] * inverse[i - 1, j]
    from_last = [inverse[i, 0] * low[0] for i in range(7)]
    from_own = [inverse[i, 6] * high[6] for i in range(7)]

    def turned(values, by):
        return pltpu.roll(values, by % 8, 0) if by % 8 else values

    face_main = main[7] - low[7] * from_own[6] - high[7] * turned(from_last[0], -1)
    face_low = -low[7] * from_last[6]
    face_high = -high[7] * turned(from_own[0], -1)
    spread_by = {0: jnp.ones((8, 128), jnp.float32)}
    for far in (1, 2, 4):
        over = reciprocal(face_main)
        alpha = -face_low * turned(over, far)
        gamma = -face_high * turned(over, -far)
        face_main = face_main + alpha * turned(face_high, far) + gamma * turned(face_low, -far)
        face_low, face_high = alpha * turned(face_low, far), gamma * turned(face_high, -far)
        wider = dict(spread_by)
        for by, values in spread_by.items():
            for step, factor in ((far, alpha), (-far, gamma)):
                term = factor * turned(values, step)
                key = (by + step) % 8
                wider[key] = wider[key] + term if key in wider else term
        spread_by = wider
    over = reciprocal(face_main)
    own_by = [over * spread_by[by] for by in range(8)]
    next_by = [own_by[(by + 1) % 8] * turned(high[7], by + 1) for by in range(8)]
    for i in range(7):
        for j in range(7):
            c_inverse[7 * i + j] = inverse[i, j]
        c_inverse[49 + i] = from_last[i]
        c_inverse[56 + i] = from_own[i]
    for by in range(8):
        c_inverse[64 + by] = own_by[by]
        c_inverse[72 + by] = next_by[by]
        c_inverse[80 + by] = turned(own_by[by - 1], 1)
        c_inverse[88 + by] = turned(next_by[by - 1], 1)
    c_inverse[63] = low[7]

    def lines(values):
        inner = [total([c_inverse[7 * i + j] * values[j] for j in range(7)]) for i in range(7)]
        face = values[7] - c_inverse[63] * inner[6]
        faces = [turned(face, by) for by in range(8)]
        firsts = [turned(inner[0], by) for by in range(8)]

        def interface(at):
            terms = [c_inverse[at + by] * faces[by] for by in range(8)]
            return total(terms) - total([c_inverse[at + 8 + by] * firsts[by] for by in range(8)])

        here, before = interface(64), interface(80)
        return tuple(inner[i] - (c_inverse[49 + i] * before + c_inverse[56 + i] * here) for i in range(7)) + (here,)

    received(MID_OUT)
    for region in late:
        m_in[region] = m_wide[region]
    mid_weights(3)
    for at in (COEF_Y, MID_F, FINE_V, MID_OUT):
        sent(at)

    received(COARSE_F)
    source = lax.dot_general(
        jnp.concatenate([fold_c] * 2, axis=1),
        jnp.concatenate(pieces(c_src[:, 8:24, :].reshape(128, 128), 2), axis=1),
        (((1,), (1,)), ((), ())),
        preferred_element_type=jnp.float32,
    )
    sources = [source[8 * place : 8 * place + 8] for place in range(8)]

    def turn(_, z):
        pushed = []
        for place in range(8):
            own = z[place]
            along_x = c_weights[0, place] * pltpu.roll(own, 112, 1) + c_weights[1, place] * pltpu.roll(own, 16, 1)
            along_y = c_weights[2, place] * next_of(own, 1) + c_weights[3, place] * prev_of(own, 1)
            pushed.append(sources[place] + (along_x + along_y))
        return lines(pushed)

    z = lax.fori_loop(0, KC - 1, turn, lines(sources))
    c_ext[...] = times_one_hot(jnp.concatenate(z, axis=0).T[0:96], fold_c, 2).reshape(6, 16, 128)

    received(MID_V)

    def raise_mid(x, _):
        rows = c_ext[x, 5:13, :]
        for along in range(2):
            for parity in range(2):
                m_a[2 * x + along, parity] = m_y[2 * x + along, parity] + rows
        return 0

    lax.fori_loop(0, 6, raise_mid, 0, unroll=True)
    sweep(mid, m_src, m_a, m_b, (O - 3, O + 7))
    sweep(mid, m_src, m_b, m_a, (O - 2, O + 6))

    received(FINE_V)

    def raise_fine(x, _):
        for parity in range(2):
            m_fold[x, pl.ds(parity, 4, stride=2), :] = m_a[O - 2 + x, parity, 1:5]
        rows = m_fold[x]
        for along in range(2):
            for parity in range(2):
                for half in range(2):
                    at = (2 * x + along, parity, half)
                    f_a[at] = f_x[at] + rows
        return 0

    lax.fori_loop(0, 8, raise_fine, 0, unroll=True)
    sweep(fine, f_src, f_a, f_b, (O - 2, O + 10))
    sweep(fine, f_src, f_b, f_a, (O - 1, O + 9))


    def in_order(field, result):
        def sort_back(x, _):
            for parity in range(2):
                for half in range(2):
                    f_rows[half, x, pl.ds(parity, 8, stride=2), :] = field[O + x, parity, half]
            return 0

        lax.fori_loop(0, 8, sort_back, 0, unroll=True)
        halves = [f_rows[half, :, O : O + 8, :].reshape(64, 128) for half in range(2)]
        result[...] = times_one_hot(jnp.concatenate(halves, axis=1), together[...], 2).reshape(8, 8, 256)

    in_order(f_a, pressure)

    for x in blocks(fine, (O, O + 8)):
        f_b[x] = residual_of(fine, f_src, f_a, x)
    in_order(f_b, residual)
    for at in (COARSE_F, MID_V):
        sent(at)


def publish(pressure, residual, pressure_h, residual_h, sem):
    copies = [
        pltpu.make_async_copy(pressure, pressure_h, sem.at[0]),
        pltpu.make_async_copy(residual, residual_h, sem.at[1]),
    ]
    for copy in copies:
        copy.start()
    for copy in copies:
        copy.wait()


def local(pressure_rhs, storage_fine, mobility_fine, storage_mid, mobility_mid, storage_coarse, mobility_coarse):
    count_x = lax.axis_size("gx")
    count_y = lax.axis_size("gy")
    f32 = jnp.float32
    fine = pltpu.VMEM((8 + 2 * O, 2, 2, 8, 128), f32)
    mid = pltpu.VMEM((4 + 2 * O, 2, 8, 128), f32)
    in_hbm = pl.BlockSpec(memory_space=pltpu.HBM)
    in_vmem = pl.BlockSpec(memory_space=pltpu.VMEM)
    arrays = (pressure_rhs, storage_fine, mobility_fine, storage_mid, mobility_mid, storage_coarse, mobility_coarse)
    result = pl.pallas_call(
        functools.partial(kernel, count_x, count_y),
        out_shape=(pltpu.VMEM(pressure_rhs.shape, f32),) * 2,
        in_specs=[in_hbm] * 7,
        out_specs=(in_vmem, in_vmem),
        scratch_shapes=[
            pltpu.VMEM((5, 8, 8, 256), f32),
            pltpu.VMEM((2, 40, 8, 128), f32),
            pltpu.VMEM((5, 8 + 2 * O, 2, 2, 8, 128), f32),
            *[fine] * 10,
            pltpu.VMEM((4, 4 + 2 * O, 2, 8, 128), f32),
            pltpu.VMEM((4, 4 + 2 * O, 2, 8, 128), f32),
            *[mid] * 11,
            pltpu.VMEM((8, 8, 128), f32),
            pltpu.VMEM((2, 8, 16, 128), f32),
            pltpu.VMEM((256, 256), jnp.bfloat16),
            pltpu.VMEM((4, 8, 32, 64), f32),
            pltpu.VMEM((8, 32, 128), f32),
            pltpu.VMEM((6, 16, 128), f32),
            pltpu.VMEM((4, 8, 8, 128), f32),
            pltpu.VMEM((7, 64, 128), f32),
            pltpu.VMEM((97, 8, 128), f32),
            pltpu.VMEM((1024, 128), f32),
            pltpu.VMEM((4096, 128), f32),
            pltpu.VMEM((4, 2, 2, 64), f32),
            pltpu.SemaphoreType.DMA((16,)),
            pltpu.SemaphoreType.DMA((EXCHANGES,)),
            pltpu.SemaphoreType.DMA((EXCHANGES,)),
        ],
        compiler_params=pltpu.CompilerParams(
            collective_id=0, has_side_effects=True, vmem_limit_bytes=32 * 1024 * 1024
        ),
    )(*[pltpu.with_memory_space_constraint(array, pltpu.HBM) for array in arrays])
    out = jax.ShapeDtypeStruct(pressure_rhs.shape, f32)
    return pl.pallas_call(
        publish,
        out_shape=(out, out),
        in_specs=[in_vmem] * 2,
        out_specs=(in_hbm, in_hbm),
        scratch_shapes=[pltpu.SemaphoreType.DMA((2,))],
        compiler_params=pltpu.CompilerParams(vmem_limit_bytes=16 * 1024 * 1024),
    )(*result)


def solution(mesh):
    placed = (
        P("gx", "gy", None),
        P("gx", "gy", None),
        P(None, "gx", "gy", None),
        P("gx", "gy", None),
        P(None, "gx", "gy", None),
        P("gx", "gy", None),
        P(None, "gx", "gy", None),
    )
    return jax.shard_map(
        local,
        mesh=mesh,
        in_specs=placed,
        out_specs=(P("gx", "gy", None), P("gx", "gy", None)),
        check_vma=False,
    )
```

```python
import functools

import jax
import jax.numpy as jnp
from jax import lax
from jax.experimental import pallas as pl
from jax.experimental.pallas import tpu as pltpu
from jax.sharding import PartitionSpec as P

KC = 6
GROUP = 8
REACH = 4
DAMPING = 2.0 / 3.0

MESH = pl.DeviceIdType.MESH

O = 4
OP = 2
M0, M2, STORE, SOURCE, M1 = range(5)
OWN_C = slice(15, 17)
FINE_X, FINE_Y, COEF_X, COEF_Y, MID_IN, MID_F, FINE_V, COARSE_F, MID_V = range(9)
EXCHANGES = 9
NEIGHBOURS = ((1, 0), (-1, 0), (1, 1), (1, -1), (-1, 1), (-1, -1), (0, 1), (0, -1))


def reciprocal(values):
    guess = pl.reciprocal(values, approx=True)
    return guess * (2.0 - values * guess)


def harmonic(left, right):
    return 2.0 * left * right * reciprocal(left + right)


def next_of(values, axis):
    return pltpu.roll(values, values.shape[axis] - 1, axis)


def prev_of(values, axis):
    return pltpu.roll(values, 1, axis)


def next_paired(values, axis, pairs):
    first, second = lax.slice_in_dim(values, 0, 1, axis=axis), lax.slice_in_dim(values, 1, 2, axis=axis)
    return jnp.concatenate([second, next_of(first, pairs)], axis=axis)


def prev_paired(values, axis, pairs):
    first, second = lax.slice_in_dim(values, 0, 1, axis=axis), lax.slice_in_dim(values, 1, 2, axis=axis)
    return jnp.concatenate([prev_of(second, pairs), first], axis=axis)


def next_y(values):
    return next_paired(values, 1, values.ndim - 2)


def prev_y(values):
    return prev_paired(values, 1, values.ndim - 2)


def next_z(values):
    return next_paired(values, 2, 4) if values.ndim == 5 else next_of(values, 3)


def prev_z(values):
    return prev_paired(values, 2, 4) if values.ndim == 5 else prev_of(values, 3)


def blocks(level, rows):
    first, last = rows
    most = 4 if len(level[0].shape) == 5 else 6
    count = -(-(last - first) // most)
    edges = [first + (last - first) * at // count for at in range(count + 1)]
    return [slice(*pair) for pair in zip(edges[:-1], edges[1:])]


def moved(rows, by):
    return slice(rows.start + by, rows.stop + by)


def one_hot(shape, test):
    row = lax.broadcasted_iota(jnp.int32, shape, 0)
    column = lax.broadcasted_iota(jnp.int32, shape, 1)
    return jnp.where(test(row, column), 1.0, 0.0).astype(jnp.bfloat16)


def pieces(values, count):
    parts = []
    for _ in range(count - 1):
        parts.append(values.astype(jnp.bfloat16))
        values = values - parts[-1].astype(jnp.float32)
    return parts + [values.astype(jnp.bfloat16)]


def times_one_hot(values, matrix, count):
    rows = values.shape[0]
    product = jnp.dot(jnp.concatenate(pieces(values, count), axis=0), matrix, preferred_element_type=jnp.float32)
    return total([product[at * rows : (at + 1) * rows] for at in range(count)])


def total(terms):
    while len(terms) > 1:
        pairs = [terms[i] + terms[i + 1] for i in range(0, len(terms) - 1, 2)]
        terms = pairs + terms[len(terms) - len(terms) % 2 :]
    return terms[0]


def source_span(step, first, n, width):
    return slice(first + n - width, first + n) if step > 0 else slice(first, first + (width if step < 0 else n))


def target_span(step, first, n, width):
    if step > 0:
        return slice(first - width, first)
    return slice(first + n, first + n + width) if step < 0 else slice(first, first + n)


def weights_x(level, mob, rows):
    for x in blocks(level, rows):
        level[0][x] = harmonic(mob[0][x], mob[0][moved(x, 1)])


def weights_yz(level, mob, rows, keep_y, keep_z):
    wx, wyu, wyd, wzu, wzd, diag, damp = level
    for x in blocks(level, rows):
        second = mob[1][x]
        up_y = harmonic(second, next_y(second)) * keep_y
        wyu[x] = up_y
        wyd[x] = prev_y(up_y)
        third = mob[2][x]
        up_z = harmonic(third, next_z(third)) * keep_z
        wzu[x] = up_z
        wzd[x] = prev_z(up_z)


def diagonals(level, store, rows):
    wx, wyu, wyd, wzu, wzd, diag, damp = level
    for x in blocks(level, rows):
        all_of_it = store[x] + (wx[x] + wx[moved(x, -1)]) + (wyu[x] + wyd[x]) + (wzu[x] + wzd[x])
        diag[x] = all_of_it
        damp[x] = DAMPING * reciprocal(all_of_it)


def residual_of(level, source, field, x):
    wx, wyu, wyd, wzu, wzd, diag, damp = level
    v = field[x]
    left = source[x] - diag[x] * v
    left = left + (wx[x] * field[moved(x, 1)] + wx[moved(x, -1)] * field[moved(x, -1)])
    left = left + (wyu[x] * next_y(v) + wyd[x] * prev_y(v))
    return left + (wzu[x] * next_z(v) + wzd[x] * prev_z(v))


def sweep(level, source, field, result, rows):
    damp = level[6]
    for x in blocks(level, rows):
        result[x] = field[x] + damp[x] * residual_of(level, source, field, x)


def start_sweep(level, source, result, rows):
    damp = level[6]
    for x in blocks(level, rows):
        result[x] = damp[x] * source[x]


def kernel(
    count_x,
    count_y,
    rhs_h,
    store_f_h,
    mob_f_h,
    store_m_h,
    mob_m_h,
    store_c_h,
    mob_c_h,
    pressure,
    residual,
    f_stage,
    f_mixed,
    f_in,
    f_wx,
    f_wyu,
    f_wyd,
    f_wzu,
    f_wzd,
    f_diag,
    f_damp,
    f_a,
    f_b,
    f_x,
    m_in,
    m_src,
    m_wx,
    m_wyu,
    m_wyd,
    m_wzu,
    m_wzd,
    m_diag,
    m_damp,
    m_a,
    m_b,
    m_y,
    m_fold,
    f_rows,
    together,
    c_coef,
    c_src,
    c_ext,
    c_weights,
    c_bands,
    c_inverse,
    meter,
    spare,
    c_spare,
    local_sem,
    send_sem,
    recv_sem,
):
    gx = lax.axis_index("gx")
    gy = lax.axis_index("gy")

    def stepped(at, step, count):
        to = at + step
        if step > 0:
            return jnp.where(to >= count, to - count, to)
        return jnp.where(to < 0, to + count, to) if step < 0 else at

    along_gx = {step: stepped(gx, step, count_x) for step in (-1, 0, 1)}
    along_gy = {step: stepped(gy, step, count_y) for step in range(-REACH, REACH + 1)}

    def beside(sx, sy):
        return {"gx": along_gx[sx], "gy": along_gy[sy]}

    def ahead_of(sx):
        return gx < count_x - 1 if sx > 0 else gx > 0

    barrier = pltpu.get_barrier_semaphore()

    def greet(steps):
        for step in steps:
            pl.semaphore_signal(barrier, inc=1, device_id=beside(*step), device_id_type=MESH)

    for side in (1, -1):

        @pl.when(ahead_of(side))
        def _():
            greet([step for step in NEIGHBOURS if step[0] == side])

    straight = [(0, e) for e in range(-REACH, REACH + 1) if e != 0]
    greet(straight)
    partners = len(straight) + jnp.where(gx > 0, 3, 0) + jnp.where(gx < count_x - 1, 3, 0)

    c_coef[:, 6:8] = jnp.ones((4, 2, 32, 64), jnp.float32)
    c_src[6:8] = jnp.zeros((2, 32, 128), jnp.float32)

    locals_ = []

    def bring(source, target):
        copy = pltpu.make_async_copy(source, target, local_sem.at[len(locals_)])
        copy.start()
        locals_.append(copy)
        return copy

    def exchange(at, messages):
        sizes = []
        for source, _, _ in messages:
            rows = 1
            for size in source.shape[:-1]:
                rows = rows * size
            sizes.append(rows)
        rows_of[at] = rows_of.get(at, 0) + sum(sizes)

        def send(side):
            for source, target, step in messages:
                if step[0] == side:
                    pltpu.make_async_remote_copy(
                        src_ref=source,
                        dst_ref=target,
                        send_sem=send_sem.at[at],
                        recv_sem=recv_sem.at[at],
                        device_id=beside(*step),
                        device_id_type=MESH,
                    ).start()

        for side in (1, -1):
            rows = sum(size for size, message in zip(sizes, messages) if message[2][0] == side)
            if rows == 0:
                continue
            first = spent[0]
            spent[0] += rows

            @pl.when(ahead_of(side))
            def _():
                send(side)

            @pl.when(jnp.logical_not(ahead_of(side)))
            def _():
                if at == COEF_X:
                    pltpu.make_async_copy(c_coef.at[:, 2:4, OWN_C, :], c_spare, send_sem.at[at]).start()
                else:
                    spare_to = spare.at[first : first + rows, :]
                    pltpu.make_async_copy(meter.at[0:rows, :], spare_to, send_sem.at[at]).start()

            @pl.when(jnp.logical_not(ahead_of(-side)))
            def _():
                for source, target, step in messages:
                    if step[0] == side:
                        pltpu.make_async_copy(source, target, recv_sem.at[at]).start()

        send(0)

    spent = [0]
    rows_of = {}

    def all_of(at):
        if at == COEF_X:
            return c_coef.at[:, 0:4, 0:2, :]
        if at == COEF_Y:
            return c_coef.at[:, 0:6, 0:16, :]
        return meter.at[0 : rows_of[at], :]

    def received(at):
        pltpu.make_async_copy(all_of(at), all_of(at), recv_sem.at[at]).wait()

    def sent(at):
        pltpu.make_async_copy(all_of(at), all_of(at), send_sem.at[at]).wait()

    own8, pairs8 = slice(O, O + 8), slice(OP, OP + 4)
    own4, pairs4 = slice(O, O + 4), slice(OP, OP + 2)
    fine_in = [
        bring(mob_f_h, f_stage.at[0:3]),
        bring(store_f_h, f_stage.at[3]),
        bring(rhs_h, f_stage.at[4]),
    ]
    coarse_in = [
        bring(store_c_h, c_coef.at[0, 2:4, OWN_C, :]),
        bring(mob_c_h, c_coef.at[1:4, 2:4, OWN_C, :]),
    ]
    mid_in = []
    for y in range(4):
        parity, pair = y % 2, OP + y // 2
        mid_in.append(bring(mob_m_h.at[:, :, y, :], m_in.at[0:3, own4, parity, pair, :]))
        mid_in.append(bring(store_m_h.at[:, y, :], m_in.at[3, own4, parity, pair, :]))
    f_src = f_in.at[SOURCE]

    def spans(sx, sy, n, wide_x, wide_y):
        return (
            source_span(sx, O, n, wide_x),
            source_span(sy, OP, n // 2, wide_y),
            target_span(sx, O, n, wide_x),
            target_span(sy, OP, n // 2, wide_y),
        )

    faces_x = [step for step in NEIGHBOURS if step[1] == 0]
    faces_y = [step for step in NEIGHBOURS if step[0] == 0]
    corners = [step for step in NEIGHBOURS if step[0] != 0 and step[1] != 0]

    apart = one_hot((256, 256), lambda row, column: row == 2 * (column % 128) + column // 128)
    for copy in fine_in:
        copy.wait()
    sorted_z = times_one_hot(f_stage[...].reshape(320, 256), apart, 2)
    for half in range(2):
        f_mixed[half] = sorted_z[:, 128 * half : 128 * half + 128].reshape(40, 8, 128)

    def sort_y(x, _):
        for at, to in enumerate((M0, M1, M2, STORE, SOURCE)):
            for parity in range(2):
                for half in range(2):
                    rows = f_mixed[half, 8 * at + x, pl.ds(parity, 4, stride=2), :]
                    f_in[to, O + x, parity, half, pairs8] = rows
        return 0

    lax.fori_loop(0, 8, sort_y, 0, unroll=True)
    pl.semaphore_wait(barrier, partners)

    def part(first, last, step, wide_x, wide_y, parity=slice(0, 2)):
        fields = slice(first, last + 1)
        ax, ay, bx, by = spans(*step, 8, wide_x, wide_y)
        return (f_in.at[fields, ax, parity, :, ay, :], f_in.at[fields, bx, parity, :, by, :], step)

    for copy in coarse_in:
        copy.wait()
    exchange(
        COEF_X,
        [
            (c_coef.at[:, 2:4, OWN_C, :], c_coef.at[:, 2 - 2 * sx : 4 - 2 * sx, OWN_C, :], (sx, sy))
            for sx, sy in faces_x
        ],
    )

    messages = []
    for step in faces_x:
        messages += [part(M0, M0, step, 3, 1), part(M2, M1, step, 2, 1)]
    for step in corners:
        nearest = slice(1, 2) if step[1] > 0 else slice(0, 1)
        messages += [part(M0, M0, step, 2, 1), part(M1, M1, step, 2, 1), part(M2, SOURCE, step, 1, 1, nearest)]
    exchange(FINE_X, messages)
    messages = []
    for step in faces_y:
        messages += [part(M0, SOURCE, step, 1, 1), part(M1, M1, step, 1, 2)]
    exchange(FINE_Y, messages)

    for copy in mid_in:
        copy.wait()
    messages = []

    def mid_part(first, last, step, wide_x, wide_y, beyond_y=0):
        fields = slice(first, last + 1)
        ax, ay, bx, by = spans(*step, 4, wide_x, wide_y)
        if beyond_y and step[1] > 0:
            ay, by = slice(ay.start, ay.stop - beyond_y), slice(by.start, by.stop - beyond_y)
        elif beyond_y:
            ay, by = slice(ay.start + beyond_y, ay.stop), slice(by.start + beyond_y, by.stop)
        return (m_in.at[fields, ax, :, ay, :], m_in.at[fields, bx, :, by, :], step)

    for step in faces_x:
        messages += [mid_part(0, 0, step, 4, 1), mid_part(1, 3, step, 3, 1)]
    for step in corners:
        messages += [mid_part(0, 1, step, 3, 1), mid_part(0, 1, step, 1, 2, 1), mid_part(2, 3, step, 2, 1)]
    for step in faces_y:
        messages.append(mid_part(0, 3, step, 4, 2))
    exchange(MID_IN, messages)

    one = jnp.float32(1.0)
    nil = jnp.float32(0.0)
    keep_x = (jnp.where(gx == 0, nil, one), jnp.where(gx == count_x - 1, nil, one))

    def keep_yz(own, shape):
        def index(axis):
            return lax.broadcasted_iota(jnp.int32, shape, axis)

        parity, pair, lane = index(0), index(len(shape) - 2), index(len(shape) - 1)
        end = jnp.where(gy == 0, OP - 1, -1)
        other = jnp.where(gy == count_y - 1, OP + own // 2 - 1, -1)
        keep_y = jnp.where((parity == 1) & ((pair == end) | (pair == other)), 0.0, 1.0)
        last_z = (lane == 127) if len(shape) == 3 else (lane == 127) & (index(1) == 1)
        return keep_y, jnp.where(last_z, 0.0, 1.0)

    together[...] = one_hot((256, 256), lambda row, column: column == 2 * (row % 128) + row // 128)
    fold_c = one_hot((64, 128), lambda row, column: row // 8 + 8 * (row % 8) == column // 2)

    fine = (f_wx, f_wyu, f_wyd, f_wzu, f_wzd, f_diag, f_damp)
    f_mob = (f_in.at[M0], f_in.at[M1], f_in.at[M2])
    f_store = f_in.at[STORE]
    keep_y, keep_z = keep_yz(8, (2, 2, 8, 128))
    received(FINE_Y)
    weights_yz(fine, f_mob, (O, O + 8), keep_y, keep_z)
    weights_x(fine, f_mob, (O, O + 7))
    diagonals(fine, f_store, (O + 1, O + 7))
    start_sweep(fine, f_src, f_a, (O + 1, O + 7))
    received(COEF_X)
    messages = []
    for step in straight:
        target = c_coef.at[:, 0:6, OWN_C.start - 2 * step[1] : OWN_C.stop - 2 * step[1], :]
        messages.append((c_coef.at[:, 0:6, OWN_C, :], target, step))
    exchange(COEF_Y, messages)
    sweep(fine, f_src, f_a, f_b, (O + 2, O + 6))
    received(FINE_X)
    for rows in ((O - 3, O), (O + 7, O + 10)):
        weights_x(fine, f_mob, rows)
    f_wx[O - 1] = f_wx[O - 1] * keep_x[0]
    f_wx[O + 7] = f_wx[O + 7] * keep_x[1]
    for rows in ((O - 2, O), (O + 8, O + 10)):
        weights_yz(fine, f_mob, rows, keep_y, keep_z)
    for rows in ((O - 2, O + 1), (O + 7, O + 10)):
        diagonals(fine, f_store, rows)
        start_sweep(fine, f_src, f_a, rows)
    for rows in ((O - 1, O + 2), (O + 6, O + 9)):
        sweep(fine, f_src, f_a, f_b, rows)

    for x in blocks(fine, (O, O + 8)):
        left = residual_of(fine, f_src, f_b, x)
        for pair in range(2):
            both = left[2 * pair] + left[2 * pair + 1]
            m_fold[(x.start - O) // 2 + pair] = (both[0, 0] + both[0, 1]) + (both[1, 0] + both[1, 1])
    for x in range(4):
        for parity in range(2):
            m_src[O + x, parity, pairs4] = m_fold[x, pl.ds(OP + parity, 2, stride=2), :]
    messages = []
    for step in NEIGHBOURS:
        ax, ay, bx, by = spans(*step, 4, 2 if step in corners else 3, 1 if step in corners else 2)
        messages.append((m_src.at[ax, :, ay, :], m_src.at[bx, :, by, :], step))
    exchange(MID_F, messages)

    mid = (m_wx, m_wyu, m_wyd, m_wzu, m_wzd, m_diag, m_damp)
    m_mob = (m_in.at[0], m_in.at[1], m_in.at[2])
    keep_y, keep_z = keep_yz(4, (2, 8, 128))
    received(MID_IN)
    weights_x(mid, m_mob, (O - 4, O + 7))
    m_wx[O - 1] = m_wx[O - 1] * keep_x[0]
    m_wx[O + 3] = m_wx[O + 3] * keep_x[1]
    weights_yz(mid, m_mob, (O - 3, O + 7), keep_y, keep_z)
    diagonals(mid, m_in.at[3], (O - 3, O + 7))

    for at in (FINE_X, FINE_Y, COEF_X, MID_IN):
        sent(at)

    received(MID_F)
    start_sweep(mid, m_src, m_a, (O - 2, O + 6))
    sweep(mid, m_src, m_a, m_b, (O - 1, O + 5))
    left = residual_of(mid, m_src, m_b, own4)
    for ix in range(2):
        fold = left[2 * ix] + left[2 * ix + 1]
        c_src[2 + ix, OWN_C, :] = (fold[0] + fold[1])[pairs4]
    messages = []
    for e in sorted(range(-REACH, REACH + 1), key=lambda e: -abs(e)):
        for g in (1, -1, 0):
            if (g, e) != (0, 0):
                target = c_src.at[2 - 2 * g : 4 - 2 * g, OWN_C.start - 2 * e : OWN_C.stop - 2 * e, :]
                messages.append((c_src.at[2:4, OWN_C, :], target, (g, e)))
    exchange(COARSE_F, messages)

    def keep_mid(x, _):
        m_y[x, :, pairs4] = m_b[x, :, pairs4]
        return 0

    lax.fori_loop(O, O + 4, keep_mid, 0, unroll=True)
    messages = []
    for step in NEIGHBOURS:
        ax, ay, bx, by = spans(*step, 4, 3 if step in corners else 4, 2)
        messages.append((m_y.at[ax, :, ay, :], m_y.at[bx, :, by, :], step))
    exchange(MID_V, messages)

    def keep_fine(x, _):
        f_x[x, :, :, pairs8] = f_b[x, :, :, pairs8]
        return 0

    lax.fori_loop(O, O + 8, keep_fine, 0, unroll=True)
    messages = []
    for step in NEIGHBOURS:
        ax, ay, bx, by = spans(*step, 8, 2 if step in corners else 3, 1 if step in corners else 2)
        messages.append((f_x.at[ax, :, :, ay, :], f_x.at[bx, :, :, by, :], step))
    exchange(FINE_V, messages)

    received(COEF_Y)
    coef = [c_coef[k, :, 8:24, :].reshape(128, 64).T for k in range(4)]
    second_prev = c_coef[2, :, 7:23, :].reshape(128, 64).T
    second_next = c_coef[2, :, 9:25, :].reshape(128, 64).T
    column = lax.broadcasted_iota(jnp.int32, (64, 128), 1)
    level_row = lax.broadcasted_iota(jnp.int32, (64, 128), 0)
    cells = 2 * count_y
    cell = 2 * gy + lax.rem(column, 16) + (cells - 7)
    block = 2 * GROUP
    offset = 4 + cells - (cells // block) * block
    shut_up = (lax.rem(cell + 1 - offset + 2 * block, block) == 0) | (lax.rem(cell + 1, cells) == 0)
    shut_down = (lax.rem(cell - offset + 2 * block, block) == 0) | (lax.rem(cell, cells) == 0)
    up_x = jnp.where(lax.rem(column, 32) < 16, harmonic(coef[1], pltpu.roll(coef[1], 112, 1)), 0.0)
    down_x = pltpu.roll(up_x, 16, 1)
    up_y = jnp.where(shut_up, 0.0, harmonic(coef[2], second_next))
    down_y = jnp.where(shut_down, 0.0, harmonic(second_prev, coef[2]))
    up_z = jnp.where(level_row == 63, 0.0, harmonic(coef[3], next_of(coef[3], 0)))
    down_z = prev_of(up_z, 0)
    main = coef[0] + (up_x + down_x) + (up_y + down_y) + (up_z + down_z)
    for at, band in enumerate((up_x, down_x, up_y, down_y, -down_z, main, -up_z)):
        c_bands[at] = band

    def registers(at):
        return [c_bands[at, pl.ds(place, 8, stride=8), :] for place in range(8)]

    for at in range(4):
        for place, values in enumerate(registers(at)):
            c_weights[at, place] = values
    low, main, high = (registers(at) for at in (4, 5, 6))
    ahead, back = [reciprocal(main[0])], {6: reciprocal(main[6])}
    upto, onfrom = [main[0]], {6: main[6]}
    for i in range(1, 7):
        upto.append(main[i] - low[i] * high[i - 1] * ahead[i - 1])
        ahead.append(reciprocal(upto[i]))
        j = 6 - i
        onfrom[j] = main[j] - high[j] * low[j + 1] * back[j + 1]
        back[j] = reciprocal(onfrom[j])
    rise = [-high[i] * ahead[i] for i in range(7)]
    fall = [-low[i] * back[i] for i in range(7)]
    inverse = {}
    for j in range(7):
        inverse[j, j] = reciprocal(upto[j] + onfrom[j] - main[j])
        for i in range(j - 1, -1, -1):
            inverse[i, j] = rise[i] * inverse[i + 1, j]
        for i in range(j + 1, 7):
            inverse[i, j] = fall[i] * inverse[i - 1, j]
    from_last = [inverse[i, 0] * low[0] for i in range(7)]
    from_own = [inverse[i, 6] * high[6] for i in range(7)]

    def turned(values, by):
        return pltpu.roll(values, by % 8, 0) if by % 8 else values

    face_main = main[7] - low[7] * from_own[6] - high[7] * turned(from_last[0], -1)
    face_low = -low[7] * from_last[6]
    face_high = -high[7] * turned(from_own[0], -1)
    spread_by = {0: jnp.ones((8, 128), jnp.float32)}
    for far in (1, 2, 4):
        over = reciprocal(face_main)
        alpha = -face_low * turned(over, far)
        gamma = -face_high * turned(over, -far)
        face_main = face_main + alpha * turned(face_high, far) + gamma * turned(face_low, -far)
        face_low, face_high = alpha * turned(face_low, far), gamma * turned(face_high, -far)
        wider = dict(spread_by)
        for by, values in spread_by.items():
            for step, factor in ((far, alpha), (-far, gamma)):
                term = factor * turned(values, step)
                key = (by + step) % 8
                wider[key] = wider[key] + term if key in wider else term
        spread_by = wider
    over = reciprocal(face_main)
    own_by = [over * spread_by[by] for by in range(8)]
    next_by = [own_by[(by + 1) % 8] * turned(high[7], by + 1) for by in range(8)]
    for i in range(7):
        for j in range(7):
            c_inverse[7 * i + j] = inverse[i, j]
        c_inverse[49 + i] = from_last[i]
        c_inverse[56 + i] = from_own[i]
    for by in range(8):
        c_inverse[64 + by] = own_by[by]
        c_inverse[72 + by] = next_by[by]
        c_inverse[80 + by] = turned(own_by[by - 1], 1)
        c_inverse[88 + by] = turned(next_by[by - 1], 1)
    c_inverse[63] = low[7]

    def lines(values):
        inner = [total([c_inverse[7 * i + j] * values[j] for j in range(7)]) for i in range(7)]
        face = values[7] - c_inverse[63] * inner[6]
        faces = [turned(face, by) for by in range(8)]
        firsts = [turned(inner[0], by) for by in range(8)]

        def interface(at):
            terms = [c_inverse[at + by] * faces[by] for by in range(8)]
            return total(terms) - total([c_inverse[at + 8 + by] * firsts[by] for by in range(8)])

        here, before = interface(64), interface(80)
        return tuple(inner[i] - (c_inverse[49 + i] * before + c_inverse[56 + i] * here) for i in range(7)) + (here,)

    for at in (COEF_Y, MID_F):
        sent(at)

    received(COARSE_F)
    source = lax.dot_general(
        jnp.concatenate([fold_c] * 2, axis=1),
        jnp.concatenate(pieces(c_src[:, 8:24, :].reshape(128, 128), 2), axis=1),
        (((1,), (1,)), ((), ())),
        preferred_element_type=jnp.float32,
    )
    sources = [source[8 * place : 8 * place + 8] for place in range(8)]

    def turn(_, z):
        pushed = []
        for place in range(8):
            own = z[place]
            along_x = c_weights[0, place] * pltpu.roll(own, 112, 1) + c_weights[1, place] * pltpu.roll(own, 16, 1)
            along_y = c_weights[2, place] * next_of(own, 1) + c_weights[3, place] * prev_of(own, 1)
            pushed.append(sources[place] + (along_x + along_y))
        return lines(pushed)

    z = lax.fori_loop(0, KC - 1, turn, lines(sources))
    c_ext[...] = times_one_hot(jnp.concatenate(z, axis=0).T[0:96], fold_c, 2).reshape(6, 16, 128)

    received(MID_V)

    def raise_mid(x, _):
        rows = c_ext[x, 5:13, :]
        for along in range(2):
            for parity in range(2):
                m_a[2 * x + along, parity] = m_y[2 * x + along, parity] + rows
        return 0

    lax.fori_loop(0, 6, raise_mid, 0, unroll=True)
    sweep(mid, m_src, m_a, m_b, (O - 3, O + 7))
    sweep(mid, m_src, m_b, m_a, (O - 2, O + 6))

    received(FINE_V)

    def raise_fine(x, _):
        for parity in range(2):
            m_fold[x, pl.ds(parity, 4, stride=2), :] = m_a[O - 2 + x, parity, 1:5]
        rows = m_fold[x]
        for along in range(2):
            for parity in range(2):
                for half in range(2):
                    at = (2 * x + along, parity, half)
                    f_a[at] = f_x[at] + rows
        return 0

    lax.fori_loop(0, 8, raise_fine, 0, unroll=True)
    sweep(fine, f_src, f_a, f_b, (O - 2, O + 10))
    sweep(fine, f_src, f_b, f_a, (O - 1, O + 9))


    def in_order(field, result):
        def sort_back(x, _):
            for parity in range(2):
                for half in range(2):
                    f_rows[half, x, pl.ds(parity, 8, stride=2), :] = field[O + x, parity, half]
            return 0

        lax.fori_loop(0, 8, sort_back, 0, unroll=True)
        halves = [f_rows[half, :, O : O + 8, :].reshape(64, 128) for half in range(2)]
        result[...] = times_one_hot(jnp.concatenate(halves, axis=1), together[...], 2).reshape(8, 8, 256)

    in_order(f_a, pressure)

    for x in blocks(fine, (O, O + 8)):
        f_b[x] = residual_of(fine, f_src, f_a, x)
    in_order(f_b, residual)
    for at in (COARSE_F, MID_V, FINE_V):
        sent(at)


def publish(pressure, residual, pressure_h, residual_h, sem):
    copies = [
        pltpu.make_async_copy(pressure, pressure_h, sem.at[0]),
        pltpu.make_async_copy(residual, residual_h, sem.at[1]),
    ]
    for copy in copies:
        copy.start()
    for copy in copies:
        copy.wait()


def local(pressure_rhs, storage_fine, mobility_fine, storage_mid, mobility_mid, storage_coarse, mobility_coarse):
    count_x = lax.axis_size("gx")
    count_y = lax.axis_size("gy")
    f32 = jnp.float32
    fine = pltpu.VMEM((8 + 2 * O, 2, 2, 8, 128), f32)
    mid = pltpu.VMEM((4 + 2 * O, 2, 8, 128), f32)
    in_hbm = pl.BlockSpec(memory_space=pltpu.HBM)
    in_vmem = pl.BlockSpec(memory_space=pltpu.VMEM)
    arrays = (pressure_rhs, storage_fine, mobility_fine, storage_mid, mobility_mid, storage_coarse, mobility_coarse)
    result = pl.pallas_call(
        functools.partial(kernel, count_x, count_y),
        out_shape=(pltpu.VMEM(pressure_rhs.shape, f32),) * 2,
        in_specs=[in_hbm] * 7,
        out_specs=(in_vmem, in_vmem),
        scratch_shapes=[
            pltpu.VMEM((5, 8, 8, 256), f32),
            pltpu.VMEM((2, 40, 8, 128), f32),
            pltpu.VMEM((5, 8 + 2 * O, 2, 2, 8, 128), f32),
            *[fine] * 10,
            pltpu.VMEM((4, 4 + 2 * O, 2, 8, 128), f32),
            *[mid] * 11,
            pltpu.VMEM((8, 8, 128), f32),
            pltpu.VMEM((2, 8, 16, 128), f32),
            pltpu.VMEM((256, 256), jnp.bfloat16),
            pltpu.VMEM((4, 8, 32, 64), f32),
            pltpu.VMEM((8, 32, 128), f32),
            pltpu.VMEM((6, 16, 128), f32),
            pltpu.VMEM((4, 8, 8, 128), f32),
            pltpu.VMEM((7, 64, 128), f32),
            pltpu.VMEM((97, 8, 128), f32),
            pltpu.VMEM((1024, 128), f32),
            pltpu.VMEM((4096, 128), f32),
            pltpu.VMEM((4, 2, 2, 64), f32),
            pltpu.SemaphoreType.DMA((16,)),
            pltpu.SemaphoreType.DMA((EXCHANGES,)),
            pltpu.SemaphoreType.DMA((EXCHANGES,)),
        ],
        compiler_params=pltpu.CompilerParams(
            collective_id=0, has_side_effects=True, vmem_limit_bytes=32 * 1024 * 1024
        ),
    )(*[pltpu.with_memory_space_constraint(array, pltpu.HBM) for array in arrays])
    out = jax.ShapeDtypeStruct(pressure_rhs.shape, f32)
    return pl.pallas_call(
        publish,
        out_shape=(out, out),
        in_specs=[in_vmem] * 2,
        out_specs=(in_hbm, in_hbm),
        scratch_shapes=[pltpu.SemaphoreType.DMA((2,))],
        compiler_params=pltpu.CompilerParams(vmem_limit_bytes=16 * 1024 * 1024),
    )(*result)


def solution(mesh):
    placed = (
        P("gx", "gy", None),
        P("gx", "gy", None),
        P(None, "gx", "gy", None),
        P("gx", "gy", None),
        P(None, "gx", "gy", None),
        P("gx", "gy", None),
        P(None, "gx", "gy", None),
    )
    return jax.shard_map(
        local,
        mesh=mesh,
        in_specs=placed,
        out_specs=(P("gx", "gy", None), P("gx", "gy", None)),
        check_vma=False,
    )
```
